32 devices in a mesh: grp: 4 (over y, x), smp: 8 (over z, core).
Axes of the slice: x: 2, y: 2, z: 4, core: 2. Of those that a mesh axis runs over, the one named last changes fastest.
Arguments:
- currents: bfloat16 [2, 8, 262144], P(None, None, ('grp', 'smp')), may hold values from -6 to 6
- near_blocks: bfloat16 [2, 8192, 32, 256], P(None, ('grp', 'smp')), may hold values from -0.25 to 0.25
- near_list: int32 [8192, 8], P(('grp', 'smp')), may hold values from 0 to 8191, as said below
- near_count: int32 [8192], P(('grp', 'smp')), may hold values from 1 to 8, as said below
- radiation: bfloat16 [2, 8192, 32, 128], P(None, ('grp', 'smp')), may hold values from -0.75 to 0.75
- interp: bfloat16 [64, 1024], replicated, may hold values from -0.75 to 0.75
- shift_angle: float32 [8, 1024], replicated, may hold values from -3.140625 to 3.140625
- translation: bfloat16 [2, 316, 2048], P(None, None, ('grp', 'smp')), may hold values from -0.0625 to 0.0625
- trans_box: int32 [1024, 12], replicated, may hold values from 0 to 1023
- trans_off: int32 [1024, 12], replicated, may hold values from 0 to 315
Outputs:
- product_field: float32 [2, 8, 262144], P(None, None, ('grp', 'smp'))
The draws below stay inside these ranges and needn't reach their ends.
Inputs may be any that keep to these rules, and one draw needn't show every extreme that they name: `near_list`: entry 0 of row c is c itself, and every entry of row c lies within 256 clusters of c. Slots 0 to near_count[c] - 1 of row c of near_list are live; the other slots are ignored.
All inputs are finite; a program needn't handle non-finite values.
Results may differ from the reference program's by a relative error of at most 0.0056.
Values may be sent and summed in bfloat16 or wider, within the bound.
No kernel may reach another device: no remote copies, remote signals or barrier semaphores. Data moves between devices by JAX's collectives and lax.ppermute only.
A program may use at most 128 MiB of HBM per device.

```python
import jax
import jax.numpy as jnp
from jax import lax

R = 8
U = 32
NBR = 8
K0 = 64
K1 = 1024
OFFS = 316
IL = 12
NC = 256
Q0 = 128
Q1 = 2048
CLUSTERS = 8192
UNKNOWNS = 262144
NB_ALL = 1024


def draw_near_list(key, part):
    key = jax.random.fold_in(key, 11)
    offsets = jax.random.randint(key, (CLUSTERS, NBR), -NC, NC + 1).astype(jnp.int32)
    offsets = offsets.at[:, 0].set(0)
    owners = jnp.arange(CLUSTERS, dtype=jnp.int32)[:, None]
    return jnp.clip(owners + offsets, 0, CLUSTERS - 1).astype(jnp.int32)


def draw_near_count(key, part):
    key = jax.random.fold_in(key, 23)
    first_key, second_key = jax.random.split(key)
    groups = CLUSTERS // NC
    floors = jax.random.randint(first_key, (groups, 1), 1, NBR + 1).astype(jnp.int32)
    counted = jax.random.randint(second_key, (groups, NC), floors, NBR + 1).astype(jnp.int32)
    counted = counted.reshape(CLUSTERS)
    return counted.at[0].set(NBR).astype(jnp.int32)


def place_ends(result, rng, smallest, high):
    longest = result.shape.index(max(result.shape))
    spots = []
    for shift in (0, 1):
        where = [jax.random.randint(jax.random.fold_in(rng, axis), (), 0, length) for axis, length in enumerate(result.shape)]
        where[longest] = (where[longest] + shift) % result.shape[longest]
        spots.append(tuple(where))
    return result.at[spots[0]].set(smallest).at[spots[1]].set(high)


def steps_of(rng, shape, shards, least, largest):
    loudness, own = 1.0, jax.random.fold_in(rng, 6)
    for axis_at, parts in shards:
        draws = jnp.exp(jax.random.uniform(jax.random.fold_in(own, axis_at), (parts,), jnp.float32, least / len(shards), largest / len(shards)))
        loudness = loudness * jnp.repeat(draws, shape[axis_at] // parts).reshape([-1 if axis == axis_at else 1 for axis in range(len(shape))])
    return loudness


def normal_values(own_key, extent, scale, bound, pieces=(), held_as=jnp.bfloat16):
    result = scale * jax.random.normal(own_key, extent, jnp.float32)
    if pieces:
        result = result * steps_of(own_key, extent, pieces, -0.22, 0.18)
    return jnp.clip(result, -bound, bound).astype(held_as)


def setup_inputs(seed: int = 0) -> dict:
    key_list = jax.random.split(jax.random.key(seed), 11)
    return {
        "currents": normal_values(key_list[0], (2, R, UNKNOWNS), 1.0, 6.0, ((2, 32),)),
        "near_blocks": normal_values(key_list[1], (2, CLUSTERS, U, NBR * U), (2 * NBR * U) ** -0.5, 0.25, ((1, 32),)),
        "near_list": draw_near_list(jax.random.fold_in(key_list[10], 71), 0),
        "near_count": draw_near_count(jax.random.fold_in(key_list[10], 71), 0),
        "radiation": normal_values(key_list[4], (2, CLUSTERS, U, Q0), (2 * U) ** -0.5, 0.75, ((1, 32),)),
        "interp": normal_values(key_list[5], (K0, K1), K0 ** -0.5, 0.75),
        "shift_angle": jnp.clip(jax.random.uniform(key_list[6], (8, K1), jnp.float32, -3.140625, 3.140625), -3.140625, 3.140625),
        "translation": normal_values(key_list[7], (2, OFFS, Q1), 0.0113, 0.0625, ((2, 32),)),
        "trans_box": place_ends(jax.random.randint(key_list[8], (NB_ALL, IL), 0, NB_ALL), jax.random.fold_in(key_list[8], 1), 0, NB_ALL - 1).astype(jnp.int32),
        "trans_off": place_ends(jax.random.randint(key_list[9], (NB_ALL, IL), 0, OFFS), jax.random.fold_in(key_list[9], 1), 0, OFFS - 1).astype(jnp.int32),
    }


def product(pattern, left_side, right_side):
    return jnp.einsum(pattern, left_side.astype(jnp.float32), right_side.astype(jnp.float32))


def complex_terms(pattern, left_side, right_side, conjugate):
    if conjugate:
        real_part = product(pattern, left_side[0], right_side[0]) + product(pattern, left_side[1], right_side[1])
        imag_part = product(pattern, left_side[1], right_side[0]) - product(pattern, left_side[0], right_side[1])
    else:
        real_part = product(pattern, left_side[0], right_side[0]) - product(pattern, left_side[1], right_side[1])
        imag_part = product(pattern, left_side[1], right_side[0]) + product(pattern, left_side[0], right_side[1])
    return jnp.stack([real_part, imag_part])


def aggregate(current_block, radiation_block, interp, shift_angle):
    leaf_pattern = complex_terms("rcu,cuq->rcq", current_block, radiation_block, False).astype(jnp.bfloat16)
    clusters_here = leaf_pattern.shape[2]
    upward = jnp.dot(leaf_pattern.reshape(2, R, clusters_here, 2, K0), interp, preferred_element_type=jnp.float32)
    upward = upward.reshape(2, R, clusters_here // 8, 8, 2, K1)
    cosine = jnp.cos(shift_angle)[:, None, :]
    sine_part = jnp.sin(shift_angle)[:, None, :]
    real_part = upward[0] * cosine - upward[1] * sine_part
    imag_part = upward[0] * sine_part + upward[1] * cosine
    summed = jnp.stack([real_part.sum(axis=2), imag_part.sum(axis=2)])
    return summed.reshape(2, R, clusters_here // 8, 2 * K1).astype(jnp.bfloat16)


def disaggregate(received, radiation_block, interp, shift_angle):
    boxes_here = received.shape[2]
    widened = received.astype(jnp.float32).reshape(2, R, boxes_here, 1, 2, K1)
    cosine = jnp.cos(shift_angle)[:, None, :]
    sine_part = jnp.sin(shift_angle)[:, None, :]
    real_part = widened[0] * cosine + widened[1] * sine_part
    imag_part = widened[1] * cosine - widened[0] * sine_part
    shifted = jnp.stack([real_part, imag_part]).astype(jnp.bfloat16)
    downward = jnp.dot(shifted, interp.T, preferred_element_type=jnp.float32).astype(jnp.bfloat16)
    downward = downward.reshape(2, R, boxes_here * 8, 2 * K0)
    return complex_terms("rcq,cuq->rcu", downward, radiation_block, True)


def reference(currents, near_blocks, near_list, near_count, radiation, interp, shift_angle, translation, trans_box, trans_off):
    current_grid = currents.reshape(2, R, CLUSTERS, U)
    blocks = CLUSTERS // NC
    block_ids = jnp.arange(blocks, dtype=jnp.int32)
    slots = jnp.arange(NBR, dtype=jnp.int32)

    def near_block(block_id):
        first_row = (block_id * NC).astype(jnp.int32)
        listed = lax.dynamic_slice_in_dim(near_list, first_row, NC, 0)
        counted = lax.dynamic_slice_in_dim(near_count, first_row, NC, 0)
        live_mask = (slots[None, :] < counted[:, None]).astype(jnp.bfloat16)
        gathered = current_grid[:, :, listed, :] * live_mask[None, None, :, :, None]
        gathered = gathered.reshape(2, R, NC, NBR * U)
        matrices = lax.dynamic_slice_in_dim(near_blocks, first_row, NC, 1)
        return complex_terms("cum,rcm->rcu", matrices, gathered, False)

    def far_up(block_id):
        first_row = (block_id * NC).astype(jnp.int32)
        current_block = lax.dynamic_slice_in_dim(current_grid, first_row, NC, 2)
        radiation_block = lax.dynamic_slice_in_dim(radiation, first_row, NC, 1)
        return aggregate(current_block, radiation_block, interp, shift_angle)

    box_pattern = lax.map(far_up, block_ids)
    box_pattern = box_pattern.transpose(1, 2, 0, 3, 4).reshape(2, R, NB_ALL, Q1)

    def turn(column, totals):
        partner = box_pattern[:, :, trans_box[:, column], :].astype(jnp.float32)
        operator = translation[:, trans_off[:, column], :].astype(jnp.float32)
        real_part = totals[0] + operator[0][None] * partner[0] - operator[1][None] * partner[1]
        imag_part = totals[1] + operator[0][None] * partner[1] + operator[1][None] * partner[0]
        return jnp.stack([real_part, imag_part])

    translated = lax.fori_loop(0, IL, turn, jnp.zeros((2, R, NB_ALL, Q1), jnp.float32)).astype(jnp.bfloat16)

    def far_down(block_id):
        first_row = (block_id * NC).astype(jnp.int32)
        first_box = (block_id * (NC // 8)).astype(jnp.int32)
        received = lax.dynamic_slice_in_dim(translated, first_box, NC // 8, 2)
        radiation_block = lax.dynamic_slice_in_dim(radiation, first_row, NC, 1)
        return disaggregate(received, radiation_block, interp, shift_angle)

    near_field = lax.map(near_block, block_ids)
    far_field = lax.map(far_down, block_ids)
    total = (near_field + far_field).transpose(1, 2, 0, 3, 4)
    return total.reshape(2, R, UNKNOWNS)
```

```python
import functools

import jax
import jax.numpy as jnp
from jax import lax
from jax.experimental import pallas as pl
from jax.experimental.pallas import tpu as pltpu
from jax.sharding import Mesh
from jax.sharding import PartitionSpec as P

R = 8
U = 32
NBR = 8
K0 = 64
K1 = 1024
IL = 12
CHILDREN = 8
WIDE = CHILDREN * U
LANES = 128
HALF = 64
CHIPS = K1 // LANES
DEPTH = 2 * CHILDREN * K0
ALL = ("grp", "hi", "mid", "core")
INSIDE = ("grp", "mid")
F32 = jnp.float32
BF16 = jnp.bfloat16
ROOM = pltpu.CompilerParams(vmem_limit_bytes=58 * 2**20)


def cost(megabytes):
    return pl.CostEstimate(flops=10**6, bytes_accessed=megabytes * 10**6, transcendentals=0)


def passed_along(array, by):
    size = lax.axis_size(ALL)
    pairs = [(i, i + by) for i in range(size) if 0 <= i + by < size]
    return lax.ppermute(array, ALL, pairs)


def across(array, axis):
    return lax.ppermute(array, axis, [(0, 1), (1, 0)])


def swap_halves(array):
    return pltpu.roll(array, HALF, 1)


def low_lanes(rows):
    return lax.broadcasted_iota(jnp.int32, (rows, LANES), 1) < HALF


def times_transposed(left, right):
    return lax.dot_general(left, right, (((1,), (1,)), ((), ())), preferred_element_type=F32)


def own_columns(pieces):
    child = lax.broadcasted_iota(jnp.int32, (R, WIDE), 1) // U
    picked = pieces[0]
    for i in range(1, CHILDREN):
        picked = jnp.where(child == i, pieces[i], picked)
    return picked


def leaf_kernel(hi_ref, cur_ref, rad_ref, own_ref, other_ref):
    low_half = hi_ref[0] == 0
    boxes = cur_ref.shape[2] // WIDE
    low = low_lanes(2 * R)
    row_child = lax.broadcasted_iota(jnp.int32, (2 * R * CHILDREN, WIDE), 0) // (2 * R)
    col_child = lax.broadcasted_iota(jnp.int32, (2 * R * CHILDREN, WIDE), 1) // U
    diagonal = row_child == col_child
    for pair in range(boxes // 2):
        found = []
        for box in (2 * pair, 2 * pair + 1):
            cols = slice(box * WIDE, (box + 1) * WIDE)
            own = [cur_ref[0, :, cols].astype(F32), cur_ref[1, :, cols].astype(F32)]
            spread = jnp.where(diagonal, jnp.concatenate(own * CHILDREN, axis=0), 0.0)
            slab = jnp.concatenate([rad_ref[0, cols, :], rad_ref[1, cols, :]], axis=1)
            found.append(jnp.dot(spread.astype(BF16), slab, preferred_element_type=F32))
        for i in range(CHILDREN):
            by_real = jnp.concatenate([f[2 * R * i : 2 * R * i + R] for f in found], axis=0)
            by_imag = jnp.concatenate([f[2 * R * i + R : 2 * R * (i + 1)] for f in found], axis=0)
            real = by_real[:, :LANES] - by_imag[:, LANES:]
            imag = by_real[:, LANES:] + by_imag[:, :LANES]
            zero = jnp.where(low, real, swap_halves(imag))
            one = jnp.where(low, swap_halves(real), imag)
            rows = slice(pair * 2 * R, (pair + 1) * 2 * R)
            cols = slice(i * LANES, (i + 1) * LANES)
            own_ref[rows, cols] = jnp.where(low_half, zero, one).astype(BF16)
            other_ref[rows, cols] = jnp.where(low_half, one, zero).astype(BF16)


def leaves(hi, currents, radiation):
    width = currents.shape[2]
    rows = width // WIDE * R
    steps = 4
    per_step = width // steps
    shape = jax.ShapeDtypeStruct((rows, DEPTH), BF16)
    spec = pl.BlockSpec((rows // steps, DEPTH), lambda s, *_: (s, 0))
    return pl.pallas_call(
        leaf_kernel,
        grid_spec=pltpu.PrefetchScalarGridSpec(
            num_scalar_prefetch=1,
            grid=(steps,),
            in_specs=[
                pl.BlockSpec((2, R, per_step), lambda s, *_: (0, 0, s)),
                pl.BlockSpec((2, per_step, LANES), lambda s, *_: (0, s, 0)),
            ],
            out_specs=[spec, spec],
        ),
        out_shape=[shape, shape],
        compiler_params=ROOM,
        cost_estimate=cost(1),
        name="leaves",
    )(hi, currents, radiation)


def put_patterns(box_ref, patterns):
    boxes = patterns.shape[0] // R
    for chip in range(box_ref.shape[0]):
        real = patterns[:, 2 * chip * LANES : (2 * chip + 1) * LANES].reshape(boxes, 1, R, LANES)
        imag = patterns[:, (2 * chip + 1) * LANES : (2 * chip + 2) * LANES].reshape(boxes, 1, R, LANES)
        both = jnp.concatenate([real, imag], axis=1).reshape(boxes * 2 * R, LANES)
        box_ref[chip] = both.astype(BF16)


def up_kernel(lhs_ref, interp_ref, angle_ref, box_ref, mat_ref):
    cosine, sine = jnp.cos(angle_ref[...]), jnp.sin(angle_ref[...])
    for chip in range(box_ref.shape[0]):
        cols = slice(chip * LANES, (chip + 1) * LANES)
        to_real = slice(2 * chip * LANES, (2 * chip + 1) * LANES)
        to_imag = slice((2 * chip + 1) * LANES, (2 * chip + 2) * LANES)
        weights = interp_ref[:, cols].astype(F32)
        for i in range(CHILDREN):
            from_real = slice(2 * i * K0, (2 * i + 1) * K0)
            from_imag = slice((2 * i + 1) * K0, (2 * i + 2) * K0)
            even, odd = weights * cosine[i : i + 1, cols], weights * sine[i : i + 1, cols]
            mat_ref[from_real, to_real] = even.astype(BF16)
            mat_ref[from_real, to_imag] = odd.astype(BF16)
            mat_ref[from_imag, to_real] = (-odd).astype(BF16)
            mat_ref[from_imag, to_imag] = even.astype(BF16)
    put_patterns(box_ref, jnp.dot(lhs_ref[...], mat_ref[...], preferred_element_type=F32))


def again_kernel(lhs_ref, mat_ref, box_ref):
    put_patterns(box_ref, jnp.dot(lhs_ref[...], mat_ref[...], preferred_element_type=F32))


def to_boxes(lhs, interp, angle):
    rows = lhs.shape[0]
    steps = 4
    chips = CHIPS // steps
    return pl.pallas_call(
        up_kernel,
        grid=(steps,),
        in_specs=[
            pl.BlockSpec((rows, DEPTH), lambda s: (0, 0)),
            pl.BlockSpec((K0, chips * LANES), lambda s: (0, s)),
            pl.BlockSpec((CHILDREN, chips * LANES), lambda s: (0, s)),
        ],
        out_specs=[
            pl.BlockSpec((chips, 2 * rows, LANES), lambda s: (s, 0, 0)),
            pl.BlockSpec((DEPTH, 2 * chips * LANES), lambda s: (0, s)),
        ],
        out_shape=[
            jax.ShapeDtypeStruct((CHIPS, 2 * rows, LANES), BF16),
            jax.ShapeDtypeStruct((DEPTH, 2 * K1), BF16),
        ],
        compiler_params=ROOM,
        cost_estimate=cost(1),
        name="to_boxes",
    )(lhs, interp, angle)


def to_boxes_again(lhs, matrix):
    rows = lhs.shape[0]
    steps = 4
    chips = CHIPS // steps
    return pl.pallas_call(
        again_kernel,
        grid=(steps,),
        in_specs=[
            pl.BlockSpec((rows, DEPTH), lambda s: (0, 0)),
            pl.BlockSpec((DEPTH, 2 * chips * LANES), lambda s: (0, s)),
        ],
        out_specs=pl.BlockSpec((chips, 2 * rows, LANES), lambda s: (s, 0, 0)),
        out_shape=jax.ShapeDtypeStruct((CHIPS, 2 * rows, LANES), BF16),
        compiler_params=ROOM,
        cost_estimate=cost(70),
        name="to_boxes_again",
    )(lhs, matrix)


def translate_kernel(list_ref, oper_ref, one_ref, two_ref, three_ref, four_ref, out_ref, box_ref, table_ref, sems, *, group):
    step = pl.program_id(0)
    per_step = out_ref.shape[0]

    @pl.when(step == 0)
    def fetch():
        copies = []
        for at, source in enumerate((one_ref, two_ref, three_ref, four_ref)):
            boxes = source.shape[0]
            copies.append(pltpu.make_async_copy(source, box_ref.at[pl.ds(at * boxes, boxes)], sems.at[at]))
        for copy in copies:
            copy.start()

        def spread(at, _):
            for part in range(2):
                some = oper_ref[part, pl.ds(pl.multiple_of(at * R, R), R), :]
                for one in range(R):
                    table_ref[at * R + one, part] = jnp.broadcast_to(some[one : one + 1], (R, LANES))
            return 0

        lax.fori_loop(0, oper_ref.shape[1] // R, spread, 0)
        for copy in copies:
            copy.wait()

    def body(at, _):
        first = (step * per_step + at * group) * (2 * IL)
        done = []
        for k in range(group):
            real = imag = None
            for j in range(IL):
                entry = first + k * 2 * IL + j
                tile = box_ref[list_ref[entry]].astype(F32)
                offset = list_ref[entry + IL]
                by_real, by_imag = table_ref[offset, 0], table_ref[offset, 1]
                box_real, box_imag = tile[:R], tile[R:]
                one = by_real * box_real - by_imag * box_imag
                two = by_real * box_imag + by_imag * box_real
                real = one if j == 0 else real + one
                imag = two if j == 0 else imag + two
            done.append(jnp.concatenate([real, imag], axis=0).astype(BF16))
        for k in range(group):
            out_ref[at * group + k] = done[k]
        return 0

    lax.fori_loop(0, per_step // group, body, 0)


def translate(lists, operators, parts):
    targets = lists.shape[0] // (2 * IL)
    boxes = parts[0].shape[0]
    steps = 2
    per_step = targets // steps
    anywhere = pl.BlockSpec(memory_space=pl.ANY)
    return pl.pallas_call(
        functools.partial(translate_kernel, group=8),
        grid_spec=pltpu.PrefetchScalarGridSpec(
            num_scalar_prefetch=1,
            grid=(steps,),
            in_specs=[pl.BlockSpec(operators.shape, lambda s, *_: (0, 0, 0))] + [anywhere] * 4,
            out_specs=pl.BlockSpec((per_step, 2 * R, LANES), lambda s, *_: (s, 0, 0)),
            scratch_shapes=[
                pltpu.VMEM((4 * boxes, 2 * R, LANES), BF16),
                pltpu.VMEM((operators.shape[1], 2, R, LANES), F32),
                pltpu.SemaphoreType.DMA((4,)),
            ],
        ),
        out_shape=jax.ShapeDtypeStruct((targets, 2 * R, LANES), BF16),
        compiler_params=ROOM,
        cost_estimate=cost(25),
        name="translate",
    )(lists, operators, *parts)


def near_kernel(idx_ref, below_ref, own_ref, above_ref, blocks_ref, out_ref, table_ref, lhs_ref):
    step = pl.program_id(0)
    width = own_ref.shape[2]
    per_source = width // LANES
    clusters = blocks_ref.shape[1] // U
    per_tile = LANES // U
    place = lax.broadcasted_iota(jnp.int32, (2 * R, LANES), 1) // U

    @pl.when(step == 0)
    def fill():
        unrolled = 4
        for at, source in enumerate((below_ref, own_ref, above_ref)):

            def body(some, _):
                for one in range(unrolled):
                    tile = some * unrolled + one
                    cols = pl.ds(pl.multiple_of(tile * LANES, LANES), LANES)
                    parts = [source[0, :, cols].astype(F32), source[1, :, cols].astype(F32)]
                    whole = jnp.concatenate(parts, axis=0)
                    turned = [whole] + [pltpu.roll(whole, n * U, 1) for n in range(1, per_tile)]
                    for a in range(per_tile):
                        copied = turned[(0 - a) % per_tile]
                        for g in range(1, per_tile):
                            copied = jnp.where(place == g, turned[(g - a) % per_tile], copied)
                        table_ref[(at * per_source + tile) * per_tile + a] = copied
                return 0

            lax.fori_loop(0, per_source // unrolled, body, 0)
        table_ref[3 * per_source * per_tile] = jnp.zeros((2 * R, LANES), F32)

    def body(some, _):
        for one in range(CHILDREN):
            c = some * CHILDREN + one
            entry = (step * clusters + c) * NBR
            for half in range(NBR // per_tile):
                joined = table_ref[idx_ref[entry + half * per_tile]]
                for k in range(1, per_tile):
                    joined = jnp.where(place == k, table_ref[idx_ref[entry + half * per_tile + k]], joined)
                first = pl.multiple_of(c * 2 * R, 2 * R)
                lhs_ref[pl.ds(first, 2 * R), half * LANES : (half + 1) * LANES] = joined.astype(BF16)
        return 0

    lax.fori_loop(0, clusters // CHILDREN, body, 0)
    for box in range(clusters // CHILDREN):
        rows = slice(box * 2 * R * CHILDREN, (box + 1) * 2 * R * CHILDREN)
        cols = slice(box * WIDE, (box + 1) * WIDE)
        by_real = times_transposed(lhs_ref[rows, :], blocks_ref[0, cols, :])
        by_imag = times_transposed(lhs_ref[rows, :], blocks_ref[1, cols, :])
        real = []
        imag = []
        for i in range(CHILDREN):
            top = slice(2 * R * i, 2 * R * i + R)
            bottom = slice(2 * R * i + R, 2 * R * (i + 1))
            real.append(by_real[top] - by_imag[bottom])
            imag.append(by_imag[top] + by_real[bottom])
        out_ref[0, :, cols] = own_columns(real)
        out_ref[1, :, cols] = own_columns(imag)


def near_part(index, below, own, above, blocks):
    width = own.shape[2]
    steps = 8
    per_step = width // steps
    whole = pl.BlockSpec((2, R, width), lambda s, *_: (0, 0, 0))
    return pl.pallas_call(
        near_kernel,
        grid_spec=pltpu.PrefetchScalarGridSpec(
            num_scalar_prefetch=1,
            grid=(steps,),
            in_specs=[whole, whole, whole, pl.BlockSpec((2, per_step, NBR * U), lambda s, *_: (0, s, 0))],
            out_specs=pl.BlockSpec((2, R, per_step), lambda s, *_: (0, 0, s)),
            scratch_shapes=[
                pltpu.VMEM((3 * width // U + 1, 2 * R, LANES), F32),
                pltpu.VMEM((per_step // U * 2 * R, NBR * U), BF16),
            ],
        ),
        out_shape=jax.ShapeDtypeStruct((2, R, width), F32),
        compiler_params=ROOM,
        cost_estimate=cost(1),
        name="near_part",
    )(index, below, own, above, blocks)


def down_kernel(got_ref, mat_ref, out_ref, sum_ref):
    step = pl.program_id(0)
    last = pl.num_programs(0) - 1
    pieces = []
    for chip in range(got_ref.shape[0]):
        both = got_ref[chip].astype(F32).reshape(-1, 2, R, LANES)
        pieces += [both[:, 0].reshape(-1, LANES), both[:, 1].reshape(-1, LANES)]
    added = times_transposed(jnp.concatenate(pieces, axis=1).astype(BF16), mat_ref[...])

    @pl.when(step == 0)
    def begin():
        sum_ref[...] = added

    @pl.when(jnp.logical_and(step > 0, step < last))
    def go_on():
        sum_ref[...] += added

    @pl.when(step == last)
    def end():
        out_ref[...] = (sum_ref[...] + added).astype(BF16)


def from_boxes(received, matrix):
    rows = received.shape[1] // 2
    steps = 4
    chips = CHIPS // steps
    return pl.pallas_call(
        down_kernel,
        grid=(steps,),
        in_specs=[
            pl.BlockSpec((chips, 2 * rows, LANES), lambda s: (s, 0, 0)),
            pl.BlockSpec((DEPTH, 2 * chips * LANES), lambda s: (0, s)),
        ],
        out_specs=pl.BlockSpec((rows, DEPTH), lambda s: (0, 0)),
        out_shape=jax.ShapeDtypeStruct((rows, DEPTH), BF16),
        scratch_shapes=[pltpu.VMEM((rows, DEPTH), F32)],
        compiler_params=ROOM,
        cost_estimate=cost(1),
        name="from_boxes",
    )(received, matrix)


def far_kernel(hi_ref, own_ref, other_ref, rad_ref, near_ref, out_ref):
    low_half = hi_ref[0] == 0
    boxes = out_ref.shape[2] // WIDE
    low = low_lanes(2 * R)
    for pair in range(boxes // 2):
        rows = slice(pair * 2 * R, (pair + 1) * 2 * R)
        pieces = [[], []]
        for i in range(CHILDREN):
            cols = slice(i * LANES, (i + 1) * LANES)
            own, other = own_ref[rows, cols].astype(F32), other_ref[rows, cols].astype(F32)
            zero, one = jnp.where(low_half, own, other), jnp.where(low_half, other, own)
            real = jnp.where(low, zero, swap_halves(one))
            imag = jnp.where(low, swap_halves(zero), one)
            for k in range(2):
                part = slice(k * R, (k + 1) * R)
                pieces[k].append(jnp.concatenate([real[part], imag[part]], axis=1))
                pieces[k].append(jnp.concatenate([imag[part], -real[part]], axis=1))
        for k in range(2):
            fields = jnp.concatenate(pieces[k], axis=0).astype(BF16)
            cols = slice((2 * pair + k) * WIDE, (2 * pair + k + 1) * WIDE)
            slab = jnp.concatenate([rad_ref[0, cols, :], rad_ref[1, cols, :]], axis=1)
            terms = times_transposed(fields, slab)
            for part in range(2):
                own = [terms[2 * R * i + part * R : 2 * R * i + (part + 1) * R] for i in range(CHILDREN)]
                out_ref[part, :, cols] = near_ref[part, :, cols] + own_columns(own)


def far_part(hi, own, other, radiation, near_field):
    width = near_field.shape[2]
    rows = own.shape[0]
    steps = 4
    per_step = width // steps
    field = pl.BlockSpec((rows // steps, DEPTH), lambda s, *_: (s, 0))
    wave = pl.BlockSpec((2, R, per_step), lambda s, *_: (0, 0, s))
    return pl.pallas_call(
        far_kernel,
        grid_spec=pltpu.PrefetchScalarGridSpec(
            num_scalar_prefetch=1,
            grid=(steps,),
            in_specs=[field, field, pl.BlockSpec((2, per_step, LANES), lambda s, *_: (0, s, 0)), wave],
            out_specs=wave,
        ),
        out_shape=jax.ShapeDtypeStruct((2, R, width), F32),
        compiler_params=ROOM,
        cost_estimate=cost(1),
        name="far_part",
    )(hi, own, other, radiation, near_field)


def swapped(array):
    return lax.all_to_all(array, INSIDE, split_axis=0, concat_axis=0, tiled=True)


def padded(array):
    return jnp.pad(array, [(0, 0)] * (array.ndim - 1) + [(0, LANES - array.shape[-1])])


def to_owners(boxes, samples):
    rows = boxes.shape[1]
    if samples != LANES:
        boxes = boxes.reshape(CHIPS, rows, LANES // samples, samples).transpose(0, 2, 1, 3).reshape(-1, rows, samples)
    got = swapped(boxes)
    if samples != LANES:
        got = padded(got)
    return got.reshape(-1, 2 * R, LANES)


def from_owners(fields, rows, samples):
    fields = fields.reshape(-1, rows, LANES)
    if samples == LANES:
        return swapped(fields)
    got = swapped(fields[..., :samples]).reshape(CHIPS, LANES // samples, rows, samples)
    return got.transpose(0, 2, 1, 3).reshape(CHIPS, rows, LANES)


def operator_table(translation):
    groups, mids = lax.axis_size("grp"), lax.axis_size("mid")
    core = lax.axis_index("core")
    got = []
    for turned in range(2):
        pairs = [
            (((h * groups + g) * mids + m) * 2 + (c ^ turned), ((g * 2 + h) * mids + m) * 2 + c)
            for g in range(groups)
            for h in range(2)
            for m in range(mids)
            for c in range(2)
        ]
        got.append(lax.ppermute(translation, ALL, pairs).astype(F32))
    low = jnp.where(core == 0, got[0], got[1])
    high = jnp.where(core == 0, got[1], got[0])
    operator = padded(jnp.concatenate([low, high], axis=2))
    return jnp.pad(operator, ((0, 0), (0, -operator.shape[1] % R), (0, 0)))


def target_lists(trans_box, trans_off, hi, core):
    groups, mids = lax.axis_size("grp"), lax.axis_size("mid")
    total = trans_box.shape[0]
    per = total // (groups * mids * 4)
    device, inside = trans_box // per, trans_box % per
    group, side = device // (4 * mids), device // (2 * mids) % 2
    mid, its_core = device // 2 % mids, device % 2
    block = (side ^ hi) * 2 + (its_core ^ core)
    place = (block * (groups * mids) + group * mids + mid) * per + inside
    lists = jnp.concatenate([place, trans_off], axis=1).reshape(groups, 2, mids, 2, per, 2 * IL)
    lists = jnp.where(core == 0, lists[:, :, :, 0], lists[:, :, :, 1])
    first, second = lists[:, 0].reshape(-1), lists[:, 1].reshape(-1)
    return jnp.where(hi == 0, first, second), jnp.where(hi == 0, second, first)


def local(
    currents,
    near_blocks,
    near_list,
    near_count,
    radiation,
    interp,
    shift_angle,
    translation,
    trans_box,
    trans_off,
):
    clusters = near_list.shape[0]
    samples = 2 * translation.shape[2]
    rows = clusters // CHILDREN * 2 * R
    hi, core = lax.axis_index("hi"), lax.axis_index("core")
    side = hi.reshape(1).astype(jnp.int32)
    radiation = radiation.reshape(2, clusters * U, LANES)
    near_blocks = near_blocks.reshape(2, clusters * U, NBR * U)

    below = passed_along(currents, 1)
    above = passed_along(currents, -1)
    first = (lax.axis_index(ALL) - 1) * clusters
    live = jnp.arange(NBR, dtype=jnp.int32)[None, :] < near_count[:, None]
    index = jnp.where(live, near_list - first, 3 * clusters).reshape(-1)

    leaf_own, leaf_other = leaves(side, currents, radiation)
    leaf_partner = across(leaf_other, "hi")
    boxes_own, matrix = to_boxes(leaf_own, interp, shift_angle)
    rows_own = to_owners(boxes_own, samples)
    swapped_own = across(rows_own, "core")
    near_field = near_part(index, below, currents, above, near_blocks)
    leaf_partner, near_field = lax.optimization_barrier((leaf_partner, near_field))
    rows_partner = to_owners(to_boxes_again(leaf_partner, matrix), samples)
    parts = (rows_own, swapped_own, rows_partner, across(rows_partner, "core"))

    operators = operator_table(translation)
    list_own, list_partner = target_lists(trans_box, trans_off, hi, core)
    fields_partner = translate(list_partner, operators, parts)
    down_partner = from_boxes(from_owners(fields_partner, rows, samples), matrix)
    down_other = across(down_partner, "hi")
    fields_own = translate(list_own, operators, parts)
    down_own = from_boxes(from_owners(fields_own, rows, samples), matrix)
    return far_part(side, down_own, down_other, radiation, near_field)


def solution(mesh):
    devices = mesh.devices
    groups, rest = devices.shape
    cut = Mesh(devices.reshape(groups, 2, rest // 4, 2), ALL)
    placed = (
        P(None, None, ALL),
        P(None, ALL, None, None),
        P(ALL, None),
        P(ALL),
        P(None, ALL, None, None),
        P(),
        P(),
        P(None, None, ALL),
        P(),
        P(),
    )
    return jax.shard_map(local, mesh=cut, in_specs=placed, out_specs=P(None, None, ALL), check_vma=False)
```

```python
import functools

import jax
import jax.numpy as jnp
from jax import lax
from jax.experimental import pallas as pl
from jax.experimental.pallas import tpu as pltpu
from jax.sharding import Mesh
from jax.sharding import PartitionSpec as P

R = 8
U = 32
NBR = 8
K0 = 64
K1 = 1024
IL = 12
CHILDREN = 8
WIDE = CHILDREN * U
LANES = 128
HALF = 64
CHIPS = K1 // LANES
DEPTH = 2 * CHILDREN * K0
ALL = ("grp", "hi", "mid", "core")
INSIDE = ("grp", "mid")
F32 = jnp.float32
BF16 = jnp.bfloat16
ROOM = pltpu.CompilerParams(vmem_limit_bytes=58 * 2**20)


def cost(megabytes):
    return pl.CostEstimate(flops=10**6, bytes_accessed=megabytes * 10**6, transcendentals=0)


def passed_along(array, by):
    size = lax.axis_size(ALL)
    pairs = [(i, i + by) for i in range(size) if 0 <= i + by < size]
    return lax.ppermute(array, ALL, pairs)


def across(array, axis):
    return lax.ppermute(array, axis, [(0, 1), (1, 0)])


def swap_halves(array):
    return pltpu.roll(array, HALF, 1)


def low_lanes(rows):
    return lax.broadcasted_iota(jnp.int32, (rows, LANES), 1) < HALF


def times_transposed(left, right):
    return lax.dot_general(left, right, (((1,), (1,)), ((), ())), preferred_element_type=F32)


def own_columns(pieces):
    child = lax.broadcasted_iota(jnp.int32, (R, WIDE), 1) // U
    picked = pieces[0]
    for i in range(1, CHILDREN):
        picked = jnp.where(child == i, pieces[i], picked)
    return picked


def leaf_kernel(hi_ref, cur_ref, rad_ref, own_ref, other_ref):
    low_half = hi_ref[0] == 0
    boxes = cur_ref.shape[2] // WIDE
    low = low_lanes(2 * R)
    row_child = lax.broadcasted_iota(jnp.int32, (2 * R * CHILDREN, WIDE), 0) // (2 * R)
    col_child = lax.broadcasted_iota(jnp.int32, (2 * R * CHILDREN, WIDE), 1) // U
    diagonal = row_child == col_child
    for pair in range(boxes // 2):
        found = []
        for box in (2 * pair, 2 * pair + 1):
            cols = slice(box * WIDE, (box + 1) * WIDE)
            own = [cur_ref[0, :, cols].astype(F32), cur_ref[1, :, cols].astype(F32)]
            spread = jnp.where(diagonal, jnp.concatenate(own * CHILDREN, axis=0), 0.0)
            slab = jnp.concatenate([rad_ref[0, cols, :], rad_ref[1, cols, :]], axis=1)
            found.append(jnp.dot(spread.astype(BF16), slab, preferred_element_type=F32))
        for i in range(CHILDREN):
            by_real = jnp.concatenate([f[2 * R * i : 2 * R * i + R] for f in found], axis=0)
            by_imag = jnp.concatenate([f[2 * R * i + R : 2 * R * (i + 1)] for f in found], axis=0)
            real = by_real[:, :LANES] - by_imag[:, LANES:]
            imag = by_real[:, LANES:] + by_imag[:, :LANES]
            zero = jnp.where(low, real, swap_halves(imag))
            one = jnp.where(low, swap_halves(real), imag)
            rows = slice(pair * 2 * R, (pair + 1) * 2 * R)
            cols = slice(i * LANES, (i + 1) * LANES)
            own_ref[rows, cols] = jnp.where(low_half, zero, one).astype(BF16)
            other_ref[rows, cols] = jnp.where(low_half, one, zero).astype(BF16)


def leaves(hi, currents, radiation):
    width = currents.shape[2]
    rows = width // WIDE * R
    steps = 4
    per_step = width // steps
    shape = jax.ShapeDtypeStruct((rows, DEPTH), BF16)
    spec = pl.BlockSpec((rows // steps, DEPTH), lambda s, *_: (s, 0))
    return pl.pallas_call(
        leaf_kernel,
        grid_spec=pltpu.PrefetchScalarGridSpec(
            num_scalar_prefetch=1,
            grid=(steps,),
            in_specs=[
                pl.BlockSpec((2, R, per_step), lambda s, *_: (0, 0, s)),
                pl.BlockSpec((2, per_step, LANES), lambda s, *_: (0, s, 0)),
            ],
            out_specs=[spec, spec],
        ),
        out_shape=[shape, shape],
        compiler_params=ROOM,
        cost_estimate=cost(1),
        name="leaves",
    )(hi, currents, radiation)


def put_patterns(box_ref, patterns):
    boxes = patterns.shape[0] // R
    for chip in range(box_ref.shape[0]):
        real = patterns[:, 2 * chip * LANES : (2 * chip + 1) * LANES].reshape(boxes, 1, R, LANES)
        imag = patterns[:, (2 * chip + 1) * LANES : (2 * chip + 2) * LANES].reshape(boxes, 1, R, LANES)
        both = jnp.concatenate([real, imag], axis=1).reshape(boxes * 2 * R, LANES)
        box_ref[chip] = both.astype(BF16)


def up_kernel(lhs_ref, interp_ref, angle_ref, box_ref, mat_ref):
    cosine, sine = jnp.cos(angle_ref[...]), jnp.sin(angle_ref[...])
    for chip in range(box_ref.shape[0]):
        cols = slice(chip * LANES, (chip + 1) * LANES)
        to_real = slice(2 * chip * LANES, (2 * chip + 1) * LANES)
        to_imag = slice((2 * chip + 1) * LANES, (2 * chip + 2) * LANES)
        weights = interp_ref[:, cols].astype(F32)
        for i in range(CHILDREN):
            from_real = slice(2 * i * K0, (2 * i + 1) * K0)
            from_imag = slice((2 * i + 1) * K0, (2 * i + 2) * K0)
            even, odd = weights * cosine[i : i + 1, cols], weights * sine[i : i + 1, cols]
            mat_ref[from_real, to_real] = even.astype(BF16)
            mat_ref[from_real, to_imag] = odd.astype(BF16)
            mat_ref[from_imag, to_real] = (-odd).astype(BF16)
            mat_ref[from_imag, to_imag] = even.astype(BF16)
    put_patterns(box_ref, jnp.dot(lhs_ref[...], mat_ref[...], preferred_element_type=F32))


def again_kernel(lhs_ref, mat_ref, box_ref):
    put_patterns(box_ref, jnp.dot(lhs_ref[...], mat_ref[...], preferred_element_type=F32))


def to_boxes(lhs, interp, angle):
    rows = lhs.shape[0]
    steps = 4
    chips = CHIPS // steps
    return pl.pallas_call(
        up_kernel,
        grid=(steps,),
        in_specs=[
            pl.BlockSpec((rows, DEPTH), lambda s: (0, 0)),
            pl.BlockSpec((K0, chips * LANES), lambda s: (0, s)),
            pl.BlockSpec((CHILDREN, chips * LANES), lambda s: (0, s)),
        ],
        out_specs=[
            pl.BlockSpec((chips, 2 * rows, LANES), lambda s: (s, 0, 0)),
            pl.BlockSpec((DEPTH, 2 * chips * LANES), lambda s: (0, s)),
        ],
        out_shape=[
            jax.ShapeDtypeStruct((CHIPS, 2 * rows, LANES), BF16),
            jax.ShapeDtypeStruct((DEPTH, 2 * K1), BF16),
        ],
        compiler_params=ROOM,
        cost_estimate=cost(1),
        name="to_boxes",
    )(lhs, interp, angle)


def to_boxes_again(lhs, matrix):
    rows = lhs.shape[0]
    steps = 4
    chips = CHIPS // steps
    return pl.pallas_call(
        again_kernel,
        grid=(steps,),
        in_specs=[
            pl.BlockSpec((rows, DEPTH), lambda s: (0, 0)),
            pl.BlockSpec((DEPTH, 2 * chips * LANES), lambda s: (0, s)),
        ],
        out_specs=pl.BlockSpec((chips, 2 * rows, LANES), lambda s: (s, 0, 0)),
        out_shape=jax.ShapeDtypeStruct((CHIPS, 2 * rows, LANES), BF16),
        compiler_params=ROOM,
        cost_estimate=cost(4000),
        name="to_boxes_again",
    )(lhs, matrix)


def translate_kernel(list_ref, oper_ref, one_ref, two_ref, three_ref, four_ref, out_ref, box_ref, table_ref, sems, *, group):
    step = pl.program_id(0)
    per_step = out_ref.shape[0]

    @pl.when(step == 0)
    def fetch():
        copies = []
        for at, source in enumerate((one_ref, two_ref, three_ref, four_ref)):
            boxes = source.shape[0]
            copies.append(pltpu.make_async_copy(source, box_ref.at[pl.ds(at * boxes, boxes)], sems.at[at]))
        for copy in copies:
            copy.start()

        def spread(at, _):
            for part in range(2):
                some = oper_ref[part, pl.ds(pl.multiple_of(at * R, R), R), :]
                for one in range(R):
                    table_ref[at * R + one, part] = jnp.broadcast_to(some[one : one + 1], (R, LANES))
            return 0

        lax.fori_loop(0, oper_ref.shape[1] // R, spread, 0)
        for copy in copies:
            copy.wait()

    def body(at, _):
        first = (step * per_step + at * group) * (2 * IL)
        done = []
        for k in range(group):
            real = imag = None
            for j in range(IL):
                entry = first + k * 2 * IL + j
                tile = box_ref[list_ref[entry]].astype(F32)
                offset = list_ref[entry + IL]
                by_real, by_imag = table_ref[offset, 0], table_ref[offset, 1]
                box_real, box_imag = tile[:R], tile[R:]
                one = by_real * box_real - by_imag * box_imag
                two = by_real * box_imag + by_imag * box_real
                real = one if j == 0 else real + one
                imag = two if j == 0 else imag + two
            done.append(jnp.concatenate([real, imag], axis=0).astype(BF16))
        for k in range(group):
            out_ref[at * group + k] = done[k]
        return 0

    lax.fori_loop(0, per_step // group, body, 0)


def translate(lists, operators, parts):
    targets = lists.shape[0] // (2 * IL)
    boxes = parts[0].shape[0]
    steps = 2
    per_step = targets // steps
    anywhere = pl.BlockSpec(memory_space=pl.ANY)
    return pl.pallas_call(
        functools.partial(translate_kernel, group=8),
        grid_spec=pltpu.PrefetchScalarGridSpec(
            num_scalar_prefetch=1,
            grid=(steps,),
            in_specs=[pl.BlockSpec(operators.shape, lambda s, *_: (0, 0, 0))] + [anywhere] * 4,
            out_specs=pl.BlockSpec((per_step, 2 * R, LANES), lambda s, *_: (s, 0, 0)),
            scratch_shapes=[
                pltpu.VMEM((4 * boxes, 2 * R, LANES), BF16),
                pltpu.VMEM((operators.shape[1], 2, R, LANES), F32),
                pltpu.SemaphoreType.DMA((4,)),
            ],
        ),
        out_shape=jax.ShapeDtypeStruct((targets, 2 * R, LANES), BF16),
        compiler_params=ROOM,
        cost_estimate=cost(25),
        name="translate",
    )(lists, operators, *parts)


def near_kernel(idx_ref, below_ref, own_ref, above_ref, blocks_ref, out_ref, table_ref, lhs_ref):
    step = pl.program_id(0)
    width = own_ref.shape[2]
    per_source = width // LANES
    clusters = blocks_ref.shape[1] // U
    per_tile = LANES // U
    place = lax.broadcasted_iota(jnp.int32, (2 * R, LANES), 1) // U

    @pl.when(step == 0)
    def fill():
        unrolled = 4
        for at, source in enumerate((below_ref, own_ref, above_ref)):

            def body(some, _):
                for one in range(unrolled):
                    tile = some * unrolled + one
                    cols = pl.ds(pl.multiple_of(tile * LANES, LANES), LANES)
                    parts = [source[0, :, cols].astype(F32), source[1, :, cols].astype(F32)]
                    whole = jnp.concatenate(parts, axis=0)
                    turned = [whole] + [pltpu.roll(whole, n * U, 1) for n in range(1, per_tile)]
                    for a in range(per_tile):
                        copied = turned[(0 - a) % per_tile]
                        for g in range(1, per_tile):
                            copied = jnp.where(place == g, turned[(g - a) % per_tile], copied)
                        table_ref[(at * per_source + tile) * per_tile + a] = copied
                return 0

            lax.fori_loop(0, per_source // unrolled, body, 0)
        table_ref[3 * per_source * per_tile] = jnp.zeros((2 * R, LANES), F32)

    def body(some, _):
        for one in range(CHILDREN):
            c = some * CHILDREN + one
            entry = (step * clusters + c) * NBR
            for half in range(NBR // per_tile):
                joined = table_ref[idx_ref[entry + half * per_tile]]
                for k in range(1, per_tile):
                    joined = jnp.where(place == k, table_ref[idx_ref[entry + half * per_tile + k]], joined)
                first = pl.multiple_of(c * 2 * R, 2 * R)
                lhs_ref[pl.ds(first, 2 * R), half * LANES : (half + 1) * LANES] = joined.astype(BF16)
        return 0

    lax.fori_loop(0, clusters // CHILDREN, body, 0)
    for box in range(clusters // CHILDREN):
        rows = slice(box * 2 * R * CHILDREN, (box + 1) * 2 * R * CHILDREN)
        cols = slice(box * WIDE, (box + 1) * WIDE)
        by_real = times_transposed(lhs_ref[rows, :], blocks_ref[0, cols, :])
        by_imag = times_transposed(lhs_ref[rows, :], blocks_ref[1, cols, :])
        real = []
        imag = []
        for i in range(CHILDREN):
            top = slice(2 * R * i, 2 * R * i + R)
            bottom = slice(2 * R * i + R, 2 * R * (i + 1))
            real.append(by_real[top] - by_imag[bottom])
            imag.append(by_imag[top] + by_real[bottom])
        out_ref[0, :, cols] = own_columns(real)
        out_ref[1, :, cols] = own_columns(imag)


def near_part(index, below, own, above, blocks):
    width = own.shape[2]
    steps = 8
    per_step = width // steps
    whole = pl.BlockSpec((2, R, width), lambda s, *_: (0, 0, 0))
    return pl.pallas_call(
        near_kernel,
        grid_spec=pltpu.PrefetchScalarGridSpec(
            num_scalar_prefetch=1,
            grid=(steps,),
            in_specs=[whole, whole, whole, pl.BlockSpec((2, per_step, NBR * U), lambda s, *_: (0, s, 0))],
            out_specs=pl.BlockSpec((2, R, per_step), lambda s, *_: (0, 0, s)),
            scratch_shapes=[
                pltpu.VMEM((3 * width // U + 1, 2 * R, LANES), F32),
                pltpu.VMEM((per_step // U * 2 * R, NBR * U), BF16),
            ],
        ),
        out_shape=jax.ShapeDtypeStruct((2, R, width), F32),
        compiler_params=ROOM,
        cost_estimate=cost(1),
        name="near_part",
    )(index, below, own, above, blocks)


def down_kernel(got_ref, mat_ref, out_ref, sum_ref):
    step = pl.program_id(0)
    last = pl.num_programs(0) - 1
    pieces = []
    for chip in range(got_ref.shape[0]):
        both = got_ref[chip].astype(F32).reshape(-1, 2, R, LANES)
        pieces += [both[:, 0].reshape(-1, LANES), both[:, 1].reshape(-1, LANES)]
    added = times_transposed(jnp.concatenate(pieces, axis=1).astype(BF16), mat_ref[...])

    @pl.when(step == 0)
    def begin():
        sum_ref[...] = added

    @pl.when(jnp.logical_and(step > 0, step < last))
    def go_on():
        sum_ref[...] += added

    @pl.when(step == last)
    def end():
        out_ref[...] = (sum_ref[...] + added).astype(BF16)


def from_boxes(received, matrix):
    rows = received.shape[1] // 2
    steps = 4
    chips = CHIPS // steps
    return pl.pallas_call(
        down_kernel,
        grid=(steps,),
        in_specs=[
            pl.BlockSpec((chips, 2 * rows, LANES), lambda s: (s, 0, 0)),
            pl.BlockSpec((DEPTH, 2 * chips * LANES), lambda s: (0, s)),
        ],
        out_specs=pl.BlockSpec((rows, DEPTH), lambda s: (0, 0)),
        out_shape=jax.ShapeDtypeStruct((rows, DEPTH), BF16),
        scratch_shapes=[pltpu.VMEM((rows, DEPTH), F32)],
        compiler_params=ROOM,
        cost_estimate=cost(1),
        name="from_boxes",
    )(received, matrix)


def far_kernel(hi_ref, own_ref, other_ref, rad_ref, near_ref, out_ref):
    low_half = hi_ref[0] == 0
    boxes = out_ref.shape[2] // WIDE
    low = low_lanes(2 * R)
    for pair in range(boxes // 2):
        rows = slice(pair * 2 * R, (pair + 1) * 2 * R)
        pieces = [[], []]
        for i in range(CHILDREN):
            cols = slice(i * LANES, (i + 1) * LANES)
            own, other = own_ref[rows, cols].astype(F32), other_ref[rows, cols].astype(F32)
            zero, one = jnp.where(low_half, own, other), jnp.where(low_half, other, own)
            real = jnp.where(low, zero, swap_halves(one))
            imag = jnp.where(low, swap_halves(zero), one)
            for k in range(2):
                part = slice(k * R, (k + 1) * R)
                pieces[k].append(jnp.concatenate([real[part], imag[part]], axis=1))
                pieces[k].append(jnp.concatenate([imag[part], -real[part]], axis=1))
        for k in range(2):
            fields = jnp.concatenate(pieces[k], axis=0).astype(BF16)
            cols = slice((2 * pair + k) * WIDE, (2 * pair + k + 1) * WIDE)
            slab = jnp.concatenate([rad_ref[0, cols, :], rad_ref[1, cols, :]], axis=1)
            terms = times_transposed(fields, slab)
            for part in range(2):
                own = [terms[2 * R * i + part * R : 2 * R * i + (part + 1) * R] for i in range(CHILDREN)]
                out_ref[part, :, cols] = near_ref[part, :, cols] + own_columns(own)


def far_part(hi, own, other, radiation, near_field):
    width = near_field.shape[2]
    rows = own.shape[0]
    steps = 4
    per_step = width // steps
    field = pl.BlockSpec((rows // steps, DEPTH), lambda s, *_: (s, 0))
    wave = pl.BlockSpec((2, R, per_step), lambda s, *_: (0, 0, s))
    return pl.pallas_call(
        far_kernel,
        grid_spec=pltpu.PrefetchScalarGridSpec(
            num_scalar_prefetch=1,
            grid=(steps,),
            in_specs=[field, field, pl.BlockSpec((2, per_step, LANES), lambda s, *_: (0, s, 0)), wave],
            out_specs=wave,
        ),
        out_shape=jax.ShapeDtypeStruct((2, R, width), F32),
        compiler_params=ROOM,
        cost_estimate=cost(1),
        name="far_part",
    )(hi, own, other, radiation, near_field)


def swapped(array):
    return lax.all_to_all(array, INSIDE, split_axis=0, concat_axis=0, tiled=True)


def padded(array):
    return jnp.pad(array, [(0, 0)] * (array.ndim - 1) + [(0, LANES - array.shape[-1])])


def to_owners(boxes, samples):
    rows = boxes.shape[1]
    if samples != LANES:
        boxes = boxes.reshape(CHIPS, rows, LANES // samples, samples).transpose(0, 2, 1, 3).reshape(-1, rows, samples)
    got = swapped(boxes)
    if samples != LANES:
        got = padded(got)
    return got.reshape(-1, 2 * R, LANES)


def from_owners(fields, rows, samples):
    fields = fields.reshape(-1, rows, LANES)
    if samples == LANES:
        return swapped(fields)
    got = swapped(fields[..., :samples]).reshape(CHIPS, LANES // samples, rows, samples)
    return got.transpose(0, 2, 1, 3).reshape(CHIPS, rows, LANES)


def operator_table(translation):
    groups, mids = lax.axis_size("grp"), lax.axis_size("mid")
    core = lax.axis_index("core")
    got = []
    for turned in range(2):
        pairs = [
            (((h * groups + g) * mids + m) * 2 + (c ^ turned), ((g * 2 + h) * mids + m) * 2 + c)
            for g in range(groups)
            for h in range(2)
            for m in range(mids)
            for c in range(2)
        ]
        got.append(lax.ppermute(translation, ALL, pairs).astype(F32))
    low = jnp.where(core == 0, got[0], got[1])
    high = jnp.where(core == 0, got[1], got[0])
    operator = padded(jnp.concatenate([low, high], axis=2))
    return jnp.pad(operator, ((0, 0), (0, -operator.shape[1] % R), (0, 0)))


def target_lists(trans_box, trans_off, hi, core):
    groups, mids = lax.axis_size("grp"), lax.axis_size("mid")
    total = trans_box.shape[0]
    per = total // (groups * mids * 4)
    device, inside = trans_box // per, trans_box % per
    group, side = device // (4 * mids), device // (2 * mids) % 2
    mid, its_core = device // 2 % mids, device % 2
    block = (side ^ hi) * 2 + (its_core ^ core)
    place = (block * (groups * mids) + group * mids + mid) * per + inside
    lists = jnp.concatenate([place, trans_off], axis=1).reshape(groups, 2, mids, 2, per, 2 * IL)
    lists = jnp.where(core == 0, lists[:, :, :, 0], lists[:, :, :, 1])
    first, second = lists[:, 0].reshape(-1), lists[:, 1].reshape(-1)
    return jnp.where(hi == 0, first, second), jnp.where(hi == 0, second, first)


def local(
    currents,
    near_blocks,
    near_list,
    near_count,
    radiation,
    interp,
    shift_angle,
    translation,
    trans_box,
    trans_off,
):
    clusters = near_list.shape[0]
    samples = 2 * translation.shape[2]
    rows = clusters // CHILDREN * 2 * R
    hi, core = lax.axis_index("hi"), lax.axis_index("core")
    side = hi.reshape(1).astype(jnp.int32)
    radiation = radiation.reshape(2, clusters * U, LANES)
    near_blocks = near_blocks.reshape(2, clusters * U, NBR * U)

    first = (lax.axis_index(ALL) - 1) * clusters
    live = jnp.arange(NBR, dtype=jnp.int32)[None, :] < near_count[:, None]
    index = jnp.where(live, near_list - first, 3 * clusters).reshape(-1)
    lists = target_lists(trans_box, trans_off, hi, core)

    leaf_own, leaf_other = leaves(side, currents, radiation)
    leaf_partner = across(leaf_other, "hi")
    boxes_own, matrix = to_boxes(leaf_own, interp, shift_angle)
    rows_own = to_owners(boxes_own, samples)
    swapped_own = across(rows_own, "core")

    leaf_partner, lists, index, late_currents, translation = lax.optimization_barrier(
        (leaf_partner, lists, index, currents, translation)
    )
    rows_partner = to_owners(to_boxes_again(leaf_partner, matrix), samples)
    below = passed_along(late_currents, 1)
    above = passed_along(late_currents, -1)
    operators = operator_table(translation)
    parts = (rows_own, swapped_own, rows_partner, across(rows_partner, "core"))
    parts, operators, below, above = lax.optimization_barrier((parts, operators, below, above))

    fields_partner = translate(lists[1], operators, parts)
    down_partner = from_boxes(from_owners(fields_partner, rows, samples), matrix)
    fields_own = translate(lists[0], operators, parts)
    down_partner, index = lax.optimization_barrier((down_partner, index))
    down_other = across(down_partner, "hi")
    near_field = near_part(index, below, currents, above, near_blocks)
    down_own = from_boxes(from_owners(fields_own, rows, samples), matrix)
    return far_part(side, down_own, down_other, radiation, near_field)


def solution(mesh):
    devices = mesh.devices
    groups, rest = devices.shape
    cut = Mesh(devices.reshape(groups, 2, rest // 4, 2), ALL)
    placed = (
        P(None, None, ALL),
        P(None, ALL, None, None),
        P(ALL, None),
        P(ALL),
        P(None, ALL, None, None),
        P(),
        P(),
        P(None, None, ALL),
        P(),
        P(),
    )
    return jax.shard_map(local, mesh=cut, in_specs=placed, out_specs=P(None, None, ALL), check_vma=False)
```

```python
import functools

import jax
import jax.numpy as jnp
from jax import lax
from jax.experimental import pallas as pl
from jax.experimental.pallas import tpu as pltpu
from jax.sharding import Mesh
from jax.sharding import PartitionSpec as P

R = 8
U = 32
NBR = 8
K0 = 64
K1 = 1024
IL = 12
CHILDREN = 8
WIDE = CHILDREN * U
LANES = 128
HALF = 64
CHIPS = K1 // LANES
DEPTH = 2 * CHILDREN * K0
ALL = ("grp", "hi", "mid", "core")
INSIDE = ("grp", "mid")
F32 = jnp.float32
BF16 = jnp.bfloat16
ROOM = pltpu.CompilerParams(vmem_limit_bytes=58 * 2**20)


def cost(megabytes):
    return pl.CostEstimate(flops=10**6, bytes_accessed=megabytes * 10**6, transcendentals=0)


def passed_along(array, by):
    size = lax.axis_size(ALL)
    pairs = [(i, i + by) for i in range(size) if 0 <= i + by < size]
    return lax.ppermute(array, ALL, pairs)


def across(array, axis):
    return lax.ppermute(array, axis, [(0, 1), (1, 0)])


def swap_halves(array):
    return pltpu.roll(array, HALF, 1)


def low_lanes(rows):
    return lax.broadcasted_iota(jnp.int32, (rows, LANES), 1) < HALF


def times_transposed(left, right):
    return lax.dot_general(left, right, (((1,), (1,)), ((), ())), preferred_element_type=F32)


def own_columns(pieces):
    child = lax.broadcasted_iota(jnp.int32, (R, WIDE), 1) // U
    picked = pieces[0]
    for i in range(1, CHILDREN):
        picked = jnp.where(child == i, pieces[i], picked)
    return picked


def leaf_kernel(hi_ref, cur_ref, rad_ref, own_ref, other_ref):
    low_half = hi_ref[0] == 0
    boxes = cur_ref.shape[2] // WIDE
    low = low_lanes(2 * R)
    row_child = lax.broadcasted_iota(jnp.int32, (2 * R * CHILDREN, WIDE), 0) // (2 * R)
    col_child = lax.broadcasted_iota(jnp.int32, (2 * R * CHILDREN, WIDE), 1) // U
    diagonal = row_child == col_child
    for pair in range(boxes // 2):
        found = []
        for box in (2 * pair, 2 * pair + 1):
            cols = slice(box * WIDE, (box + 1) * WIDE)
            own = [cur_ref[0, :, cols].astype(F32), cur_ref[1, :, cols].astype(F32)]
            spread = jnp.where(diagonal, jnp.concatenate(own * CHILDREN, axis=0), 0.0)
            slab = jnp.concatenate([rad_ref[0, cols, :], rad_ref[1, cols, :]], axis=1)
            found.append(jnp.dot(spread.astype(BF16), slab, preferred_element_type=F32))
        for i in range(CHILDREN):
            by_real = jnp.concatenate([f[2 * R * i : 2 * R * i + R] for f in found], axis=0)
            by_imag = jnp.concatenate([f[2 * R * i + R : 2 * R * (i + 1)] for f in found], axis=0)
            real = by_real[:, :LANES] - by_imag[:, LANES:]
            imag = by_real[:, LANES:] + by_imag[:, :LANES]
            zero = jnp.where(low, real, swap_halves(imag))
            one = jnp.where(low, swap_halves(real), imag)
            rows = slice(pair * 2 * R, (pair + 1) * 2 * R)
            cols = slice(i * LANES, (i + 1) * LANES)
            own_ref[rows, cols] = jnp.where(low_half, zero, one).astype(BF16)
            other_ref[rows, cols] = jnp.where(low_half, one, zero).astype(BF16)


def leaves(hi, currents, radiation):
    width = currents.shape[2]
    rows = width // WIDE * R
    steps = 4
    per_step = width // steps
    shape = jax.ShapeDtypeStruct((rows, DEPTH), BF16)
    spec = pl.BlockSpec((rows // steps, DEPTH), lambda s, *_: (s, 0))
    return pl.pallas_call(
        leaf_kernel,
        grid_spec=pltpu.PrefetchScalarGridSpec(
            num_scalar_prefetch=1,
            grid=(steps,),
            in_specs=[
                pl.BlockSpec((2, R, per_step), lambda s, *_: (0, 0, s)),
                pl.BlockSpec((2, per_step, LANES), lambda s, *_: (0, s, 0)),
            ],
            out_specs=[spec, spec],
        ),
        out_shape=[shape, shape],
        compiler_params=ROOM,
        cost_estimate=cost(1),
        name="leaves",
    )(hi, currents, radiation)


def put_patterns(box_ref, patterns):
    boxes = patterns.shape[0] // R
    for chip in range(box_ref.shape[0]):
        real = patterns[:, 2 * chip * LANES : (2 * chip + 1) * LANES].reshape(boxes, 1, R, LANES)
        imag = patterns[:, (2 * chip + 1) * LANES : (2 * chip + 2) * LANES].reshape(boxes, 1, R, LANES)
        both = jnp.concatenate([real, imag], axis=1).reshape(boxes * 2 * R, LANES)
        box_ref[chip] = both.astype(BF16)


def up_kernel(lhs_ref, interp_ref, angle_ref, box_ref, mat_ref):
    cosine, sine = jnp.cos(angle_ref[...]), jnp.sin(angle_ref[...])
    for chip in range(box_ref.shape[0]):
        cols = slice(chip * LANES, (chip + 1) * LANES)
        to_real = slice(2 * chip * LANES, (2 * chip + 1) * LANES)
        to_imag = slice((2 * chip + 1) * LANES, (2 * chip + 2) * LANES)
        weights = interp_ref[:, cols].astype(F32)
        for i in range(CHILDREN):
            from_real = slice(2 * i * K0, (2 * i + 1) * K0)
            from_imag = slice((2 * i + 1) * K0, (2 * i + 2) * K0)
            even, odd = weights * cosine[i : i + 1, cols], weights * sine[i : i + 1, cols]
            mat_ref[from_real, to_real] = even.astype(BF16)
            mat_ref[from_real, to_imag] = odd.astype(BF16)
            mat_ref[from_imag, to_real] = (-odd).astype(BF16)
            mat_ref[from_imag, to_imag] = even.astype(BF16)
    put_patterns(box_ref, jnp.dot(lhs_ref[...], mat_ref[...], preferred_element_type=F32))


def again_kernel(lhs_ref, mat_ref, box_ref):
    put_patterns(box_ref, jnp.dot(lhs_ref[...], mat_ref[...], preferred_element_type=F32))


def to_boxes(lhs, interp, angle):
    rows = lhs.shape[0]
    steps = 4
    chips = CHIPS // steps
    return pl.pallas_call(
        up_kernel,
        grid=(steps,),
        in_specs=[
            pl.BlockSpec((rows, DEPTH), lambda s: (0, 0)),
            pl.BlockSpec((K0, chips * LANES), lambda s: (0, s)),
            pl.BlockSpec((CHILDREN, chips * LANES), lambda s: (0, s)),
        ],
        out_specs=[
            pl.BlockSpec((chips, 2 * rows, LANES), lambda s: (s, 0, 0)),
            pl.BlockSpec((DEPTH, 2 * chips * LANES), lambda s: (0, s)),
        ],
        out_shape=[
            jax.ShapeDtypeStruct((CHIPS, 2 * rows, LANES), BF16),
            jax.ShapeDtypeStruct((DEPTH, 2 * K1), BF16),
        ],
        compiler_params=ROOM,
        cost_estimate=cost(1),
        name="to_boxes",
    )(lhs, interp, angle)


def to_boxes_again(lhs, matrix):
    rows = lhs.shape[0]
    steps = 4
    chips = CHIPS // steps
    return pl.pallas_call(
        again_kernel,
        grid=(steps,),
        in_specs=[
            pl.BlockSpec((rows, DEPTH), lambda s: (0, 0)),
            pl.BlockSpec((DEPTH, 2 * chips * LANES), lambda s: (0, s)),
        ],
        out_specs=pl.BlockSpec((chips, 2 * rows, LANES), lambda s: (s, 0, 0)),
        out_shape=jax.ShapeDtypeStruct((CHIPS, 2 * rows, LANES), BF16),
        compiler_params=ROOM,
        cost_estimate=cost(6),
        name="to_boxes_again",
    )(lhs, matrix)


def translate_kernel(list_ref, oper_ref, one_ref, two_ref, three_ref, four_ref, out_ref, box_ref, table_ref, sems, *, group):
    step = pl.program_id(0)
    per_step = out_ref.shape[0]

    @pl.when(step == 0)
    def fetch():
        copies = []
        for at, source in enumerate((one_ref, two_ref, three_ref, four_ref)):
            boxes = source.shape[0]
            copies.append(pltpu.make_async_copy(source, box_ref.at[pl.ds(at * boxes, boxes)], sems.at[at]))
        for copy in copies:
            copy.start()

        def spread(at, _):
            for part in range(2):
                some = oper_ref[part, pl.ds(pl.multiple_of(at * R, R), R), :]
                for one in range(R):
                    table_ref[at * R + one, part] = jnp.broadcast_to(some[one : one + 1], (R, LANES))
            return 0

        lax.fori_loop(0, oper_ref.shape[1] // R, spread, 0)
        for copy in copies:
            copy.wait()

    def body(at, _):
        first = (step * per_step + at * group) * (2 * IL)
        done = []
        for k in range(group):
            real = imag = None
            for j in range(IL):
                entry = first + k * 2 * IL + j
                tile = box_ref[list_ref[entry]].astype(F32)
                offset = list_ref[entry + IL]
                by_real, by_imag = table_ref[offset, 0], table_ref[offset, 1]
                box_real, box_imag = tile[:R], tile[R:]
                one = by_real * box_real - by_imag * box_imag
                two = by_real * box_imag + by_imag * box_real
                real = one if j == 0 else real + one
                imag = two if j == 0 else imag + two
            done.append(jnp.concatenate([real, imag], axis=0).astype(BF16))
        for k in range(group):
            out_ref[at * group + k] = done[k]
        return 0

    lax.fori_loop(0, per_step // group, body, 0)


def translate(lists, operators, parts):
    targets = lists.shape[0] // (2 * IL)
    boxes = parts[0].shape[0]
    steps = 2
    per_step = targets // steps
    anywhere = pl.BlockSpec(memory_space=pl.ANY)
    return pl.pallas_call(
        functools.partial(translate_kernel, group=8),
        grid_spec=pltpu.PrefetchScalarGridSpec(
            num_scalar_prefetch=1,
            grid=(steps,),
            in_specs=[pl.BlockSpec(operators.shape, lambda s, *_: (0, 0, 0))] + [anywhere] * 4,
            out_specs=pl.BlockSpec((per_step, 2 * R, LANES), lambda s, *_: (s, 0, 0)),
            scratch_shapes=[
                pltpu.VMEM((4 * boxes, 2 * R, LANES), BF16),
                pltpu.VMEM((operators.shape[1], 2, R, LANES), F32),
                pltpu.SemaphoreType.DMA((4,)),
            ],
        ),
        out_shape=jax.ShapeDtypeStruct((targets, 2 * R, LANES), BF16),
        compiler_params=ROOM,
        cost_estimate=cost(25),
        name="translate",
    )(lists, operators, *parts)


def near_kernel(idx_ref, below_ref, own_ref, above_ref, blocks_ref, out_ref, table_ref, lhs_ref):
    step = pl.program_id(0)
    width = own_ref.shape[2]
    per_source = width // LANES
    clusters = blocks_ref.shape[1] // U
    per_tile = LANES // U
    place = lax.broadcasted_iota(jnp.int32, (2 * R, LANES), 1) // U

    @pl.when(step == 0)
    def fill():
        unrolled = 4
        for at, source in enumerate((below_ref, own_ref, above_ref)):

            def body(some, _):
                for one in range(unrolled):
                    tile = some * unrolled + one
                    cols = pl.ds(pl.multiple_of(tile * LANES, LANES), LANES)
                    parts = [source[0, :, cols].astype(F32), source[1, :, cols].astype(F32)]
                    whole = jnp.concatenate(parts, axis=0)
                    turned = [whole] + [pltpu.roll(whole, n * U, 1) for n in range(1, per_tile)]
                    for a in range(per_tile):
                        copied = turned[(0 - a) % per_tile]
                        for g in range(1, per_tile):
                            copied = jnp.where(place == g, turned[(g - a) % per_tile], copied)
                        table_ref[(at * per_source + tile) * per_tile + a] = copied
                return 0

            lax.fori_loop(0, per_source // unrolled, body, 0)
        table_ref[3 * per_source * per_tile] = jnp.zeros((2 * R, LANES), F32)

    def body(some, _):
        for one in range(CHILDREN):
            c = some * CHILDREN + one
            entry = (step * clusters + c) * NBR
            for half in range(NBR // per_tile):
                joined = table_ref[idx_ref[entry + half * per_tile]]
                for k in range(1, per_tile):
                    joined = jnp.where(place == k, table_ref[idx_ref[entry + half * per_tile + k]], joined)
                first = pl.multiple_of(c * 2 * R, 2 * R)
                lhs_ref[pl.ds(first, 2 * R), half * LANES : (half + 1) * LANES] = joined.astype(BF16)
        return 0

    lax.fori_loop(0, clusters // CHILDREN, body, 0)
    for box in range(clusters // CHILDREN):
        rows = slice(box * 2 * R * CHILDREN, (box + 1) * 2 * R * CHILDREN)
        cols = slice(box * WIDE, (box + 1) * WIDE)
        by_real = times_transposed(lhs_ref[rows, :], blocks_ref[0, cols, :])
        by_imag = times_transposed(lhs_ref[rows, :], blocks_ref[1, cols, :])
        real = []
        imag = []
        for i in range(CHILDREN):
            top = slice(2 * R * i, 2 * R * i + R)
            bottom = slice(2 * R * i + R, 2 * R * (i + 1))
            real.append(by_real[top] - by_imag[bottom])
            imag.append(by_imag[top] + by_real[bottom])
        out_ref[0, :, cols] = own_columns(real)
        out_ref[1, :, cols] = own_columns(imag)


def near_part(index, below, own, above, blocks):
    width = own.shape[2]
    steps = 8
    per_step = width // steps
    whole = pl.BlockSpec((2, R, width), lambda s, *_: (0, 0, 0))
    return pl.pallas_call(
        near_kernel,
        grid_spec=pltpu.PrefetchScalarGridSpec(
            num_scalar_prefetch=1,
            grid=(steps,),
            in_specs=[whole, whole, whole, pl.BlockSpec((2, per_step, NBR * U), lambda s, *_: (0, s, 0))],
            out_specs=pl.BlockSpec((2, R, per_step), lambda s, *_: (0, 0, s)),
            scratch_shapes=[
                pltpu.VMEM((3 * width // U + 1, 2 * R, LANES), F32),
                pltpu.VMEM((per_step // U * 2 * R, NBR * U), BF16),
            ],
        ),
        out_shape=jax.ShapeDtypeStruct((2, R, width), F32),
        compiler_params=ROOM,
        cost_estimate=cost(1),
        name="near_part",
    )(index, below, own, above, blocks)


def down_kernel(got_ref, mat_ref, out_ref, sum_ref):
    step = pl.program_id(0)
    last = pl.num_programs(0) - 1
    pieces = []
    for chip in range(got_ref.shape[0]):
        both = got_ref[chip].astype(F32).reshape(-1, 2, R, LANES)
        pieces += [both[:, 0].reshape(-1, LANES), both[:, 1].reshape(-1, LANES)]
    added = times_transposed(jnp.concatenate(pieces, axis=1).astype(BF16), mat_ref[...])

    @pl.when(step == 0)
    def begin():
        sum_ref[...] = added

    @pl.when(jnp.logical_and(step > 0, step < last))
    def go_on():
        sum_ref[...] += added

    @pl.when(step == last)
    def end():
        out_ref[...] = (sum_ref[...] + added).astype(BF16)


def from_boxes(received, matrix):
    rows = received.shape[1] // 2
    steps = 4
    chips = CHIPS // steps
    return pl.pallas_call(
        down_kernel,
        grid=(steps,),
        in_specs=[
            pl.BlockSpec((chips, 2 * rows, LANES), lambda s: (s, 0, 0)),
            pl.BlockSpec((DEPTH, 2 * chips * LANES), lambda s: (0, s)),
        ],
        out_specs=pl.BlockSpec((rows, DEPTH), lambda s: (0, 0)),
        out_shape=jax.ShapeDtypeStruct((rows, DEPTH), BF16),
        scratch_shapes=[pltpu.VMEM((rows, DEPTH), F32)],
        compiler_params=ROOM,
        cost_estimate=cost(1),
        name="from_boxes",
    )(received, matrix)


def far_kernel(hi_ref, own_ref, other_ref, rad_ref, near_ref, out_ref):
    low_half = hi_ref[0] == 0
    boxes = out_ref.shape[2] // WIDE
    low = low_lanes(2 * R)
    for pair in range(boxes // 2):
        rows = slice(pair * 2 * R, (pair + 1) * 2 * R)
        pieces = [[], []]
        for i in range(CHILDREN):
            cols = slice(i * LANES, (i + 1) * LANES)
            own, other = own_ref[rows, cols].astype(F32), other_ref[rows, cols].astype(F32)
            zero, one = jnp.where(low_half, own, other), jnp.where(low_half, other, own)
            real = jnp.where(low, zero, swap_halves(one))
            imag = jnp.where(low, swap_halves(zero), one)
            for k in range(2):
                part = slice(k * R, (k + 1) * R)
                pieces[k].append(jnp.concatenate([real[part], imag[part]], axis=1))
                pieces[k].append(jnp.concatenate([imag[part], -real[part]], axis=1))
        for k in range(2):
            fields = jnp.concatenate(pieces[k], axis=0).astype(BF16)
            cols = slice((2 * pair + k) * WIDE, (2 * pair + k + 1) * WIDE)
            slab = jnp.concatenate([rad_ref[0, cols, :], rad_ref[1, cols, :]], axis=1)
            terms = times_transposed(fields, slab)
            for part in range(2):
                own = [terms[2 * R * i + part * R : 2 * R * i + (part + 1) * R] for i in range(CHILDREN)]
                out_ref[part, :, cols] = near_ref[part, :, cols] + own_columns(own)


def far_part(hi, own, other, radiation, near_field):
    width = near_field.shape[2]
    rows = own.shape[0]
    steps = 4
    per_step = width // steps
    field = pl.BlockSpec((rows // steps, DEPTH), lambda s, *_: (s, 0))
    wave = pl.BlockSpec((2, R, per_step), lambda s, *_: (0, 0, s))
    return pl.pallas_call(
        far_kernel,
        grid_spec=pltpu.PrefetchScalarGridSpec(
            num_scalar_prefetch=1,
            grid=(steps,),
            in_specs=[field, field, pl.BlockSpec((2, per_step, LANES), lambda s, *_: (0, s, 0)), wave],
            out_specs=wave,
        ),
        out_shape=jax.ShapeDtypeStruct((2, R, width), F32),
        compiler_params=ROOM,
        cost_estimate=cost(1),
        name="far_part",
    )(hi, own, other, radiation, near_field)


def swapped(array):
    return lax.all_to_all(array, INSIDE, split_axis=0, concat_axis=0, tiled=True)


def padded(array):
    return jnp.pad(array, [(0, 0)] * (array.ndim - 1) + [(0, LANES - array.shape[-1])])


def to_owners(boxes, samples):
    rows = boxes.shape[1]
    if samples != LANES:
        boxes = boxes.reshape(CHIPS, rows, LANES // samples, samples).transpose(0, 2, 1, 3).reshape(-1, rows, samples)
    got = swapped(boxes)
    if samples != LANES:
        got = padded(got)
    return got.reshape(-1, 2 * R, LANES)


def from_owners(fields, rows, samples):
    fields = fields.reshape(-1, rows, LANES)
    if samples == LANES:
        return swapped(fields)
    got = swapped(fields[..., :samples]).reshape(CHIPS, LANES // samples, rows, samples)
    return got.transpose(0, 2, 1, 3).reshape(CHIPS, rows, LANES)


def operator_table(translation):
    groups, mids = lax.axis_size("grp"), lax.axis_size("mid")
    core = lax.axis_index("core")
    got = []
    for turned in range(2):
        pairs = [
            (((h * groups + g) * mids + m) * 2 + (c ^ turned), ((g * 2 + h) * mids + m) * 2 + c)
            for g in range(groups)
            for h in range(2)
            for m in range(mids)
            for c in range(2)
        ]
        got.append(lax.ppermute(translation, ALL, pairs).astype(F32))
    low = jnp.where(core == 0, got[0], got[1])
    high = jnp.where(core == 0, got[1], got[0])
    operator = padded(jnp.concatenate([low, high], axis=2))
    return jnp.pad(operator, ((0, 0), (0, -operator.shape[1] % R), (0, 0)))


def target_lists(trans_box, trans_off, hi, core):
    groups, mids = lax.axis_size("grp"), lax.axis_size("mid")
    total = trans_box.shape[0]
    per = total // (groups * mids * 4)
    device, inside = trans_box // per, trans_box % per
    group, side = device // (4 * mids), device // (2 * mids) % 2
    mid, its_core = device // 2 % mids, device % 2
    block = (side ^ hi) * 2 + (its_core ^ core)
    place = (block * (groups * mids) + group * mids + mid) * per + inside
    lists = jnp.concatenate([place, trans_off], axis=1).reshape(groups, 2, mids, 2, per, 2 * IL)
    lists = jnp.where(core == 0, lists[:, :, :, 0], lists[:, :, :, 1])
    first, second = lists[:, 0].reshape(-1), lists[:, 1].reshape(-1)
    return jnp.where(hi == 0, first, second), jnp.where(hi == 0, second, first)


def local(
    currents,
    near_blocks,
    near_list,
    near_count,
    radiation,
    interp,
    shift_angle,
    translation,
    trans_box,
    trans_off,
):
    clusters = near_list.shape[0]
    samples = 2 * translation.shape[2]
    rows = clusters // CHILDREN * 2 * R
    hi, core = lax.axis_index("hi"), lax.axis_index("core")
    side = hi.reshape(1).astype(jnp.int32)
    radiation = radiation.reshape(2, clusters * U, LANES)
    near_blocks = near_blocks.reshape(2, clusters * U, NBR * U)

    first = (lax.axis_index(ALL) - 1) * clusters
    live = jnp.arange(NBR, dtype=jnp.int32)[None, :] < near_count[:, None]
    index = jnp.where(live, near_list - first, 3 * clusters).reshape(-1)
    lists = target_lists(trans_box, trans_off, hi, core)

    leaf_own, leaf_other = leaves(side, currents, radiation)
    leaf_partner = across(leaf_other, "hi")
    boxes_own, matrix = to_boxes(leaf_own, interp, shift_angle)
    rows_own = to_owners(boxes_own, samples)
    swapped_own = across(rows_own, "core")

    leaf_partner, lists, index, late_currents, translation = lax.optimization_barrier(
        (leaf_partner, lists, index, currents, translation)
    )
    rows_partner = to_owners(to_boxes_again(leaf_partner, matrix), samples)
    below = passed_along(late_currents, 1)
    above = passed_along(late_currents, -1)
    operators = operator_table(translation)
    rows_partner, operators, below, above = lax.optimization_barrier((rows_partner, operators, below, above))
    parts = (rows_own, swapped_own, rows_partner, across(rows_partner, "core"))

    fields_partner = translate(lists[1], operators, parts)
    down_partner = from_boxes(from_owners(fields_partner, rows, samples), matrix)
    fields_own = translate(lists[0], operators, parts)
    down_partner, index = lax.optimization_barrier((down_partner, index))
    down_other = across(down_partner, "hi")
    near_field = near_part(index, below, currents, above, near_blocks)
    down_own = from_boxes(from_owners(fields_own, rows, samples), matrix)
    return far_part(side, down_own, down_other, radiation, near_field)


def solution(mesh):
    devices = mesh.devices
    groups, rest = devices.shape
    cut = Mesh(devices.reshape(groups, 2, rest // 4, 2), ALL)
    placed = (
        P(None, None, ALL),
        P(None, ALL, None, None),
        P(ALL, None),
        P(ALL),
        P(None, ALL, None, None),
        P(),
        P(),
        P(None, None, ALL),
        P(),
        P(),
    )
    return jax.shard_map(local, mesh=cut, in_specs=placed, out_specs=P(None, None, ALL), check_vma=False)
```

```python
import functools

import jax
import jax.numpy as jnp
from jax import lax
from jax.experimental import pallas as pl
from jax.experimental.pallas import tpu as pltpu
from jax.sharding import Mesh
from jax.sharding import PartitionSpec as P

R = 8
U = 32
NBR = 8
K0 = 64
K1 = 1024
IL = 12
CHILDREN = 8
WIDE = CHILDREN * U
LANES = 128
HALF = 64
CHIPS = K1 // LANES
DEPTH = 2 * CHILDREN * K0
ALL = ("grp", "hi", "mid", "core")
INSIDE = ("grp", "mid")
F32 = jnp.float32
BF16 = jnp.bfloat16
ROOM = pltpu.CompilerParams(vmem_limit_bytes=58 * 2**20)
LESS = pltpu.CompilerParams(vmem_limit_bytes=28 * 2**20)


def cost(megabytes):
    return pl.CostEstimate(flops=10**6, bytes_accessed=megabytes * 10**6, transcendentals=0)


def passed_along(array, by):
    size = lax.axis_size(ALL)
    pairs = [(i, i + by) for i in range(size) if 0 <= i + by < size]
    return lax.ppermute(array, ALL, pairs)


def across(array, axis):
    return lax.ppermute(array, axis, [(0, 1), (1, 0)])


def swap_halves(array):
    return pltpu.roll(array, HALF, 1)


def low_lanes(rows):
    return lax.broadcasted_iota(jnp.int32, (rows, LANES), 1) < HALF


def times_transposed(left, right):
    return lax.dot_general(left, right, (((1,), (1,)), ((), ())), preferred_element_type=F32)


def own_columns(pieces):
    child = lax.broadcasted_iota(jnp.int32, (R, WIDE), 1) // U
    picked = pieces[0]
    for i in range(1, CHILDREN):
        picked = jnp.where(child == i, pieces[i], picked)
    return picked


def leaf_kernel(hi_ref, cur_ref, rad_ref, own_ref, other_ref):
    low_half = hi_ref[0] == 0
    boxes = cur_ref.shape[2] // WIDE
    low = low_lanes(2 * R)
    row_child = lax.broadcasted_iota(jnp.int32, (2 * R * CHILDREN, WIDE), 0) // (2 * R)
    col_child = lax.broadcasted_iota(jnp.int32, (2 * R * CHILDREN, WIDE), 1) // U
    diagonal = row_child == col_child
    for pair in range(boxes // 2):
        found = []
        for box in (2 * pair, 2 * pair + 1):
            cols = slice(box * WIDE, (box + 1) * WIDE)
            own = [cur_ref[0, :, cols].astype(F32), cur_ref[1, :, cols].astype(F32)]
            spread = jnp.where(diagonal, jnp.concatenate(own * CHILDREN, axis=0), 0.0)
            slab = jnp.concatenate([rad_ref[0, cols, :], rad_ref[1, cols, :]], axis=1)
            found.append(jnp.dot(spread.astype(BF16), slab, preferred_element_type=F32))
        for i in range(CHILDREN):
            by_real = jnp.concatenate([f[2 * R * i : 2 * R * i + R] for f in found], axis=0)
            by_imag = jnp.concatenate([f[2 * R * i + R : 2 * R * (i + 1)] for f in found], axis=0)
            real = by_real[:, :LANES] - by_imag[:, LANES:]
            imag = by_real[:, LANES:] + by_imag[:, :LANES]
            zero = jnp.where(low, real, swap_halves(imag))
            one = jnp.where(low, swap_halves(real), imag)
            rows = slice(pair * 2 * R, (pair + 1) * 2 * R)
            cols = slice(i * LANES, (i + 1) * LANES)
            own_ref[rows, cols] = jnp.where(low_half, zero, one).astype(BF16)
            other_ref[rows, cols] = jnp.where(low_half, one, zero).astype(BF16)


def leaves(hi, currents, radiation):
    width = currents.shape[2]
    rows = width // WIDE * R
    steps = 4
    per_step = width // steps
    shape = jax.ShapeDtypeStruct((rows, DEPTH), BF16)
    spec = pl.BlockSpec((rows // steps, DEPTH), lambda s, *_: (s, 0))
    return pl.pallas_call(
        leaf_kernel,
        grid_spec=pltpu.PrefetchScalarGridSpec(
            num_scalar_prefetch=1,
            grid=(steps,),
            in_specs=[
                pl.BlockSpec((2, R, per_step), lambda s, *_: (0, 0, s)),
                pl.BlockSpec((2, per_step, LANES), lambda s, *_: (0, s, 0)),
            ],
            out_specs=[spec, spec],
        ),
        out_shape=[shape, shape],
        compiler_params=ROOM,
        cost_estimate=cost(1),
        name="leaves",
    )(hi, currents, radiation)


def put_patterns(box_ref, patterns):
    boxes = patterns.shape[0] // R
    for chip in range(box_ref.shape[0]):
        real = patterns[:, 2 * chip * LANES : (2 * chip + 1) * LANES].reshape(boxes, 1, R, LANES)
        imag = patterns[:, (2 * chip + 1) * LANES : (2 * chip + 2) * LANES].reshape(boxes, 1, R, LANES)
        both = jnp.concatenate([real, imag], axis=1).reshape(boxes * 2 * R, LANES)
        box_ref[chip] = both.astype(BF16)


def up_kernel(lhs_ref, interp_ref, angle_ref, box_ref, mat_ref):
    cosine, sine = jnp.cos(angle_ref[...]), jnp.sin(angle_ref[...])
    for chip in range(box_ref.shape[0]):
        cols = slice(chip * LANES, (chip + 1) * LANES)
        to_real = slice(2 * chip * LANES, (2 * chip + 1) * LANES)
        to_imag = slice((2 * chip + 1) * LANES, (2 * chip + 2) * LANES)
        weights = interp_ref[:, cols].astype(F32)
        for i in range(CHILDREN):
            from_real = slice(2 * i * K0, (2 * i + 1) * K0)
            from_imag = slice((2 * i + 1) * K0, (2 * i + 2) * K0)
            even, odd = weights * cosine[i : i + 1, cols], weights * sine[i : i + 1, cols]
            mat_ref[from_real, to_real] = even.astype(BF16)
            mat_ref[from_real, to_imag] = odd.astype(BF16)
            mat_ref[from_imag, to_real] = (-odd).astype(BF16)
            mat_ref[from_imag, to_imag] = even.astype(BF16)
    put_patterns(box_ref, jnp.dot(lhs_ref[...], mat_ref[...], preferred_element_type=F32))


def again_kernel(lhs_ref, mat_ref, box_ref):
    put_patterns(box_ref, jnp.dot(lhs_ref[...], mat_ref[...], preferred_element_type=F32))


def to_boxes(lhs, interp, angle):
    rows = lhs.shape[0]
    steps = 4
    chips = CHIPS // steps
    return pl.pallas_call(
        up_kernel,
        grid=(steps,),
        in_specs=[
            pl.BlockSpec((rows, DEPTH), lambda s: (0, 0)),
            pl.BlockSpec((K0, chips * LANES), lambda s: (0, s)),
            pl.BlockSpec((CHILDREN, chips * LANES), lambda s: (0, s)),
        ],
        out_specs=[
            pl.BlockSpec((chips, 2 * rows, LANES), lambda s: (s, 0, 0)),
            pl.BlockSpec((DEPTH, 2 * chips * LANES), lambda s: (0, s)),
        ],
        out_shape=[
            jax.ShapeDtypeStruct((CHIPS, 2 * rows, LANES), BF16),
            jax.ShapeDtypeStruct((DEPTH, 2 * K1), BF16),
        ],
        compiler_params=ROOM,
        cost_estimate=cost(1),
        name="to_boxes",
    )(lhs, interp, angle)


def to_boxes_again(lhs, matrix):
    rows = lhs.shape[0]
    steps = 4
    chips = CHIPS // steps
    return pl.pallas_call(
        again_kernel,
        grid=(steps,),
        in_specs=[
            pl.BlockSpec((rows, DEPTH), lambda s: (0, 0)),
            pl.BlockSpec((DEPTH, 2 * chips * LANES), lambda s: (0, s)),
        ],
        out_specs=pl.BlockSpec((chips, 2 * rows, LANES), lambda s: (s, 0, 0)),
        out_shape=jax.ShapeDtypeStruct((CHIPS, 2 * rows, LANES), BF16),
        compiler_params=LESS,
        cost_estimate=cost(6),
        name="to_boxes_again",
    )(lhs, matrix)


def translate_kernel(list_ref, oper_ref, one_ref, two_ref, three_ref, four_ref, out_ref, box_ref, table_ref, sems, *, group):
    step = pl.program_id(0)
    per_step = out_ref.shape[0]

    @pl.when(step == 0)
    def fetch():
        copies = []
        for at, source in enumerate((one_ref, two_ref, three_ref, four_ref)):
            boxes = source.shape[0]
            copies.append(pltpu.make_async_copy(source, box_ref.at[pl.ds(at * boxes, boxes)], sems.at[at]))
        for copy in copies:
            copy.start()

        def spread(at, _):
            for part in range(2):
                some = oper_ref[part, pl.ds(pl.multiple_of(at * R, R), R), :]
                for one in range(R):
                    table_ref[at * R + one, part] = jnp.broadcast_to(some[one : one + 1], (R, LANES))
            return 0

        lax.fori_loop(0, oper_ref.shape[1] // R, spread, 0)
        for copy in copies:
            copy.wait()

    def body(at, _):
        first = (step * per_step + at * group) * (2 * IL)
        done = []
        for k in range(group):
            real = imag = None
            for j in range(IL):
                entry = first + k * 2 * IL + j
                tile = box_ref[list_ref[entry]].astype(F32)
                offset = list_ref[entry + IL]
                by_real, by_imag = table_ref[offset, 0], table_ref[offset, 1]
                box_real, box_imag = tile[:R], tile[R:]
                one = by_real * box_real - by_imag * box_imag
                two = by_real * box_imag + by_imag * box_real
                real = one if j == 0 else real + one
                imag = two if j == 0 else imag + two
            done.append(jnp.concatenate([real, imag], axis=0).astype(BF16))
        for k in range(group):
            out_ref[at * group + k] = done[k]
        return 0

    lax.fori_loop(0, per_step // group, body, 0)


def translate(lists, operators, parts):
    targets = lists.shape[0] // (2 * IL)
    boxes = parts[0].shape[0]
    steps = 2
    per_step = targets // steps
    anywhere = pl.BlockSpec(memory_space=pl.ANY)
    return pl.pallas_call(
        functools.partial(translate_kernel, group=8),
        grid_spec=pltpu.PrefetchScalarGridSpec(
            num_scalar_prefetch=1,
            grid=(steps,),
            in_specs=[pl.BlockSpec(operators.shape, lambda s, *_: (0, 0, 0))] + [anywhere] * 4,
            out_specs=pl.BlockSpec((per_step, 2 * R, LANES), lambda s, *_: (s, 0, 0)),
            scratch_shapes=[
                pltpu.VMEM((4 * boxes, 2 * R, LANES), BF16),
                pltpu.VMEM((operators.shape[1], 2, R, LANES), F32),
                pltpu.SemaphoreType.DMA((4,)),
            ],
        ),
        out_shape=jax.ShapeDtypeStruct((targets, 2 * R, LANES), BF16),
        compiler_params=LESS,
        cost_estimate=cost(25),
        name="translate",
    )(lists, operators, *parts)


def near_kernel(idx_ref, below_ref, own_ref, above_ref, blocks_ref, out_ref, table_ref, lhs_ref):
    step = pl.program_id(0)
    width = own_ref.shape[2]
    per_source = width // LANES
    clusters = blocks_ref.shape[1] // U
    per_tile = LANES // U
    place = lax.broadcasted_iota(jnp.int32, (2 * R, LANES), 1) // U

    @pl.when(step == 0)
    def fill():
        unrolled = 4
        for at, source in enumerate((below_ref, own_ref, above_ref)):

            def body(some, _):
                for one in range(unrolled):
                    tile = some * unrolled + one
                    cols = pl.ds(pl.multiple_of(tile * LANES, LANES), LANES)
                    parts = [source[0, :, cols].astype(F32), source[1, :, cols].astype(F32)]
                    whole = jnp.concatenate(parts, axis=0)
                    turned = [whole] + [pltpu.roll(whole, n * U, 1) for n in range(1, per_tile)]
                    for a in range(per_tile):
                        copied = turned[(0 - a) % per_tile]
                        for g in range(1, per_tile):
                            copied = jnp.where(place == g, turned[(g - a) % per_tile], copied)
                        table_ref[(at * per_source + tile) * per_tile + a] = copied
                return 0

            lax.fori_loop(0, per_source // unrolled, body, 0)
        table_ref[3 * per_source * per_tile] = jnp.zeros((2 * R, LANES), F32)

    def body(some, _):
        for one in range(CHILDREN):
            c = some * CHILDREN + one
            entry = (step * clusters + c) * NBR
            for half in range(NBR // per_tile):
                joined = table_ref[idx_ref[entry + half * per_tile]]
                for k in range(1, per_tile):
                    joined = jnp.where(place == k, table_ref[idx_ref[entry + half * per_tile + k]], joined)
                first = pl.multiple_of(c * 2 * R, 2 * R)
                lhs_ref[pl.ds(first, 2 * R), half * LANES : (half + 1) * LANES] = joined.astype(BF16)
        return 0

    lax.fori_loop(0, clusters // CHILDREN, body, 0)
    for box in range(clusters // CHILDREN):
        rows = slice(box * 2 * R * CHILDREN, (box + 1) * 2 * R * CHILDREN)
        cols = slice(box * WIDE, (box + 1) * WIDE)
        by_real = times_transposed(lhs_ref[rows, :], blocks_ref[0, cols, :])
        by_imag = times_transposed(lhs_ref[rows, :], blocks_ref[1, cols, :])
        real = []
        imag = []
        for i in range(CHILDREN):
            top = slice(2 * R * i, 2 * R * i + R)
            bottom = slice(2 * R * i + R, 2 * R * (i + 1))
            real.append(by_real[top] - by_imag[bottom])
            imag.append(by_imag[top] + by_real[bottom])
        out_ref[0, :, cols] = own_columns(real)
        out_ref[1, :, cols] = own_columns(imag)


def near_part(index, below, own, above, blocks):
    width = own.shape[2]
    steps = 8
    per_step = width // steps
    whole = pl.BlockSpec((2, R, width), lambda s, *_: (0, 0, 0))
    return pl.pallas_call(
        near_kernel,
        grid_spec=pltpu.PrefetchScalarGridSpec(
            num_scalar_prefetch=1,
            grid=(steps,),
            in_specs=[whole, whole, whole, pl.BlockSpec((2, per_step, NBR * U), lambda s, *_: (0, s, 0))],
            out_specs=pl.BlockSpec((2, R, per_step), lambda s, *_: (0, 0, s)),
            scratch_shapes=[
                pltpu.VMEM((3 * width // U + 1, 2 * R, LANES), F32),
                pltpu.VMEM((per_step // U * 2 * R, NBR * U), BF16),
            ],
        ),
        out_shape=jax.ShapeDtypeStruct((2, R, width), F32),
        compiler_params=ROOM,
        cost_estimate=cost(1),
        name="near_part",
    )(index, below, own, above, blocks)


def down_kernel(got_ref, mat_ref, out_ref, sum_ref):
    step = pl.program_id(0)
    last = pl.num_programs(0) - 1
    pieces = []
    for chip in range(got_ref.shape[0]):
        both = got_ref[chip].astype(F32).reshape(-1, 2, R, LANES)
        pieces += [both[:, 0].reshape(-1, LANES), both[:, 1].reshape(-1, LANES)]
    added = times_transposed(jnp.concatenate(pieces, axis=1).astype(BF16), mat_ref[...])

    @pl.when(step == 0)
    def begin():
        sum_ref[...] = added

    @pl.when(jnp.logical_and(step > 0, step < last))
    def go_on():
        sum_ref[...] += added

    @pl.when(step == last)
    def end():
        out_ref[...] = (sum_ref[...] + added).astype(BF16)


def from_boxes(received, matrix):
    rows = received.shape[1] // 2
    steps = 4
    chips = CHIPS // steps
    return pl.pallas_call(
        down_kernel,
        grid=(steps,),
        in_specs=[
            pl.BlockSpec((chips, 2 * rows, LANES), lambda s: (s, 0, 0)),
            pl.BlockSpec((DEPTH, 2 * chips * LANES), lambda s: (0, s)),
        ],
        out_specs=pl.BlockSpec((rows, DEPTH), lambda s: (0, 0)),
        out_shape=jax.ShapeDtypeStruct((rows, DEPTH), BF16),
        scratch_shapes=[pltpu.VMEM((rows, DEPTH), F32)],
        compiler_params=LESS,
        cost_estimate=cost(1),
        name="from_boxes",
    )(received, matrix)


def far_kernel(hi_ref, own_ref, other_ref, rad_ref, near_ref, out_ref):
    low_half = hi_ref[0] == 0
    boxes = out_ref.shape[2] // WIDE
    low = low_lanes(2 * R)
    for pair in range(boxes // 2):
        rows = slice(pair * 2 * R, (pair + 1) * 2 * R)
        pieces = [[], []]
        for i in range(CHILDREN):
            cols = slice(i * LANES, (i + 1) * LANES)
            own, other = own_ref[rows, cols].astype(F32), other_ref[rows, cols].astype(F32)
            zero, one = jnp.where(low_half, own, other), jnp.where(low_half, other, own)
            real = jnp.where(low, zero, swap_halves(one))
            imag = jnp.where(low, swap_halves(zero), one)
            for k in range(2):
                part = slice(k * R, (k + 1) * R)
                pieces[k].append(jnp.concatenate([real[part], imag[part]], axis=1))
                pieces[k].append(jnp.concatenate([imag[part], -real[part]], axis=1))
        for k in range(2):
            fields = jnp.concatenate(pieces[k], axis=0).astype(BF16)
            cols = slice((2 * pair + k) * WIDE, (2 * pair + k + 1) * WIDE)
            slab = jnp.concatenate([rad_ref[0, cols, :], rad_ref[1, cols, :]], axis=1)
            terms = times_transposed(fields, slab)
            for part in range(2):
                own = [terms[2 * R * i + part * R : 2 * R * i + (part + 1) * R] for i in range(CHILDREN)]
                out_ref[part, :, cols] = near_ref[part, :, cols] + own_columns(own)


def far_part(hi, own, other, radiation, near_field):
    width = near_field.shape[2]
    rows = own.shape[0]
    steps = 4
    per_step = width // steps
    field = pl.BlockSpec((rows // steps, DEPTH), lambda s, *_: (s, 0))
    wave = pl.BlockSpec((2, R, per_step), lambda s, *_: (0, 0, s))
    return pl.pallas_call(
        far_kernel,
        grid_spec=pltpu.PrefetchScalarGridSpec(
            num_scalar_prefetch=1,
            grid=(steps,),
            in_specs=[field, field, pl.BlockSpec((2, per_step, LANES), lambda s, *_: (0, s, 0)), wave],
            out_specs=wave,
        ),
        out_shape=jax.ShapeDtypeStruct((2, R, width), F32),
        compiler_params=LESS,
        cost_estimate=cost(1),
        name="far_part",
    )(hi, own, other, radiation, near_field)


def swapped(array):
    return lax.all_to_all(array, INSIDE, split_axis=0, concat_axis=0, tiled=True)


def padded(array):
    return jnp.pad(array, [(0, 0)] * (array.ndim - 1) + [(0, LANES - array.shape[-1])])


def to_owners(boxes, samples):
    rows = boxes.shape[1]
    if samples != LANES:
        boxes = boxes.reshape(CHIPS, rows, LANES // samples, samples).transpose(0, 2, 1, 3).reshape(-1, rows, samples)
    got = swapped(boxes)
    if samples != LANES:
        got = padded(got)
    return got.reshape(-1, 2 * R, LANES)


def from_owners(fields, rows, samples):
    fields = fields.reshape(-1, rows, LANES)
    if samples == LANES:
        return swapped(fields)
    got = swapped(fields[..., :samples]).reshape(CHIPS, LANES // samples, rows, samples)
    return got.transpose(0, 2, 1, 3).reshape(CHIPS, rows, LANES)


def operator_table(translation):
    groups, mids = lax.axis_size("grp"), lax.axis_size("mid")
    core = lax.axis_index("core")
    got = []
    for turned in range(2):
        pairs = [
            (((h * groups + g) * mids + m) * 2 + (c ^ turned), ((g * 2 + h) * mids + m) * 2 + c)
            for g in range(groups)
            for h in range(2)
            for m in range(mids)
            for c in range(2)
        ]
        got.append(lax.ppermute(translation, ALL, pairs).astype(F32))
    low = jnp.where(core == 0, got[0], got[1])
    high = jnp.where(core == 0, got[1], got[0])
    operator = padded(jnp.concatenate([low, high], axis=2))
    return jnp.pad(operator, ((0, 0), (0, -operator.shape[1] % R), (0, 0)))


def target_lists(trans_box, trans_off, hi, core):
    groups, mids = lax.axis_size("grp"), lax.axis_size("mid")
    total = trans_box.shape[0]
    per = total // (groups * mids * 4)
    device, inside = trans_box // per, trans_box % per
    group, side = device // (4 * mids), device // (2 * mids) % 2
    mid, its_core = device // 2 % mids, device % 2
    block = (side ^ hi) * 2 + (its_core ^ core)
    place = (block * (groups * mids) + group * mids + mid) * per + inside
    lists = jnp.concatenate([place, trans_off], axis=1).reshape(groups, 2, mids, 2, per, 2 * IL)
    lists = jnp.where(core == 0, lists[:, :, :, 0], lists[:, :, :, 1])
    first, second = lists[:, 0].reshape(-1), lists[:, 1].reshape(-1)
    return jnp.where(hi == 0, first, second), jnp.where(hi == 0, second, first)


def local(
    currents,
    near_blocks,
    near_list,
    near_count,
    radiation,
    interp,
    shift_angle,
    translation,
    trans_box,
    trans_off,
):
    clusters = near_list.shape[0]
    samples = 2 * translation.shape[2]
    rows = clusters // CHILDREN * 2 * R
    hi, core = lax.axis_index("hi"), lax.axis_index("core")
    side = hi.reshape(1).astype(jnp.int32)
    radiation = radiation.reshape(2, clusters * U, LANES)
    near_blocks = near_blocks.reshape(2, clusters * U, NBR * U)

    first = (lax.axis_index(ALL) - 1) * clusters
    live = jnp.arange(NBR, dtype=jnp.int32)[None, :] < near_count[:, None]
    index = jnp.where(live, near_list - first, 3 * clusters).reshape(-1)
    lists = target_lists(trans_box, trans_off, hi, core)

    below = passed_along(currents, 1)
    above = passed_along(currents, -1)
    operators = operator_table(translation)
    leaf_own, leaf_other = leaves(side, currents, radiation)
    leaf_partner = across(leaf_other, "hi")
    leaf_own, below, above, operators = lax.optimization_barrier((leaf_own, below, above, operators))
    boxes_own, matrix = to_boxes(leaf_own, interp, shift_angle)
    rows_own = to_owners(boxes_own, samples)
    swapped_own = across(rows_own, "core")
    leaf_partner, lists, index = lax.optimization_barrier((leaf_partner, lists, index))
    rows_partner = to_owners(to_boxes_again(leaf_partner, matrix), samples)
    parts = (rows_own, swapped_own, rows_partner, across(rows_partner, "core"))

    fields_partner = translate(lists[1], operators, parts)
    down_partner = from_boxes(from_owners(fields_partner, rows, samples), matrix)
    fields_own = translate(lists[0], operators, parts)
    down_partner, index = lax.optimization_barrier((down_partner, index))
    down_other = across(down_partner, "hi")
    near_field = near_part(index, below, currents, above, near_blocks)
    down_own = from_boxes(from_owners(fields_own, rows, samples), matrix)
    return far_part(side, down_own, down_other, radiation, near_field)


def solution(mesh):
    devices = mesh.devices
    groups, rest = devices.shape
    cut = Mesh(devices.reshape(groups, 2, rest // 4, 2), ALL)
    placed = (
        P(None, None, ALL),
        P(None, ALL, None, None),
        P(ALL, None),
        P(ALL),
        P(None, ALL, None, None),
        P(),
        P(),
        P(None, None, ALL),
        P(),
        P(),
    )
    return jax.shard_map(local, mesh=cut, in_specs=placed, out_specs=P(None, None, ALL), check_vma=False)
```

```python
import functools

import jax
import jax.numpy as jnp
from jax import lax
from jax.experimental import pallas as pl
from jax.experimental.pallas import tpu as pltpu
from jax.sharding import Mesh
from jax.sharding import PartitionSpec as P

R = 8
U = 32
NBR = 8
K0 = 64
K1 = 1024
IL = 12
CHILDREN = 8
WIDE = CHILDREN * U
LANES = 128
HALF = 64
CHIPS = K1 // LANES
DEPTH = 2 * CHILDREN * K0
ALL = ("grp", "hi", "mid", "core")
INSIDE = ("grp", "mid")
F32 = jnp.float32
BF16 = jnp.bfloat16
ROOM = pltpu.CompilerParams(vmem_limit_bytes=58 * 2**20)
LESS = pltpu.CompilerParams(vmem_limit_bytes=28 * 2**20)


def cost(megabytes):
    return pl.CostEstimate(flops=10**6, bytes_accessed=megabytes * 10**6, transcendentals=0)


def neighbours(array):
    size = lax.axis_size(ALL)
    pairs = [(i, i + 1) for i in range(1, size - 1, 2)] + [(i + 1, i) for i in range(1, size - 1, 2)]
    outside = lax.ppermute(array, ALL, pairs)
    inside = across(array, "core")
    first = lax.axis_index("core") == 0
    return jnp.where(first, outside, inside), jnp.where(first, inside, outside)


def across(array, axis):
    return lax.ppermute(array, axis, [(0, 1), (1, 0)])


def swap_halves(array):
    return pltpu.roll(array, HALF, 1)


def low_lanes(rows):
    return lax.broadcasted_iota(jnp.int32, (rows, LANES), 1) < HALF


def times_transposed(left, right):
    return lax.dot_general(left, right, (((1,), (1,)), ((), ())), preferred_element_type=F32)


def own_columns(pieces):
    child = lax.broadcasted_iota(jnp.int32, (R, WIDE), 1) // U
    picked = pieces[0]
    for i in range(1, CHILDREN):
        picked = jnp.where(child == i, pieces[i], picked)
    return picked


def leaf_kernel(hi_ref, cur_ref, rad_ref, own_ref, other_ref):
    low_half = hi_ref[0] == 0
    boxes = cur_ref.shape[2] // WIDE
    low = low_lanes(2 * R)
    row_child = lax.broadcasted_iota(jnp.int32, (2 * R * CHILDREN, WIDE), 0) // (2 * R)
    col_child = lax.broadcasted_iota(jnp.int32, (2 * R * CHILDREN, WIDE), 1) // U
    diagonal = row_child == col_child
    for pair in range(boxes // 2):
        found = []
        for box in (2 * pair, 2 * pair + 1):
            cols = slice(box * WIDE, (box + 1) * WIDE)
            own = [cur_ref[0, :, cols].astype(F32), cur_ref[1, :, cols].astype(F32)]
            spread = jnp.where(diagonal, jnp.concatenate(own * CHILDREN, axis=0), 0.0)
            slab = jnp.concatenate([rad_ref[0, cols, :], rad_ref[1, cols, :]], axis=1)
            found.append(jnp.dot(spread.astype(BF16), slab, preferred_element_type=F32))
        for i in range(CHILDREN):
            by_real = jnp.concatenate([f[2 * R * i : 2 * R * i + R] for f in found], axis=0)
            by_imag = jnp.concatenate([f[2 * R * i + R : 2 * R * (i + 1)] for f in found], axis=0)
            real = by_real[:, :LANES] - by_imag[:, LANES:]
            imag = by_real[:, LANES:] + by_imag[:, :LANES]
            zero = jnp.where(low, real, swap_halves(imag))
            one = jnp.where(low, swap_halves(real), imag)
            rows = slice(pair * 2 * R, (pair + 1) * 2 * R)
            cols = slice(i * LANES, (i + 1) * LANES)
            own_ref[rows, cols] = jnp.where(low_half, zero, one).astype(BF16)
            other_ref[rows, cols] = jnp.where(low_half, one, zero).astype(BF16)


def leaves(hi, currents, radiation):
    width = currents.shape[2]
    rows = width // WIDE * R
    steps = 4
    per_step = width // steps
    shape = jax.ShapeDtypeStruct((rows, DEPTH), BF16)
    spec = pl.BlockSpec((rows // steps, DEPTH), lambda s, *_: (s, 0))
    return pl.pallas_call(
        leaf_kernel,
        grid_spec=pltpu.PrefetchScalarGridSpec(
            num_scalar_prefetch=1,
            grid=(steps,),
            in_specs=[
                pl.BlockSpec((2, R, per_step), lambda s, *_: (0, 0, s)),
                pl.BlockSpec((2, per_step, LANES), lambda s, *_: (0, s, 0)),
            ],
            out_specs=[spec, spec],
        ),
        out_shape=[shape, shape],
        compiler_params=ROOM,
        cost_estimate=cost(1),
        name="leaves",
    )(hi, currents, radiation)


def put_patterns(box_ref, patterns):
    boxes = patterns.shape[0] // R
    for chip in range(box_ref.shape[0]):
        real = patterns[:, 2 * chip * LANES : (2 * chip + 1) * LANES].reshape(boxes, 1, R, LANES)
        imag = patterns[:, (2 * chip + 1) * LANES : (2 * chip + 2) * LANES].reshape(boxes, 1, R, LANES)
        both = jnp.concatenate([real, imag], axis=1).reshape(boxes * 2 * R, LANES)
        box_ref[chip] = both.astype(BF16)


def up_kernel(lhs_ref, interp_ref, angle_ref, box_ref, mat_ref):
    cosine, sine = jnp.cos(angle_ref[...]), jnp.sin(angle_ref[...])
    for chip in range(box_ref.shape[0]):
        cols = slice(chip * LANES, (chip + 1) * LANES)
        to_real = slice(2 * chip * LANES, (2 * chip + 1) * LANES)
        to_imag = slice((2 * chip + 1) * LANES, (2 * chip + 2) * LANES)
        weights = interp_ref[:, cols].astype(F32)
        for i in range(CHILDREN):
            from_real = slice(2 * i * K0, (2 * i + 1) * K0)
            from_imag = slice((2 * i + 1) * K0, (2 * i + 2) * K0)
            even, odd = weights * cosine[i : i + 1, cols], weights * sine[i : i + 1, cols]
            mat_ref[from_real, to_real] = even.astype(BF16)
            mat_ref[from_real, to_imag] = odd.astype(BF16)
            mat_ref[from_imag, to_real] = (-odd).astype(BF16)
            mat_ref[from_imag, to_imag] = even.astype(BF16)
    put_patterns(box_ref, jnp.dot(lhs_ref[...], mat_ref[...], preferred_element_type=F32))


def again_kernel(lhs_ref, mat_ref, box_ref):
    put_patterns(box_ref, jnp.dot(lhs_ref[...], mat_ref[...], preferred_element_type=F32))


def to_boxes(lhs, interp, angle):
    rows = lhs.shape[0]
    steps = 4
    chips = CHIPS // steps
    return pl.pallas_call(
        up_kernel,
        grid=(steps,),
        in_specs=[
            pl.BlockSpec((rows, DEPTH), lambda s: (0, 0)),
            pl.BlockSpec((K0, chips * LANES), lambda s: (0, s)),
            pl.BlockSpec((CHILDREN, chips * LANES), lambda s: (0, s)),
        ],
        out_specs=[
            pl.BlockSpec((chips, 2 * rows, LANES), lambda s: (s, 0, 0)),
            pl.BlockSpec((DEPTH, 2 * chips * LANES), lambda s: (0, s)),
        ],
        out_shape=[
            jax.ShapeDtypeStruct((CHIPS, 2 * rows, LANES), BF16),
            jax.ShapeDtypeStruct((DEPTH, 2 * K1), BF16),
        ],
        compiler_params=ROOM,
        cost_estimate=cost(1),
        name="to_boxes",
    )(lhs, interp, angle)


def to_boxes_again(lhs, matrix):
    rows = lhs.shape[0]
    steps = 4
    chips = CHIPS // steps
    return pl.pallas_call(
        again_kernel,
        grid=(steps,),
        in_specs=[
            pl.BlockSpec((rows, DEPTH), lambda s: (0, 0)),
            pl.BlockSpec((DEPTH, 2 * chips * LANES), lambda s: (0, s)),
        ],
        out_specs=pl.BlockSpec((chips, 2 * rows, LANES), lambda s: (s, 0, 0)),
        out_shape=jax.ShapeDtypeStruct((CHIPS, 2 * rows, LANES), BF16),
        compiler_params=LESS,
        cost_estimate=cost(6),
        name="to_boxes_again",
    )(lhs, matrix)


def translate_kernel(list_ref, oper_ref, one_ref, two_ref, three_ref, four_ref, out_ref, box_ref, table_ref, sems, *, group):
    step = pl.program_id(0)
    per_step = out_ref.shape[0]

    @pl.when(step == 0)
    def fetch():
        copies = []
        for at, source in enumerate((one_ref, two_ref, three_ref, four_ref)):
            boxes = source.shape[0]
            copies.append(pltpu.make_async_copy(source, box_ref.at[pl.ds(at * boxes, boxes)], sems.at[at]))
        for copy in copies:
            copy.start()

        def spread(at, _):
            for part in range(2):
                some = oper_ref[part, pl.ds(pl.multiple_of(at * R, R), R), :]
                for one in range(R):
                    table_ref[at * R + one, part] = jnp.broadcast_to(some[one : one + 1], (R, LANES))
            return 0

        lax.fori_loop(0, oper_ref.shape[1] // R, spread, 0)
        for copy in copies:
            copy.wait()

    def body(at, _):
        first = (step * per_step + at * group) * (2 * IL)
        done = []
        for k in range(group):
            real = imag = None
            for j in range(IL):
                entry = first + k * 2 * IL + j
                tile = box_ref[list_ref[entry]].astype(F32)
                offset = list_ref[entry + IL]
                by_real, by_imag = table_ref[offset, 0], table_ref[offset, 1]
                box_real, box_imag = tile[:R], tile[R:]
                one = by_real * box_real - by_imag * box_imag
                two = by_real * box_imag + by_imag * box_real
                real = one if j == 0 else real + one
                imag = two if j == 0 else imag + two
            done.append(jnp.concatenate([real, imag], axis=0).astype(BF16))
        for k in range(group):
            out_ref[at * group + k] = done[k]
        return 0

    lax.fori_loop(0, per_step // group, body, 0)


def translate(lists, operators, parts):
    targets = lists.shape[0] // (2 * IL)
    boxes = parts[0].shape[0]
    steps = 2
    per_step = targets // steps
    anywhere = pl.BlockSpec(memory_space=pl.ANY)
    return pl.pallas_call(
        functools.partial(translate_kernel, group=8),
        grid_spec=pltpu.PrefetchScalarGridSpec(
            num_scalar_prefetch=1,
            grid=(steps,),
            in_specs=[pl.BlockSpec(operators.shape, lambda s, *_: (0, 0, 0))] + [anywhere] * 4,
            out_specs=pl.BlockSpec((per_step, 2 * R, LANES), lambda s, *_: (s, 0, 0)),
            scratch_shapes=[
                pltpu.VMEM((4 * boxes, 2 * R, LANES), BF16),
                pltpu.VMEM((operators.shape[1], 2, R, LANES), F32),
                pltpu.SemaphoreType.DMA((4,)),
            ],
        ),
        out_shape=jax.ShapeDtypeStruct((targets, 2 * R, LANES), BF16),
        compiler_params=LESS,
        cost_estimate=cost(25),
        name="translate",
    )(lists, operators, *parts)


def near_kernel(idx_ref, below_ref, own_ref, above_ref, blocks_ref, out_ref, table_ref, lhs_ref):
    step = pl.program_id(0)
    width = own_ref.shape[2]
    per_source = width // LANES
    clusters = blocks_ref.shape[1] // U
    per_tile = LANES // U
    place = lax.broadcasted_iota(jnp.int32, (2 * R, LANES), 1) // U

    @pl.when(step == 0)
    def fill():
        unrolled = 4
        for at, source in enumerate((below_ref, own_ref, above_ref)):

            def body(some, _):
                for one in range(unrolled):
                    tile = some * unrolled + one
                    cols = pl.ds(pl.multiple_of(tile * LANES, LANES), LANES)
                    parts = [source[0, :, cols].astype(F32), source[1, :, cols].astype(F32)]
                    whole = jnp.concatenate(parts, axis=0)
                    turned = [whole] + [pltpu.roll(whole, n * U, 1) for n in range(1, per_tile)]
                    for a in range(per_tile):
                        copied = turned[(0 - a) % per_tile]
                        for g in range(1, per_tile):
                            copied = jnp.where(place == g, turned[(g - a) % per_tile], copied)
                        table_ref[(at * per_source + tile) * per_tile + a] = copied
                return 0

            lax.fori_loop(0, per_source // unrolled, body, 0)
        table_ref[3 * per_source * per_tile] = jnp.zeros((2 * R, LANES), F32)

    def body(some, _):
        for one in range(CHILDREN):
            c = some * CHILDREN + one
            entry = (step * clusters + c) * NBR
            for half in range(NBR // per_tile):
                joined = table_ref[idx_ref[entry + half * per_tile]]
                for k in range(1, per_tile):
                    joined = jnp.where(place == k, table_ref[idx_ref[entry + half * per_tile + k]], joined)
                first = pl.multiple_of(c * 2 * R, 2 * R)
                lhs_ref[pl.ds(first, 2 * R), half * LANES : (half + 1) * LANES] = joined.astype(BF16)
        return 0

    lax.fori_loop(0, clusters // CHILDREN, body, 0)
    for box in range(clusters // CHILDREN):
        rows = slice(box * 2 * R * CHILDREN, (box + 1) * 2 * R * CHILDREN)
        cols = slice(box * WIDE, (box + 1) * WIDE)
        by_real = times_transposed(lhs_ref[rows, :], blocks_ref[0, cols, :])
        by_imag = times_transposed(lhs_ref[rows, :], blocks_ref[1, cols, :])
        real = []
        imag = []
        for i in range(CHILDREN):
            top = slice(2 * R * i, 2 * R * i + R)
            bottom = slice(2 * R * i + R, 2 * R * (i + 1))
            real.append(by_real[top] - by_imag[bottom])
            imag.append(by_imag[top] + by_real[bottom])
        out_ref[0, :, cols] = own_columns(real)
        out_ref[1, :, cols] = own_columns(imag)


def near_part(index, below, own, above, blocks):
    width = own.shape[2]
    steps = 8
    per_step = width // steps
    whole = pl.BlockSpec((2, R, width), lambda s, *_: (0, 0, 0))
    return pl.pallas_call(
        near_kernel,
        grid_spec=pltpu.PrefetchScalarGridSpec(
            num_scalar_prefetch=1,
            grid=(steps,),
            in_specs=[whole, whole, whole, pl.BlockSpec((2, per_step, NBR * U), lambda s, *_: (0, s, 0))],
            out_specs=pl.BlockSpec((2, R, per_step), lambda s, *_: (0, 0, s)),
            scratch_shapes=[
                pltpu.VMEM((3 * width // U + 1, 2 * R, LANES), F32),
                pltpu.VMEM((per_step // U * 2 * R, NBR * U), BF16),
            ],
        ),
        out_shape=jax.ShapeDtypeStruct((2, R, width), F32),
        compiler_params=ROOM,
        cost_estimate=cost(1),
        name="near_part",
    )(index, below, own, above, blocks)


def down_kernel(got_ref, mat_ref, out_ref, sum_ref):
    step = pl.program_id(0)
    last = pl.num_programs(0) - 1
    pieces = []
    for chip in range(got_ref.shape[0]):
        both = got_ref[chip].astype(F32).reshape(-1, 2, R, LANES)
        pieces += [both[:, 0].reshape(-1, LANES), both[:, 1].reshape(-1, LANES)]
    added = times_transposed(jnp.concatenate(pieces, axis=1).astype(BF16), mat_ref[...])

    @pl.when(step == 0)
    def begin():
        sum_ref[...] = added

    @pl.when(jnp.logical_and(step > 0, step < last))
    def go_on():
        sum_ref[...] += added

    @pl.when(step == last)
    def end():
        out_ref[...] = (sum_ref[...] + added).astype(BF16)


def from_boxes(received, matrix):
    rows = received.shape[1] // 2
    steps = 4
    chips = CHIPS // steps
    return pl.pallas_call(
        down_kernel,
        grid=(steps,),
        in_specs=[
            pl.BlockSpec((chips, 2 * rows, LANES), lambda s: (s, 0, 0)),
            pl.BlockSpec((DEPTH, 2 * chips * LANES), lambda s: (0, s)),
        ],
        out_specs=pl.BlockSpec((rows, DEPTH), lambda s: (0, 0)),
        out_shape=jax.ShapeDtypeStruct((rows, DEPTH), BF16),
        scratch_shapes=[pltpu.VMEM((rows, DEPTH), F32)],
        compiler_params=LESS,
        cost_estimate=cost(1),
        name="from_boxes",
    )(received, matrix)


def far_kernel(hi_ref, own_ref, other_ref, rad_ref, near_ref, out_ref):
    low_half = hi_ref[0] == 0
    boxes = out_ref.shape[2] // WIDE
    low = low_lanes(2 * R)
    for pair in range(boxes // 2):
        rows = slice(pair * 2 * R, (pair + 1) * 2 * R)
        pieces = [[], []]
        for i in range(CHILDREN):
            cols = slice(i * LANES, (i + 1) * LANES)
            own, other = own_ref[rows, cols].astype(F32), other_ref[rows, cols].astype(F32)
            zero, one = jnp.where(low_half, own, other), jnp.where(low_half, other, own)
            real = jnp.where(low, zero, swap_halves(one))
            imag = jnp.where(low, swap_halves(zero), one)
            for k in range(2):
                part = slice(k * R, (k + 1) * R)
                pieces[k].append(jnp.concatenate([real[part], imag[part]], axis=1))
                pieces[k].append(jnp.concatenate([imag[part], -real[part]], axis=1))
        for k in range(2):
            fields = jnp.concatenate(pieces[k], axis=0).astype(BF16)
            cols = slice((2 * pair + k) * WIDE, (2 * pair + k + 1) * WIDE)
            slab = jnp.concatenate([rad_ref[0, cols, :], rad_ref[1, cols, :]], axis=1)
            terms = times_transposed(fields, slab)
            for part in range(2):
                own = [terms[2 * R * i + part * R : 2 * R * i + (part + 1) * R] for i in range(CHILDREN)]
                out_ref[part, :, cols] = near_ref[part, :, cols] + own_columns(own)


def far_part(hi, own, other, radiation, near_field):
    width = near_field.shape[2]
    rows = own.shape[0]
    steps = 4
    per_step = width // steps
    field = pl.BlockSpec((rows // steps, DEPTH), lambda s, *_: (s, 0))
    wave = pl.BlockSpec((2, R, per_step), lambda s, *_: (0, 0, s))
    return pl.pallas_call(
        far_kernel,
        grid_spec=pltpu.PrefetchScalarGridSpec(
            num_scalar_prefetch=1,
            grid=(steps,),
            in_specs=[field, field, pl.BlockSpec((2, per_step, LANES), lambda s, *_: (0, s, 0)), wave],
            out_specs=wave,
        ),
        out_shape=jax.ShapeDtypeStruct((2, R, width), F32),
        compiler_params=LESS,
        cost_estimate=cost(1),
        name="far_part",
    )(hi, own, other, radiation, near_field)


def swapped(array):
    return lax.all_to_all(array, INSIDE, split_axis=0, concat_axis=0, tiled=True)


def padded(array):
    return jnp.pad(array, [(0, 0)] * (array.ndim - 1) + [(0, LANES - array.shape[-1])])


def to_owners(boxes, samples):
    rows = boxes.shape[1]
    if samples != LANES:
        boxes = boxes.reshape(CHIPS, rows, LANES // samples, samples).transpose(0, 2, 1, 3).reshape(-1, rows, samples)
    got = swapped(boxes)
    if samples != LANES:
        got = padded(got)
    return got.reshape(-1, 2 * R, LANES)


def from_owners(fields, rows, samples):
    fields = fields.reshape(-1, rows, LANES)
    if samples == LANES:
        return swapped(fields)
    got = swapped(fields[..., :samples]).reshape(CHIPS, LANES // samples, rows, samples)
    return got.transpose(0, 2, 1, 3).reshape(CHIPS, rows, LANES)


def operator_table(translation):
    groups, mids = lax.axis_size("grp"), lax.axis_size("mid")
    core = lax.axis_index("core")
    pairs = [
        (((h * groups + g) * mids + m) * 2 + c, ((g * 2 + h) * mids + m) * 2 + c)
        for g in range(groups)
        for h in range(2)
        for m in range(mids)
        for c in range(2)
    ]
    mine = lax.ppermute(translation, ALL, pairs)
    other = across(mine, "core").astype(F32)
    mine = mine.astype(F32)
    low = jnp.where(core == 0, mine, other)
    high = jnp.where(core == 0, other, mine)
    operator = padded(jnp.concatenate([low, high], axis=2))
    return jnp.pad(operator, ((0, 0), (0, -operator.shape[1] % R), (0, 0)))


def target_lists(trans_box, trans_off, hi, core):
    groups, mids = lax.axis_size("grp"), lax.axis_size("mid")
    total = trans_box.shape[0]
    per = total // (groups * mids * 4)
    device, inside = trans_box // per, trans_box % per
    group, side = device // (4 * mids), device // (2 * mids) % 2
    mid, its_core = device // 2 % mids, device % 2
    block = (side ^ hi) * 2 + (its_core ^ core)
    place = (block * (groups * mids) + group * mids + mid) * per + inside
    lists = jnp.concatenate([place, trans_off], axis=1).reshape(groups, 2, mids, 2, per, 2 * IL)
    lists = jnp.where(core == 0, lists[:, :, :, 0], lists[:, :, :, 1])
    first, second = lists[:, 0].reshape(-1), lists[:, 1].reshape(-1)
    return jnp.where(hi == 0, first, second), jnp.where(hi == 0, second, first)


def local(
    currents,
    near_blocks,
    near_list,
    near_count,
    radiation,
    interp,
    shift_angle,
    translation,
    trans_box,
    trans_off,
):
    clusters = near_list.shape[0]
    samples = 2 * translation.shape[2]
    rows = clusters // CHILDREN * 2 * R
    hi, core = lax.axis_index("hi"), lax.axis_index("core")
    side = hi.reshape(1).astype(jnp.int32)
    radiation = radiation.reshape(2, clusters * U, LANES)
    near_blocks = near_blocks.reshape(2, clusters * U, NBR * U)

    first = (lax.axis_index(ALL) - 1) * clusters
    live = jnp.arange(NBR, dtype=jnp.int32)[None, :] < near_count[:, None]
    index = jnp.where(live, near_list - first, 3 * clusters).reshape(-1)
    lists = target_lists(trans_box, trans_off, hi, core)

    leaf_own, leaf_other = leaves(side, currents, radiation)
    leaf_partner = across(leaf_other, "hi")
    boxes_own, matrix = to_boxes(leaf_own, interp, shift_angle)
    rows_own = to_owners(boxes_own, samples)
    swapped_own = across(rows_own, "core")
    operators = operator_table(translation)
    below, above = neighbours(currents)
    leaf_partner, lists, index, operators, below, above = lax.optimization_barrier(
        (leaf_partner, lists, index, operators, below, above)
    )
    rows_partner = to_owners(to_boxes_again(leaf_partner, matrix), samples)
    parts = (rows_own, swapped_own, rows_partner, across(rows_partner, "core"))

    fields_partner = translate(lists[1], operators, parts)
    down_partner = from_boxes(from_owners(fields_partner, rows, samples), matrix)
    fields_own = translate(lists[0], operators, parts)
    down_partner, index = lax.optimization_barrier((down_partner, index))
    down_other = across(down_partner, "hi")
    near_field = near_part(index, below, currents, above, near_blocks)
    down_own = from_boxes(from_owners(fields_own, rows, samples), matrix)
    return far_part(side, down_own, down_other, radiation, near_field)


def solution(mesh):
    devices = mesh.devices
    groups, rest = devices.shape
    cut = Mesh(devices.reshape(groups, 2, rest // 4, 2), ALL)
    placed = (
        P(None, None, ALL),
        P(None, ALL, None, None),
        P(ALL, None),
        P(ALL),
        P(None, ALL, None, None),
        P(),
        P(),
        P(None, None, ALL),
        P(),
        P(),
    )
    return jax.shard_map(local, mesh=cut, in_specs=placed, out_specs=P(None, None, ALL), check_vma=False)
```

```python
import functools

import jax
import jax.numpy as jnp
from jax import lax
from jax.experimental import pallas as pl
from jax.experimental.pallas import tpu as pltpu
from jax.sharding import Mesh
from jax.sharding import PartitionSpec as P

R = 8
U = 32
NBR = 8
K0 = 64
K1 = 1024
IL = 12
CHILDREN = 8
WIDE = CHILDREN * U
LANES = 128
HALF = 64
CHIPS = K1 // LANES
DEPTH = 2 * CHILDREN * K0
ALL = ("grp", "hi", "mid", "core")
INSIDE = ("grp", "mid")
F32 = jnp.float32
BF16 = jnp.bfloat16
ROOM = pltpu.CompilerParams(vmem_limit_bytes=58 * 2**20)
LESS = pltpu.CompilerParams(vmem_limit_bytes=28 * 2**20)


def cost(megabytes):
    return pl.CostEstimate(flops=10**6, bytes_accessed=megabytes * 10**6, transcendentals=0)


def next_chip(array):
    size = lax.axis_size(ALL)
    pairs = [(i, i + 1) for i in range(1, size - 1, 2)] + [(i + 1, i) for i in range(1, size - 1, 2)]
    return lax.ppermute(array, ALL, pairs)


def across(array, axis):
    return lax.ppermute(array, axis, [(0, 1), (1, 0)])


def swap_halves(array):
    return pltpu.roll(array, HALF, 1)


def low_lanes(rows):
    return lax.broadcasted_iota(jnp.int32, (rows, LANES), 1) < HALF


def times_transposed(left, right):
    return lax.dot_general(left, right, (((1,), (1,)), ((), ())), preferred_element_type=F32)


def own_columns(pieces):
    child = lax.broadcasted_iota(jnp.int32, (R, WIDE), 1) // U
    picked = pieces[0]
    for i in range(1, CHILDREN):
        picked = jnp.where(child == i, pieces[i], picked)
    return picked


def leaf_kernel(hi_ref, cur_ref, rad_ref, own_ref, other_ref):
    low_half = hi_ref[0] == 0
    boxes = cur_ref.shape[2] // WIDE
    low = low_lanes(2 * R)
    row_child = lax.broadcasted_iota(jnp.int32, (2 * R * CHILDREN, WIDE), 0) // (2 * R)
    col_child = lax.broadcasted_iota(jnp.int32, (2 * R * CHILDREN, WIDE), 1) // U
    diagonal = row_child == col_child
    for pair in range(boxes // 2):
        found = []
        for box in (2 * pair, 2 * pair + 1):
            cols = slice(box * WIDE, (box + 1) * WIDE)
            own = [cur_ref[0, :, cols].astype(F32), cur_ref[1, :, cols].astype(F32)]
            spread = jnp.where(diagonal, jnp.concatenate(own * CHILDREN, axis=0), 0.0)
            slab = jnp.concatenate([rad_ref[0, cols, :], rad_ref[1, cols, :]], axis=1)
            found.append(jnp.dot(spread.astype(BF16), slab, preferred_element_type=F32))
        for i in range(CHILDREN):
            by_real = jnp.concatenate([f[2 * R * i : 2 * R * i + R] for f in found], axis=0)
            by_imag = jnp.concatenate([f[2 * R * i + R : 2 * R * (i + 1)] for f in found], axis=0)
            real = by_real[:, :LANES] - by_imag[:, LANES:]
            imag = by_real[:, LANES:] + by_imag[:, :LANES]
            zero = jnp.where(low, real, swap_halves(imag))
            one = jnp.where(low, swap_halves(real), imag)
            rows = slice(pair * 2 * R, (pair + 1) * 2 * R)
            cols = slice(i * LANES, (i + 1) * LANES)
            own_ref[rows, cols] = jnp.where(low_half, zero, one).astype(BF16)
            other_ref[rows, cols] = jnp.where(low_half, one, zero).astype(BF16)


def leaves(hi, currents, radiation):
    width = currents.shape[2]
    rows = width // WIDE * R
    steps = 4
    per_step = width // steps
    shape = jax.ShapeDtypeStruct((rows, DEPTH), BF16)
    spec = pl.BlockSpec((rows // steps, DEPTH), lambda s, *_: (s, 0))
    return pl.pallas_call(
        leaf_kernel,
        grid_spec=pltpu.PrefetchScalarGridSpec(
            num_scalar_prefetch=1,
            grid=(steps,),
            in_specs=[
                pl.BlockSpec((2, R, per_step), lambda s, *_: (0, 0, s)),
                pl.BlockSpec((2, per_step, LANES), lambda s, *_: (0, s, 0)),
            ],
            out_specs=[spec, spec],
        ),
        out_shape=[shape, shape],
        compiler_params=ROOM,
        cost_estimate=cost(1),
        name="leaves",
    )(hi, currents, radiation)


def put_patterns(box_ref, patterns):
    boxes = patterns.shape[0] // R
    for chip in range(box_ref.shape[0]):
        real = patterns[:, 2 * chip * LANES : (2 * chip + 1) * LANES].reshape(boxes, 1, R, LANES)
        imag = patterns[:, (2 * chip + 1) * LANES : (2 * chip + 2) * LANES].reshape(boxes, 1, R, LANES)
        both = jnp.concatenate([real, imag], axis=1).reshape(boxes * 2 * R, LANES)
        box_ref[chip] = both.astype(BF16)


def up_kernel(lhs_ref, interp_ref, angle_ref, box_ref, mat_ref):
    cosine, sine = jnp.cos(angle_ref[...]), jnp.sin(angle_ref[...])
    for chip in range(box_ref.shape[0]):
        cols = slice(chip * LANES, (chip + 1) * LANES)
        to_real = slice(2 * chip * LANES, (2 * chip + 1) * LANES)
        to_imag = slice((2 * chip + 1) * LANES, (2 * chip + 2) * LANES)
        weights = interp_ref[:, cols].astype(F32)
        for i in range(CHILDREN):
            from_real = slice(2 * i * K0, (2 * i + 1) * K0)
            from_imag = slice((2 * i + 1) * K0, (2 * i + 2) * K0)
            even, odd = weights * cosine[i : i + 1, cols], weights * sine[i : i + 1, cols]
            mat_ref[from_real, to_real] = even.astype(BF16)
            mat_ref[from_real, to_imag] = odd.astype(BF16)
            mat_ref[from_imag, to_real] = (-odd).astype(BF16)
            mat_ref[from_imag, to_imag] = even.astype(BF16)
    put_patterns(box_ref, jnp.dot(lhs_ref[...], mat_ref[...], preferred_element_type=F32))


def again_kernel(lhs_ref, mat_ref, box_ref):
    put_patterns(box_ref, jnp.dot(lhs_ref[...], mat_ref[...], preferred_element_type=F32))


def to_boxes(lhs, interp, angle):
    rows = lhs.shape[0]
    steps = 4
    chips = CHIPS // steps
    return pl.pallas_call(
        up_kernel,
        grid=(steps,),
        in_specs=[
            pl.BlockSpec((rows, DEPTH), lambda s: (0, 0)),
            pl.BlockSpec((K0, chips * LANES), lambda s: (0, s)),
            pl.BlockSpec((CHILDREN, chips * LANES), lambda s: (0, s)),
        ],
        out_specs=[
            pl.BlockSpec((chips, 2 * rows, LANES), lambda s: (s, 0, 0)),
            pl.BlockSpec((DEPTH, 2 * chips * LANES), lambda s: (0, s)),
        ],
        out_shape=[
            jax.ShapeDtypeStruct((CHIPS, 2 * rows, LANES), BF16),
            jax.ShapeDtypeStruct((DEPTH, 2 * K1), BF16),
        ],
        compiler_params=ROOM,
        cost_estimate=cost(1),
        name="to_boxes",
    )(lhs, interp, angle)


def to_boxes_again(lhs, matrix):
    rows = lhs.shape[0]
    steps = 4
    chips = CHIPS // steps
    return pl.pallas_call(
        again_kernel,
        grid=(steps,),
        in_specs=[
            pl.BlockSpec((rows, DEPTH), lambda s: (0, 0)),
            pl.BlockSpec((DEPTH, 2 * chips * LANES), lambda s: (0, s)),
        ],
        out_specs=pl.BlockSpec((chips, 2 * rows, LANES), lambda s: (s, 0, 0)),
        out_shape=jax.ShapeDtypeStruct((CHIPS, 2 * rows, LANES), BF16),
        compiler_params=LESS,
        cost_estimate=cost(6),
        name="to_boxes_again",
    )(lhs, matrix)


def translate_kernel(list_ref, oper_ref, one_ref, two_ref, three_ref, four_ref, out_ref, box_ref, table_ref, sems, *, group):
    step = pl.program_id(0)
    per_step = out_ref.shape[0]

    @pl.when(step == 0)
    def fetch():
        copies = []
        for at, source in enumerate((one_ref, two_ref, three_ref, four_ref)):
            boxes = source.shape[0]
            copies.append(pltpu.make_async_copy(source, box_ref.at[pl.ds(at * boxes, boxes)], sems.at[at]))
        for copy in copies:
            copy.start()

        def spread(at, _):
            for part in range(2):
                some = oper_ref[part, pl.ds(pl.multiple_of(at * R, R), R), :]
                for one in range(R):
                    table_ref[at * R + one, part] = jnp.broadcast_to(some[one : one + 1], (R, LANES))
            return 0

        lax.fori_loop(0, oper_ref.shape[1] // R, spread, 0)
        for copy in copies:
            copy.wait()

    def body(at, _):
        first = (step * per_step + at * group) * (2 * IL)
        done = []
        for k in range(group):
            real = imag = None
            for j in range(IL):
                entry = first + k * 2 * IL + j
                tile = box_ref[list_ref[entry]].astype(F32)
                offset = list_ref[entry + IL]
                by_real, by_imag = table_ref[offset, 0], table_ref[offset, 1]
                box_real, box_imag = tile[:R], tile[R:]
                one = by_real * box_real - by_imag * box_imag
                two = by_real * box_imag + by_imag * box_real
                real = one if j == 0 else real + one
                imag = two if j == 0 else imag + two
            done.append(jnp.concatenate([real, imag], axis=0).astype(BF16))
        for k in range(group):
            out_ref[at * group + k] = done[k]
        return 0

    lax.fori_loop(0, per_step // group, body, 0)


def translate(lists, operators, parts):
    targets = lists.shape[0] // (2 * IL)
    boxes = parts[0].shape[0]
    steps = 2
    per_step = targets // steps
    anywhere = pl.BlockSpec(memory_space=pl.ANY)
    return pl.pallas_call(
        functools.partial(translate_kernel, group=8),
        grid_spec=pltpu.PrefetchScalarGridSpec(
            num_scalar_prefetch=1,
            grid=(steps,),
            in_specs=[pl.BlockSpec(operators.shape, lambda s, *_: (0, 0, 0))] + [anywhere] * 4,
            out_specs=pl.BlockSpec((per_step, 2 * R, LANES), lambda s, *_: (s, 0, 0)),
            scratch_shapes=[
                pltpu.VMEM((4 * boxes, 2 * R, LANES), BF16),
                pltpu.VMEM((operators.shape[1], 2, R, LANES), F32),
                pltpu.SemaphoreType.DMA((4,)),
            ],
        ),
        out_shape=pltpu.HBM((targets, 2 * R, LANES), BF16),
        compiler_params=LESS,
        cost_estimate=cost(25),
        name="translate",
    )(lists, operators, *parts)


def near_kernel(idx_ref, below_ref, own_ref, above_ref, blocks_ref, out_ref, table_ref, lhs_ref):
    step = pl.program_id(0)
    width = own_ref.shape[2]
    per_source = width // LANES
    clusters = blocks_ref.shape[1] // U
    per_tile = LANES // U
    place = lax.broadcasted_iota(jnp.int32, (2 * R, LANES), 1) // U

    @pl.when(step == 0)
    def fill():
        unrolled = 4
        for at, source in enumerate((below_ref, own_ref, above_ref)):

            def body(some, _):
                for one in range(unrolled):
                    tile = some * unrolled + one
                    cols = pl.ds(pl.multiple_of(tile * LANES, LANES), LANES)
                    parts = [source[0, :, cols].astype(F32), source[1, :, cols].astype(F32)]
                    whole = jnp.concatenate(parts, axis=0)
                    turned = [whole] + [pltpu.roll(whole, n * U, 1) for n in range(1, per_tile)]
                    for a in range(per_tile):
                        copied = turned[(0 - a) % per_tile]
                        for g in range(1, per_tile):
                            copied = jnp.where(place == g, turned[(g - a) % per_tile], copied)
                        table_ref[(at * per_source + tile) * per_tile + a] = copied
                return 0

            lax.fori_loop(0, per_source // unrolled, body, 0)
        table_ref[3 * per_source * per_tile] = jnp.zeros((2 * R, LANES), F32)

    def body(some, _):
        for one in range(CHILDREN):
            c = some * CHILDREN + one
            entry = (step * clusters + c) * NBR
            for half in range(NBR // per_tile):
                joined = table_ref[idx_ref[entry + half * per_tile]]
                for k in range(1, per_tile):
                    joined = jnp.where(place == k, table_ref[idx_ref[entry + half * per_tile + k]], joined)
                first = pl.multiple_of(c * 2 * R, 2 * R)
                lhs_ref[pl.ds(first, 2 * R), half * LANES : (half + 1) * LANES] = joined.astype(BF16)
        return 0

    lax.fori_loop(0, clusters // CHILDREN, body, 0)
    for box in range(clusters // CHILDREN):
        rows = slice(box * 2 * R * CHILDREN, (box + 1) * 2 * R * CHILDREN)
        cols = slice(box * WIDE, (box + 1) * WIDE)
        by_real = times_transposed(lhs_ref[rows, :], blocks_ref[0, cols, :])
        by_imag = times_transposed(lhs_ref[rows, :], blocks_ref[1, cols, :])
        real = []
        imag = []
        for i in range(CHILDREN):
            top = slice(2 * R * i, 2 * R * i + R)
            bottom = slice(2 * R * i + R, 2 * R * (i + 1))
            real.append(by_real[top] - by_imag[bottom])
            imag.append(by_imag[top] + by_real[bottom])
        out_ref[0, :, cols] = own_columns(real)
        out_ref[1, :, cols] = own_columns(imag)


def near_part(index, below, own, above, blocks):
    width = own.shape[2]
    steps = 8
    per_step = width // steps
    whole = pl.BlockSpec((2, R, width), lambda s, *_: (0, 0, 0))
    return pl.pallas_call(
        near_kernel,
        grid_spec=pltpu.PrefetchScalarGridSpec(
            num_scalar_prefetch=1,
            grid=(steps,),
            in_specs=[whole, whole, whole, pl.BlockSpec((2, per_step, NBR * U), lambda s, *_: (0, s, 0))],
            out_specs=pl.BlockSpec((2, R, per_step), lambda s, *_: (0, 0, s)),
            scratch_shapes=[
                pltpu.VMEM((3 * width // U + 1, 2 * R, LANES), F32),
                pltpu.VMEM((per_step // U * 2 * R, NBR * U), BF16),
            ],
        ),
        out_shape=jax.ShapeDtypeStruct((2, R, width), F32),
        compiler_params=ROOM,
        cost_estimate=cost(1),
        name="near_part",
    )(index, below, own, above, blocks)


def down_kernel(got_ref, mat_ref, out_ref, sum_ref):
    step = pl.program_id(0)
    last = pl.num_programs(0) - 1
    pieces = []
    for chip in range(got_ref.shape[0]):
        both = got_ref[chip].astype(F32).reshape(-1, 2, R, LANES)
        pieces += [both[:, 0].reshape(-1, LANES), both[:, 1].reshape(-1, LANES)]
    added = times_transposed(jnp.concatenate(pieces, axis=1).astype(BF16), mat_ref[...])

    @pl.when(step == 0)
    def begin():
        sum_ref[...] = added

    @pl.when(jnp.logical_and(step > 0, step < last))
    def go_on():
        sum_ref[...] += added

    @pl.when(step == last)
    def end():
        out_ref[...] = (sum_ref[...] + added).astype(BF16)


def from_boxes(received, matrix):
    rows = received.shape[1] // 2
    steps = 4
    chips = CHIPS // steps
    return pl.pallas_call(
        down_kernel,
        grid=(steps,),
        in_specs=[
            pl.BlockSpec((chips, 2 * rows, LANES), lambda s: (s, 0, 0)),
            pl.BlockSpec((DEPTH, 2 * chips * LANES), lambda s: (0, s)),
        ],
        out_specs=pl.BlockSpec((rows, DEPTH), lambda s: (0, 0)),
        out_shape=jax.ShapeDtypeStruct((rows, DEPTH), BF16),
        scratch_shapes=[pltpu.VMEM((rows, DEPTH), F32)],
        compiler_params=LESS,
        cost_estimate=cost(1),
        name="from_boxes",
    )(received, matrix)


def far_kernel(hi_ref, own_ref, other_ref, rad_ref, near_ref, out_ref):
    low_half = hi_ref[0] == 0
    boxes = out_ref.shape[2] // WIDE
    low = low_lanes(2 * R)
    for pair in range(boxes // 2):
        rows = slice(pair * 2 * R, (pair + 1) * 2 * R)
        pieces = [[], []]
        for i in range(CHILDREN):
            cols = slice(i * LANES, (i + 1) * LANES)
            own, other = own_ref[rows, cols].astype(F32), other_ref[rows, cols].astype(F32)
            zero, one = jnp.where(low_half, own, other), jnp.where(low_half, other, own)
            real = jnp.where(low, zero, swap_halves(one))
            imag = jnp.where(low, swap_halves(zero), one)
            for k in range(2):
                part = slice(k * R, (k + 1) * R)
                pieces[k].append(jnp.concatenate([real[part], imag[part]], axis=1))
                pieces[k].append(jnp.concatenate([imag[part], -real[part]], axis=1))
        for k in range(2):
            fields = jnp.concatenate(pieces[k], axis=0).astype(BF16)
            cols = slice((2 * pair + k) * WIDE, (2 * pair + k + 1) * WIDE)
            slab = jnp.concatenate([rad_ref[0, cols, :], rad_ref[1, cols, :]], axis=1)
            terms = times_transposed(fields, slab)
            for part in range(2):
                own = [terms[2 * R * i + part * R : 2 * R * i + (part + 1) * R] for i in range(CHILDREN)]
                out_ref[part, :, cols] = near_ref[part, :, cols] + own_columns(own)


def far_part(hi, own, other, radiation, near_field):
    width = near_field.shape[2]
    rows = own.shape[0]
    steps = 4
    per_step = width // steps
    field = pl.BlockSpec((rows // steps, DEPTH), lambda s, *_: (s, 0))
    wave = pl.BlockSpec((2, R, per_step), lambda s, *_: (0, 0, s))
    return pl.pallas_call(
        far_kernel,
        grid_spec=pltpu.PrefetchScalarGridSpec(
            num_scalar_prefetch=1,
            grid=(steps,),
            in_specs=[field, field, pl.BlockSpec((2, per_step, LANES), lambda s, *_: (0, s, 0)), wave],
            out_specs=wave,
        ),
        out_shape=jax.ShapeDtypeStruct((2, R, width), F32),
        compiler_params=LESS,
        cost_estimate=cost(1),
        name="far_part",
    )(hi, own, other, radiation, near_field)


def swapped(array):
    return lax.all_to_all(array, INSIDE, split_axis=0, concat_axis=0, tiled=True)


def padded(array):
    return jnp.pad(array, [(0, 0)] * (array.ndim - 1) + [(0, LANES - array.shape[-1])])


def to_owners(boxes, samples):
    rows = boxes.shape[1]
    if samples != LANES:
        boxes = boxes.reshape(CHIPS, rows, LANES // samples, samples).transpose(0, 2, 1, 3).reshape(-1, rows, samples)
    got = swapped(boxes)
    if samples != LANES:
        got = padded(got)
    return got.reshape(-1, 2 * R, LANES)


def from_owners(fields, rows, samples):
    fields = fields.reshape(-1, rows, LANES)
    if samples == LANES:
        return swapped(fields)
    got = swapped(fields[..., :samples]).reshape(CHIPS, LANES // samples, rows, samples)
    return got.transpose(0, 2, 1, 3).reshape(CHIPS, rows, LANES)


def operator_table(translation):
    groups, mids = lax.axis_size("grp"), lax.axis_size("mid")
    core = lax.axis_index("core")
    pairs = [
        (((h * groups + g) * mids + m) * 2 + c, ((g * 2 + h) * mids + m) * 2 + c)
        for g in range(groups)
        for h in range(2)
        for m in range(mids)
        for c in range(2)
    ]
    mine = lax.ppermute(jnp.swapaxes(translation, 1, 2), ALL, pairs)
    other = across(mine, "core").astype(F32)
    mine = mine.astype(F32)
    low = jnp.where(core == 0, mine, other)
    high = jnp.where(core == 0, other, mine)
    operator = padded(jnp.swapaxes(jnp.concatenate([low, high], axis=1), 1, 2))
    return jnp.pad(operator, ((0, 0), (0, -operator.shape[1] % R), (0, 0)))


def target_lists(trans_box, trans_off, hi, core):
    groups, mids = lax.axis_size("grp"), lax.axis_size("mid")
    total = trans_box.shape[0]
    per = total // (groups * mids * 4)
    device, inside = trans_box // per, trans_box % per
    group, side = device // (4 * mids), device // (2 * mids) % 2
    mid, its_core = device // 2 % mids, device % 2
    block = (side ^ hi) * 2 + (its_core ^ core)
    place = (block * (groups * mids) + group * mids + mid) * per + inside
    lists = jnp.concatenate([place, trans_off], axis=1).reshape(groups, 2, mids, 2, per, 2 * IL)
    lists = jnp.where(core == 0, lists[:, :, :, 0], lists[:, :, :, 1])
    first, second = lists[:, 0].reshape(-1), lists[:, 1].reshape(-1)
    return jnp.where(hi == 0, first, second), jnp.where(hi == 0, second, first)


def local(
    currents,
    near_blocks,
    near_list,
    near_count,
    radiation,
    interp,
    shift_angle,
    translation,
    trans_box,
    trans_off,
):
    clusters = near_list.shape[0]
    samples = 2 * translation.shape[2]
    rows = clusters // CHILDREN * 2 * R
    hi, core = lax.axis_index("hi"), lax.axis_index("core")
    side = hi.reshape(1).astype(jnp.int32)
    radiation = radiation.reshape(2, clusters * U, LANES)
    near_blocks = near_blocks.reshape(2, clusters * U, NBR * U)

    first = (lax.axis_index(ALL) - 1) * clusters
    live = jnp.arange(NBR, dtype=jnp.int32)[None, :] < near_count[:, None]
    index = jnp.where(live, near_list - first, 3 * clusters).reshape(-1)
    lists = target_lists(trans_box, trans_off, hi, core)

    leaf_own, leaf_other = leaves(side, currents, radiation)
    leaf_partner = across(leaf_other, "hi")
    boxes_own, matrix = to_boxes(leaf_own, interp, shift_angle)
    rows_own = to_owners(boxes_own, samples)
    swapped_own = across(rows_own, "core")
    operators = operator_table(translation)
    inside = across(currents, "core")
    leaf_partner, lists, index, operators, inside = lax.optimization_barrier(
        (leaf_partner, lists, index, operators, inside)
    )
    rows_partner = to_owners(to_boxes_again(leaf_partner, matrix), samples)
    parts = (rows_own, swapped_own, rows_partner, across(rows_partner, "core"))

    fields_partner = translate(lists[1], operators, parts)
    fields_partner, late_currents = lax.optimization_barrier((fields_partner, currents))
    outside = next_chip(late_currents)
    fields_own = translate(lists[0], operators, parts)
    fields_own, outside = lax.optimization_barrier((fields_own, outside))
    down_partner = from_boxes(from_owners(fields_partner, rows, samples), matrix)
    below, above = jnp.where(core == 0, outside, inside), jnp.where(core == 0, inside, outside)
    down_partner, index = lax.optimization_barrier((down_partner, index))
    down_other = across(down_partner, "hi")
    near_field = near_part(index, below, currents, above, near_blocks)
    down_own = from_boxes(from_owners(fields_own, rows, samples), matrix)
    return far_part(side, down_own, down_other, radiation, near_field)


def solution(mesh):
    devices = mesh.devices
    groups, rest = devices.shape
    cut = Mesh(devices.reshape(groups, 2, rest // 4, 2), ALL)
    placed = (
        P(None, None, ALL),
        P(None, ALL, None, None),
        P(ALL, None),
        P(ALL),
        P(None, ALL, None, None),
        P(),
        P(),
        P(None, None, ALL),
        P(),
        P(),
    )
    return jax.shard_map(local, mesh=cut, in_specs=placed, out_specs=P(None, None, ALL), check_vma=False)
```

```python
import functools

import jax
import jax.numpy as jnp
from jax import lax
from jax.experimental import pallas as pl
from jax.experimental.pallas import tpu as pltpu
from jax.sharding import Mesh
from jax.sharding import PartitionSpec as P

R = 8
U = 32
NBR = 8
K0 = 64
K1 = 1024
IL = 12
CHILDREN = 8
WIDE = CHILDREN * U
LANES = 128
HALF = 64
CHIPS = K1 // LANES
DEPTH = 2 * CHILDREN * K0
ALL = ("grp", "hi", "mid", "core")
INSIDE = ("grp", "mid")
F32 = jnp.float32
BF16 = jnp.bfloat16
ROOM = pltpu.CompilerParams(vmem_limit_bytes=58 * 2**20)
LESS = pltpu.CompilerParams(vmem_limit_bytes=28 * 2**20)


def cost(megabytes):
    return pl.CostEstimate(flops=10**6, bytes_accessed=megabytes * 10**6, transcendentals=0)


def neighbours(array):
    size = lax.axis_size(ALL)
    pairs = [(i, i + 1) for i in range(1, size - 1, 2)] + [(i + 1, i) for i in range(1, size - 1, 2)]
    outside = lax.ppermute(array, ALL, pairs)
    inside = across(array, "core")
    first = lax.axis_index("core") == 0
    return jnp.where(first, outside, inside), jnp.where(first, inside, outside)


def across(array, axis):
    return lax.ppermute(array, axis, [(0, 1), (1, 0)])


def swap_halves(array):
    return pltpu.roll(array, HALF, 1)


def low_lanes(rows):
    return lax.broadcasted_iota(jnp.int32, (rows, LANES), 1) < HALF


def times_transposed(left, right):
    return lax.dot_general(left, right, (((1,), (1,)), ((), ())), preferred_element_type=F32)


def own_columns(pieces):
    child = lax.broadcasted_iota(jnp.int32, (R, WIDE), 1) // U
    picked = pieces[0]
    for i in range(1, CHILDREN):
        picked = jnp.where(child == i, pieces[i], picked)
    return picked


def leaf_kernel(hi_ref, cur_ref, rad_ref, own_ref, other_ref):
    low_half = hi_ref[0] == 0
    boxes = cur_ref.shape[2] // WIDE
    low = low_lanes(2 * R)
    row_child = lax.broadcasted_iota(jnp.int32, (2 * R * CHILDREN, WIDE), 0) // (2 * R)
    col_child = lax.broadcasted_iota(jnp.int32, (2 * R * CHILDREN, WIDE), 1) // U
    diagonal = row_child == col_child
    for pair in range(boxes // 2):
        found = []
        for box in (2 * pair, 2 * pair + 1):
            cols = slice(box * WIDE, (box + 1) * WIDE)
            own = [cur_ref[0, :, cols].astype(F32), cur_ref[1, :, cols].astype(F32)]
            spread = jnp.where(diagonal, jnp.concatenate(own * CHILDREN, axis=0), 0.0)
            slab = jnp.concatenate([rad_ref[0, cols, :], rad_ref[1, cols, :]], axis=1)
            found.append(jnp.dot(spread.astype(BF16), slab, preferred_element_type=F32))
        for i in range(CHILDREN):
            by_real = jnp.concatenate([f[2 * R * i : 2 * R * i + R] for f in found], axis=0)
            by_imag = jnp.concatenate([f[2 * R * i + R : 2 * R * (i + 1)] for f in found], axis=0)
            real = by_real[:, :LANES] - by_imag[:, LANES:]
            imag = by_real[:, LANES:] + by_imag[:, :LANES]
            zero = jnp.where(low, real, swap_halves(imag))
            one = jnp.where(low, swap_halves(real), imag)
            rows = slice(pair * 2 * R, (pair + 1) * 2 * R)
            cols = slice(i * LANES, (i + 1) * LANES)
            own_ref[rows, cols] = jnp.where(low_half, zero, one).astype(BF16)
            other_ref[rows, cols] = jnp.where(low_half, one, zero).astype(BF16)


def leaves(hi, currents, radiation):
    width = currents.shape[2]
    rows = width // WIDE * R
    steps = 8
    per_step = width // steps
    shape = jax.ShapeDtypeStruct((rows, DEPTH), BF16)
    spec = pl.BlockSpec((rows // steps, DEPTH), lambda s, *_: (s, 0))
    return pl.pallas_call(
        leaf_kernel,
        grid_spec=pltpu.PrefetchScalarGridSpec(
            num_scalar_prefetch=1,
            grid=(steps,),
            in_specs=[
                pl.BlockSpec((2, R, per_step), lambda s, *_: (0, 0, s)),
                pl.BlockSpec((2, per_step, LANES), lambda s, *_: (0, s, 0)),
            ],
            out_specs=[spec, spec],
        ),
        out_shape=[shape, shape],
        compiler_params=ROOM,
        cost_estimate=cost(1),
        name="leaves",
    )(hi, currents, radiation)


def put_patterns(box_ref, patterns):
    boxes = patterns.shape[0] // R
    for chip in range(box_ref.shape[0]):
        real = patterns[:, 2 * chip * LANES : (2 * chip + 1) * LANES].reshape(boxes, 1, R, LANES)
        imag = patterns[:, (2 * chip + 1) * LANES : (2 * chip + 2) * LANES].reshape(boxes, 1, R, LANES)
        both = jnp.concatenate([real, imag], axis=1).reshape(boxes * 2 * R, LANES)
        box_ref[chip] = both.astype(BF16)


def up_kernel(lhs_ref, interp_ref, angle_ref, box_ref, mat_ref):
    cosine, sine = jnp.cos(angle_ref[...]), jnp.sin(angle_ref[...])
    for chip in range(box_ref.shape[0]):
        cols = slice(chip * LANES, (chip + 1) * LANES)
        to_real = slice(2 * chip * LANES, (2 * chip + 1) * LANES)
        to_imag = slice((2 * chip + 1) * LANES, (2 * chip + 2) * LANES)
        weights = interp_ref[:, cols].astype(F32)
        for i in range(CHILDREN):
            from_real = slice(2 * i * K0, (2 * i + 1) * K0)
            from_imag = slice((2 * i + 1) * K0, (2 * i + 2) * K0)
            even, odd = weights * cosine[i : i + 1, cols], weights * sine[i : i + 1, cols]
            mat_ref[from_real, to_real] = even.astype(BF16)
            mat_ref[from_real, to_imag] = odd.astype(BF16)
            mat_ref[from_imag, to_real] = (-odd).astype(BF16)
            mat_ref[from_imag, to_imag] = even.astype(BF16)
    put_patterns(box_ref, jnp.dot(lhs_ref[...], mat_ref[...], preferred_element_type=F32))


def again_kernel(lhs_ref, mat_ref, box_ref):
    put_patterns(box_ref, jnp.dot(lhs_ref[...], mat_ref[...], preferred_element_type=F32))


def to_boxes(lhs, interp, angle):
    rows = lhs.shape[0]
    steps = 4
    chips = CHIPS // steps
    return pl.pallas_call(
        up_kernel,
        grid=(steps,),
        in_specs=[
            pl.BlockSpec((rows, DEPTH), lambda s: (0, 0)),
            pl.BlockSpec((K0, chips * LANES), lambda s: (0, s)),
            pl.BlockSpec((CHILDREN, chips * LANES), lambda s: (0, s)),
        ],
        out_specs=[
            pl.BlockSpec((chips, 2 * rows, LANES), lambda s: (s, 0, 0)),
            pl.BlockSpec((DEPTH, 2 * chips * LANES), lambda s: (0, s)),
        ],
        out_shape=[
            jax.ShapeDtypeStruct((CHIPS, 2 * rows, LANES), BF16),
            jax.ShapeDtypeStruct((DEPTH, 2 * K1), BF16),
        ],
        compiler_params=ROOM,
        cost_estimate=cost(1),
        name="to_boxes",
    )(lhs, interp, angle)


def to_boxes_again(lhs, matrix):
    rows = lhs.shape[0]
    steps = 4
    chips = CHIPS // steps
    return pl.pallas_call(
        again_kernel,
        grid=(steps,),
        in_specs=[
            pl.BlockSpec((rows, DEPTH), lambda s: (0, 0)),
            pl.BlockSpec((DEPTH, 2 * chips * LANES), lambda s: (0, s)),
        ],
        out_specs=pl.BlockSpec((chips, 2 * rows, LANES), lambda s: (s, 0, 0)),
        out_shape=jax.ShapeDtypeStruct((CHIPS, 2 * rows, LANES), BF16),
        compiler_params=LESS,
        cost_estimate=cost(6),
        name="to_boxes_again",
    )(lhs, matrix)


def translate_kernel(list_ref, oper_ref, one_ref, two_ref, three_ref, four_ref, out_ref, box_ref, table_ref, sems, *, group):
    step = pl.program_id(0)
    per_step = out_ref.shape[0]

    @pl.when(step == 0)
    def fetch():
        copies = []
        for at, source in enumerate((one_ref, two_ref, three_ref, four_ref)):
            boxes = source.shape[0]
            copies.append(pltpu.make_async_copy(source, box_ref.at[pl.ds(at * boxes, boxes)], sems.at[at]))
        for copy in copies:
            copy.start()

        def spread(at, _):
            for part in range(2):
                some = oper_ref[part, pl.ds(pl.multiple_of(at * R, R), R), :]
                for one in range(R):
                    table_ref[at * R + one, part] = jnp.broadcast_to(some[one : one + 1], (R, LANES))
            return 0

        lax.fori_loop(0, oper_ref.shape[1] // R, spread, 0)
        for copy in copies:
            copy.wait()

    def body(at, _):
        first = (step * per_step + at * group) * (2 * IL)
        done = []
        for k in range(group):
            real = imag = None
            for j in range(IL):
                entry = first + k * 2 * IL + j
                tile = box_ref[list_ref[entry]].astype(F32)
                offset = list_ref[entry + IL]
                by_real, by_imag = table_ref[offset, 0], table_ref[offset, 1]
                box_real, box_imag = tile[:R], tile[R:]
                one = by_real * box_real - by_imag * box_imag
                two = by_real * box_imag + by_imag * box_real
                real = one if j == 0 else real + one
                imag = two if j == 0 else imag + two
            done.append(jnp.concatenate([real, imag], axis=0).astype(BF16))
        for k in range(group):
            out_ref[at * group + k] = done[k]
        return 0

    lax.fori_loop(0, per_step // group, body, 0)


def translate(lists, operators, parts):
    targets = lists.shape[0] // (2 * IL)
    boxes = parts[0].shape[0]
    steps = 2
    per_step = targets // steps
    anywhere = pl.BlockSpec(memory_space=pl.ANY)
    return pl.pallas_call(
        functools.partial(translate_kernel, group=8),
        grid_spec=pltpu.PrefetchScalarGridSpec(
            num_scalar_prefetch=1,
            grid=(steps,),
            in_specs=[pl.BlockSpec(operators.shape, lambda s, *_: (0, 0, 0))] + [anywhere] * 4,
            out_specs=pl.BlockSpec((per_step, 2 * R, LANES), lambda s, *_: (s, 0, 0)),
            scratch_shapes=[
                pltpu.VMEM((4 * boxes, 2 * R, LANES), BF16),
                pltpu.VMEM((operators.shape[1], 2, R, LANES), F32),
                pltpu.SemaphoreType.DMA((4,)),
            ],
        ),
        out_shape=jax.ShapeDtypeStruct((targets, 2 * R, LANES), BF16),
        compiler_params=LESS,
        cost_estimate=cost(25),
        name="translate",
    )(lists, operators, *parts)


def near_kernel(idx_ref, below_ref, own_ref, above_ref, blocks_ref, out_ref, table_ref, lhs_ref):
    step = pl.program_id(0)
    width = own_ref.shape[2]
    per_source = width // LANES
    clusters = blocks_ref.shape[1] // U
    per_tile = LANES // U
    place = lax.broadcasted_iota(jnp.int32, (2 * R, LANES), 1) // U

    @pl.when(step == 0)
    def fill():
        unrolled = 4
        for at, source in enumerate((below_ref, own_ref, above_ref)):

            def body(some, _):
                for one in range(unrolled):
                    tile = some * unrolled + one
                    cols = pl.ds(pl.multiple_of(tile * LANES, LANES), LANES)
                    parts = [source[0, :, cols].astype(F32), source[1, :, cols].astype(F32)]
                    whole = jnp.concatenate(parts, axis=0)
                    turned = [whole] + [pltpu.roll(whole, n * U, 1) for n in range(1, per_tile)]
                    for a in range(per_tile):
                        copied = turned[(0 - a) % per_tile]
                        for g in range(1, per_tile):
                            copied = jnp.where(place == g, turned[(g - a) % per_tile], copied)
                        table_ref[(at * per_source + tile) * per_tile + a] = copied
                return 0

            lax.fori_loop(0, per_source // unrolled, body, 0)
        table_ref[3 * per_source * per_tile] = jnp.zeros((2 * R, LANES), F32)

    def body(some, _):
        for one in range(CHILDREN):
            c = some * CHILDREN + one
            entry = (step * clusters + c) * NBR
            for half in range(NBR // per_tile):
                joined = table_ref[idx_ref[entry + half * per_tile]]
                for k in range(1, per_tile):
                    joined = jnp.where(place == k, table_ref[idx_ref[entry + half * per_tile + k]], joined)
                first = pl.multiple_of(c * 2 * R, 2 * R)
                lhs_ref[pl.ds(first, 2 * R), half * LANES : (half + 1) * LANES] = joined.astype(BF16)
        return 0

    lax.fori_loop(0, clusters // CHILDREN, body, 0)
    for box in range(clusters // CHILDREN):
        rows = slice(box * 2 * R * CHILDREN, (box + 1) * 2 * R * CHILDREN)
        cols = slice(box * WIDE, (box + 1) * WIDE)
        by_real = times_transposed(lhs_ref[rows, :], blocks_ref[0, cols, :])
        by_imag = times_transposed(lhs_ref[rows, :], blocks_ref[1, cols, :])
        real = []
        imag = []
        for i in range(CHILDREN):
            top = slice(2 * R * i, 2 * R * i + R)
            bottom = slice(2 * R * i + R, 2 * R * (i + 1))
            real.append(by_real[top] - by_imag[bottom])
            imag.append(by_imag[top] + by_real[bottom])
        out_ref[0, :, cols] = own_columns(real)
        out_ref[1, :, cols] = own_columns(imag)


def near_part(index, below, own, above, blocks):
    width = own.shape[2]
    steps = 8
    per_step = width // steps
    whole = pl.BlockSpec((2, R, width), lambda s, *_: (0, 0, 0))
    return pl.pallas_call(
        near_kernel,
        grid_spec=pltpu.PrefetchScalarGridSpec(
            num_scalar_prefetch=1,
            grid=(steps,),
            in_specs=[whole, whole, whole, pl.BlockSpec((2, per_step, NBR * U), lambda s, *_: (0, s, 0))],
            out_specs=pl.BlockSpec((2, R, per_step), lambda s, *_: (0, 0, s)),
            scratch_shapes=[
                pltpu.VMEM((3 * width // U + 1, 2 * R, LANES), F32),
                pltpu.VMEM((per_step // U * 2 * R, NBR * U), BF16),
            ],
        ),
        out_shape=jax.ShapeDtypeStruct((2, R, width), F32),
        compiler_params=ROOM,
        cost_estimate=cost(1),
        name="near_part",
    )(index, below, own, above, blocks)


def down_kernel(got_ref, mat_ref, out_ref, sum_ref):
    step = pl.program_id(0)
    last = pl.num_programs(0) - 1
    pieces = []
    for chip in range(got_ref.shape[0]):
        both = got_ref[chip].astype(F32).reshape(-1, 2, R, LANES)
        pieces += [both[:, 0].reshape(-1, LANES), both[:, 1].reshape(-1, LANES)]
    added = times_transposed(jnp.concatenate(pieces, axis=1).astype(BF16), mat_ref[...])

    @pl.when(step == 0)
    def begin():
        sum_ref[...] = added

    @pl.when(jnp.logical_and(step > 0, step < last))
    def go_on():
        sum_ref[...] += added

    @pl.when(step == last)
    def end():
        out_ref[...] = (sum_ref[...] + added).astype(BF16)


def from_boxes(received, matrix):
    rows = received.shape[1] // 2
    steps = 4
    chips = CHIPS // steps
    return pl.pallas_call(
        down_kernel,
        grid=(steps,),
        in_specs=[
            pl.BlockSpec((chips, 2 * rows, LANES), lambda s: (s, 0, 0)),
            pl.BlockSpec((DEPTH, 2 * chips * LANES), lambda s: (0, s)),
        ],
        out_specs=pl.BlockSpec((rows, DEPTH), lambda s: (0, 0)),
        out_shape=jax.ShapeDtypeStruct((rows, DEPTH), BF16),
        scratch_shapes=[pltpu.VMEM((rows, DEPTH), F32)],
        compiler_params=LESS,
        cost_estimate=cost(1),
        name="from_boxes",
    )(received, matrix)


def far_kernel(hi_ref, own_ref, other_ref, rad_ref, near_ref, out_ref):
    low_half = hi_ref[0] == 0
    boxes = out_ref.shape[2] // WIDE
    low = low_lanes(2 * R)
    for pair in range(boxes // 2):
        rows = slice(pair * 2 * R, (pair + 1) * 2 * R)
        pieces = [[], []]
        for i in range(CHILDREN):
            cols = slice(i * LANES, (i + 1) * LANES)
            own, other = own_ref[rows, cols].astype(F32), other_ref[rows, cols].astype(F32)
            zero, one = jnp.where(low_half, own, other), jnp.where(low_half, other, own)
            real = jnp.where(low, zero, swap_halves(one))
            imag = jnp.where(low, swap_halves(zero), one)
            for k in range(2):
                part = slice(k * R, (k + 1) * R)
                pieces[k].append(jnp.concatenate([real[part], imag[part]], axis=1))
                pieces[k].append(jnp.concatenate([imag[part], -real[part]], axis=1))
        for k in range(2):
            fields = jnp.concatenate(pieces[k], axis=0).astype(BF16)
            cols = slice((2 * pair + k) * WIDE, (2 * pair + k + 1) * WIDE)
            slab = jnp.concatenate([rad_ref[0, cols, :], rad_ref[1, cols, :]], axis=1)
            terms = times_transposed(fields, slab)
            for part in range(2):
                own = [terms[2 * R * i + part * R : 2 * R * i + (part + 1) * R] for i in range(CHILDREN)]
                out_ref[part, :, cols] = near_ref[part, :, cols] + own_columns(own)


def far_part(hi, own, other, radiation, near_field):
    width = near_field.shape[2]
    rows = own.shape[0]
    steps = 4
    per_step = width // steps
    field = pl.BlockSpec((rows // steps, DEPTH), lambda s, *_: (s, 0))
    wave = pl.BlockSpec((2, R, per_step), lambda s, *_: (0, 0, s))
    return pl.pallas_call(
        far_kernel,
        grid_spec=pltpu.PrefetchScalarGridSpec(
            num_scalar_prefetch=1,
            grid=(steps,),
            in_specs=[field, field, pl.BlockSpec((2, per_step, LANES), lambda s, *_: (0, s, 0)), wave],
            out_specs=wave,
        ),
        out_shape=jax.ShapeDtypeStruct((2, R, width), F32),
        compiler_params=LESS,
        cost_estimate=cost(1),
        name="far_part",
    )(hi, own, other, radiation, near_field)


def swapped(array):
    return lax.all_to_all(array, INSIDE, split_axis=0, concat_axis=0, tiled=True)


def padded(array):
    return jnp.pad(array, [(0, 0)] * (array.ndim - 1) + [(0, LANES - array.shape[-1])])


def to_owners(boxes, samples):
    rows = boxes.shape[1]
    if samples != LANES:
        boxes = boxes.reshape(CHIPS, rows, LANES // samples, samples).transpose(0, 2, 1, 3).reshape(-1, rows, samples)
    got = swapped(boxes)
    if samples != LANES:
        got = padded(got)
    return got.reshape(-1, 2 * R, LANES)


def from_owners(fields, rows, samples):
    fields = fields.reshape(-1, rows, LANES)
    if samples == LANES:
        return swapped(fields)
    got = swapped(fields[..., :samples]).reshape(CHIPS, LANES // samples, rows, samples)
    return got.transpose(0, 2, 1, 3).reshape(CHIPS, rows, LANES)


def operator_table(translation):
    groups, mids = lax.axis_size("grp"), lax.axis_size("mid")
    core = lax.axis_index("core")
    pairs = [
        (((h * groups + g) * mids + m) * 2 + c, ((g * 2 + h) * mids + m) * 2 + c)
        for g in range(groups)
        for h in range(2)
        for m in range(mids)
        for c in range(2)
    ]
    mine = lax.ppermute(jnp.swapaxes(translation, 1, 2), ALL, pairs)
    other = across(mine, "core").astype(F32)
    mine = mine.astype(F32)
    low = jnp.where(core == 0, mine, other)
    high = jnp.where(core == 0, other, mine)
    operator = padded(jnp.swapaxes(jnp.concatenate([low, high], axis=1), 1, 2))
    return jnp.pad(operator, ((0, 0), (0, -operator.shape[1] % R), (0, 0)))


def target_lists(trans_box, trans_off, hi, core):
    groups, mids = lax.axis_size("grp"), lax.axis_size("mid")
    total = trans_box.shape[0]
    per = total // (groups * mids * 4)
    device, inside = trans_box // per, trans_box % per
    group, side = device // (4 * mids), device // (2 * mids) % 2
    mid, its_core = device // 2 % mids, device % 2
    block = (side ^ hi) * 2 + (its_core ^ core)
    place = (block * (groups * mids) + group * mids + mid) * per + inside
    lists = jnp.concatenate([place, trans_off], axis=1).reshape(groups, 2, mids, 2, per, 2 * IL)
    lists = jnp.where(core == 0, lists[:, :, :, 0], lists[:, :, :, 1])
    first, second = lists[:, 0].reshape(-1), lists[:, 1].reshape(-1)
    return jnp.where(hi == 0, first, second), jnp.where(hi == 0, second, first)


def local(
    currents,
    near_blocks,
    near_list,
    near_count,
    radiation,
    interp,
    shift_angle,
    translation,
    trans_box,
    trans_off,
):
    clusters = near_list.shape[0]
    samples = 2 * translation.shape[2]
    rows = clusters // CHILDREN * 2 * R
    hi, core = lax.axis_index("hi"), lax.axis_index("core")
    side = hi.reshape(1).astype(jnp.int32)
    radiation = radiation.reshape(2, clusters * U, LANES)
    near_blocks = near_blocks.reshape(2, clusters * U, NBR * U)

    first = (lax.axis_index(ALL) - 1) * clusters
    live = jnp.arange(NBR, dtype=jnp.int32)[None, :] < near_count[:, None]
    index = jnp.where(live, near_list - first, 3 * clusters).reshape(-1)
    lists = target_lists(trans_box, trans_off, hi, core)

    leaf_own, leaf_other = leaves(side, currents, radiation)
    leaf_partner = across(leaf_other, "hi")
    boxes_own, matrix = to_boxes(leaf_own, interp, shift_angle)
    rows_own = to_owners(boxes_own, samples)
    swapped_own = across(rows_own, "core")
    operators = operator_table(translation)
    below, above = neighbours(currents)
    leaf_partner, lists, index, operators, below, above = lax.optimization_barrier(
        (leaf_partner, lists, index, operators, below, above)
    )
    rows_partner = to_owners(to_boxes_again(leaf_partner, matrix), samples)
    parts = (rows_own, swapped_own, rows_partner, across(rows_partner, "core"))

    fields_partner = translate(lists[1], operators, parts)
    down_partner = from_boxes(from_owners(fields_partner, rows, samples), matrix)
    fields_own = translate(lists[0], operators, parts)
    down_partner, index = lax.optimization_barrier((down_partner, index))
    down_other = across(down_partner, "hi")
    near_field = near_part(index, below, currents, above, near_blocks)
    down_own = from_boxes(from_owners(fields_own, rows, samples), matrix)
    return far_part(side, down_own, down_other, radiation, near_field)


def solution(mesh):
    devices = mesh.devices
    groups, rest = devices.shape
    cut = Mesh(devices.reshape(groups, 2, rest // 4, 2), ALL)
    placed = (
        P(None, None, ALL),
        P(None, ALL, None, None),
        P(ALL, None),
        P(ALL),
        P(None, ALL, None, None),
        P(),
        P(),
        P(None, None, ALL),
        P(),
        P(),
    )
    return jax.shard_map(local, mesh=cut, in_specs=placed, out_specs=P(None, None, ALL), check_vma=False)
```

```python
import functools

import jax
import jax.numpy as jnp
from jax import lax
from jax.experimental import pallas as pl
from jax.experimental.pallas import tpu as pltpu
from jax.sharding import Mesh
from jax.sharding import PartitionSpec as P

R = 8
U = 32
NBR = 8
K0 = 64
K1 = 1024
IL = 12
CHILDREN = 8
WIDE = CHILDREN * U
LANES = 128
HALF = 64
CHIPS = K1 // LANES
DEPTH = 2 * CHILDREN * K0
ALL = ("grp", "hi", "mid", "core")
INSIDE = ("grp", "mid")
F32 = jnp.float32
BF16 = jnp.bfloat16
ROOM = pltpu.CompilerParams(vmem_limit_bytes=58 * 2**20)
LESS = pltpu.CompilerParams(vmem_limit_bytes=28 * 2**20)


def cost(megabytes):
    return pl.CostEstimate(flops=10**6, bytes_accessed=megabytes * 10**6, transcendentals=0)


def neighbours(array):
    size = lax.axis_size(ALL)
    pairs = [(i, i + 1) for i in range(1, size - 1, 2)] + [(i + 1, i) for i in range(1, size - 1, 2)]
    outside = lax.ppermute(array, ALL, pairs)
    inside = across(array, "core")
    first = lax.axis_index("core") == 0
    return jnp.where(first, outside, inside), jnp.where(first, inside, outside)


def across(array, axis):
    return lax.ppermute(array, axis, [(0, 1), (1, 0)])


def swap_halves(array):
    return pltpu.roll(array, HALF, 1)


def low_lanes(rows):
    return lax.broadcasted_iota(jnp.int32, (rows, LANES), 1) < HALF


def times_transposed(left, right):
    return lax.dot_general(left, right, (((1,), (1,)), ((), ())), preferred_element_type=F32)


def own_columns(pieces):
    child = lax.broadcasted_iota(jnp.int32, (R, WIDE), 1) // U
    picked = pieces[0]
    for i in range(1, CHILDREN):
        picked = jnp.where(child == i, pieces[i], picked)
    return picked


def leaf_kernel(hi_ref, cur_ref, rad_ref, own_ref, other_ref):
    low_half = hi_ref[0] == 0
    boxes = cur_ref.shape[2] // WIDE
    low = low_lanes(2 * R)
    row_child = lax.broadcasted_iota(jnp.int32, (2 * R * CHILDREN, WIDE), 0) // (2 * R)
    col_child = lax.broadcasted_iota(jnp.int32, (2 * R * CHILDREN, WIDE), 1) // U
    diagonal = row_child == col_child
    for pair in range(boxes // 2):
        found = []
        for box in (2 * pair, 2 * pair + 1):
            cols = slice(box * WIDE, (box + 1) * WIDE)
            own = [cur_ref[0, :, cols].astype(F32), cur_ref[1, :, cols].astype(F32)]
            spread = jnp.where(diagonal, jnp.concatenate(own * CHILDREN, axis=0), 0.0)
            slab = jnp.concatenate([rad_ref[0, cols, :], rad_ref[1, cols, :]], axis=1)
            found.append(jnp.dot(spread.astype(BF16), slab, preferred_element_type=F32))
        for i in range(CHILDREN):
            by_real = jnp.concatenate([f[2 * R * i : 2 * R * i + R] for f in found], axis=0)
            by_imag = jnp.concatenate([f[2 * R * i + R : 2 * R * (i + 1)] for f in found], axis=0)
            real = by_real[:, :LANES] - by_imag[:, LANES:]
            imag = by_real[:, LANES:] + by_imag[:, :LANES]
            zero = jnp.where(low, real, swap_halves(imag))
            one = jnp.where(low, swap_halves(real), imag)
            rows = slice(pair * 2 * R, (pair + 1) * 2 * R)
            cols = slice(i * LANES, (i + 1) * LANES)
            own_ref[rows, cols] = jnp.where(low_half, zero, one).astype(BF16)
            other_ref[rows, cols] = jnp.where(low_half, one, zero).astype(BF16)


def leaves(hi, currents, radiation):
    width = currents.shape[2]
    rows = width // WIDE * R
    steps = 2
    per_step = width // steps
    shape = jax.ShapeDtypeStruct((rows, DEPTH), BF16)
    spec = pl.BlockSpec((rows // steps, DEPTH), lambda s, *_: (s, 0))
    return pl.pallas_call(
        leaf_kernel,
        grid_spec=pltpu.PrefetchScalarGridSpec(
            num_scalar_prefetch=1,
            grid=(steps,),
            in_specs=[
                pl.BlockSpec((2, R, per_step), lambda s, *_: (0, 0, s)),
                pl.BlockSpec((2, per_step, LANES), lambda s, *_: (0, s, 0)),
            ],
            out_specs=[spec, spec],
        ),
        out_shape=[shape, shape],
        compiler_params=ROOM,
        cost_estimate=cost(1),
        name="leaves",
    )(hi, currents, radiation)


def put_patterns(box_ref, patterns):
    boxes = patterns.shape[0] // R
    for chip in range(box_ref.shape[0]):
        real = patterns[:, 2 * chip * LANES : (2 * chip + 1) * LANES].reshape(boxes, 1, R, LANES)
        imag = patterns[:, (2 * chip + 1) * LANES : (2 * chip + 2) * LANES].reshape(boxes, 1, R, LANES)
        both = jnp.concatenate([real, imag], axis=1).reshape(boxes * 2 * R, LANES)
        box_ref[chip] = both.astype(BF16)


def up_kernel(lhs_ref, interp_ref, angle_ref, box_ref, mat_ref):
    cosine, sine = jnp.cos(angle_ref[...]), jnp.sin(angle_ref[...])
    for chip in range(box_ref.shape[0]):
        cols = slice(chip * LANES, (chip + 1) * LANES)
        to_real = slice(2 * chip * LANES, (2 * chip + 1) * LANES)
        to_imag = slice((2 * chip + 1) * LANES, (2 * chip + 2) * LANES)
        weights = interp_ref[:, cols].astype(F32)
        for i in range(CHILDREN):
            from_real = slice(2 * i * K0, (2 * i + 1) * K0)
            from_imag = slice((2 * i + 1) * K0, (2 * i + 2) * K0)
            even, odd = weights * cosine[i : i + 1, cols], weights * sine[i : i + 1, cols]
            mat_ref[from_real, to_real] = even.astype(BF16)
            mat_ref[from_real, to_imag] = odd.astype(BF16)
            mat_ref[from_imag, to_real] = (-odd).astype(BF16)
            mat_ref[from_imag, to_imag] = even.astype(BF16)
    put_patterns(box_ref, jnp.dot(lhs_ref[...], mat_ref[...], preferred_element_type=F32))


def again_kernel(lhs_ref, mat_ref, box_ref):
    put_patterns(box_ref, jnp.dot(lhs_ref[...], mat_ref[...], preferred_element_type=F32))


def to_boxes(lhs, interp, angle):
    rows = lhs.shape[0]
    steps = 2
    chips = CHIPS // steps
    return pl.pallas_call(
        up_kernel,
        grid=(steps,),
        in_specs=[
            pl.BlockSpec((rows, DEPTH), lambda s: (0, 0)),
            pl.BlockSpec((K0, chips * LANES), lambda s: (0, s)),
            pl.BlockSpec((CHILDREN, chips * LANES), lambda s: (0, s)),
        ],
        out_specs=[
            pl.BlockSpec((chips, 2 * rows, LANES), lambda s: (s, 0, 0)),
            pl.BlockSpec((DEPTH, 2 * chips * LANES), lambda s: (0, s)),
        ],
        out_shape=[
            jax.ShapeDtypeStruct((CHIPS, 2 * rows, LANES), BF16),
            jax.ShapeDtypeStruct((DEPTH, 2 * K1), BF16),
        ],
        compiler_params=ROOM,
        cost_estimate=cost(1),
        name="to_boxes",
    )(lhs, interp, angle)


def to_boxes_again(lhs, matrix):
    rows = lhs.shape[0]
    steps = 2
    chips = CHIPS // steps
    return pl.pallas_call(
        again_kernel,
        grid=(steps,),
        in_specs=[
            pl.BlockSpec((rows, DEPTH), lambda s: (0, 0)),
            pl.BlockSpec((DEPTH, 2 * chips * LANES), lambda s: (0, s)),
        ],
        out_specs=pl.BlockSpec((chips, 2 * rows, LANES), lambda s: (s, 0, 0)),
        out_shape=jax.ShapeDtypeStruct((CHIPS, 2 * rows, LANES), BF16),
        compiler_params=LESS,
        cost_estimate=cost(6),
        name="to_boxes_again",
    )(lhs, matrix)


def translate_kernel(list_ref, oper_ref, one_ref, two_ref, three_ref, four_ref, out_ref, box_ref, table_ref, sems, *, group):
    step = pl.program_id(0)
    per_step = out_ref.shape[0]

    @pl.when(step == 0)
    def fetch():
        copies = []
        for at, source in enumerate((one_ref, two_ref, three_ref, four_ref)):
            boxes = source.shape[0]
            copies.append(pltpu.make_async_copy(source, box_ref.at[pl.ds(at * boxes, boxes)], sems.at[at]))
        for copy in copies:
            copy.start()

        def spread(at, _):
            for part in range(2):
                some = oper_ref[part, pl.ds(pl.multiple_of(at * R, R), R), :]
                for one in range(R):
                    table_ref[at * R + one, part] = jnp.broadcast_to(some[one : one + 1], (R, LANES))
            return 0

        lax.fori_loop(0, oper_ref.shape[1] // R, spread, 0)
        for copy in copies:
            copy.wait()

    def body(at, _):
        first = (step * per_step + at * group) * (2 * IL)
        done = []
        for k in range(group):
            real = imag = None
            for j in range(IL):
                entry = first + k * 2 * IL + j
                tile = box_ref[list_ref[entry]].astype(F32)
                offset = list_ref[entry + IL]
                by_real, by_imag = table_ref[offset, 0], table_ref[offset, 1]
                box_real, box_imag = tile[:R], tile[R:]
                one = by_real * box_real - by_imag * box_imag
                two = by_real * box_imag + by_imag * box_real
                real = one if j == 0 else real + one
                imag = two if j == 0 else imag + two
            done.append(jnp.concatenate([real, imag], axis=0).astype(BF16))
        for k in range(group):
            out_ref[at * group + k] = done[k]
        return 0

    lax.fori_loop(0, per_step // group, body, 0)


def translate(lists, operators, parts):
    targets = lists.shape[0] // (2 * IL)
    boxes = parts[0].shape[0]
    steps = 1
    per_step = targets // steps
    anywhere = pl.BlockSpec(memory_space=pl.ANY)
    return pl.pallas_call(
        functools.partial(translate_kernel, group=8),
        grid_spec=pltpu.PrefetchScalarGridSpec(
            num_scalar_prefetch=1,
            grid=(steps,),
            in_specs=[pl.BlockSpec(operators.shape, lambda s, *_: (0, 0, 0))] + [anywhere] * 4,
            out_specs=pl.BlockSpec((per_step, 2 * R, LANES), lambda s, *_: (s, 0, 0)),
            scratch_shapes=[
                pltpu.VMEM((4 * boxes, 2 * R, LANES), BF16),
                pltpu.VMEM((operators.shape[1], 2, R, LANES), F32),
                pltpu.SemaphoreType.DMA((4,)),
            ],
        ),
        out_shape=jax.ShapeDtypeStruct((targets, 2 * R, LANES), BF16),
        compiler_params=LESS,
        cost_estimate=cost(25),
        name="translate",
    )(lists, operators, *parts)


def near_kernel(idx_ref, below_ref, own_ref, above_ref, blocks_ref, out_ref, table_ref, lhs_ref):
    step = pl.program_id(0)
    width = own_ref.shape[2]
    per_source = width // LANES
    clusters = blocks_ref.shape[1] // U
    per_tile = LANES // U
    place = lax.broadcasted_iota(jnp.int32, (2 * R, LANES), 1) // U

    @pl.when(step == 0)
    def fill():
        unrolled = 4
        for at, source in enumerate((below_ref, own_ref, above_ref)):

            def body(some, _):
                for one in range(unrolled):
                    tile = some * unrolled + one
                    cols = pl.ds(pl.multiple_of(tile * LANES, LANES), LANES)
                    parts = [source[0, :, cols].astype(F32), source[1, :, cols].astype(F32)]
                    whole = jnp.concatenate(parts, axis=0)
                    turned = [whole] + [pltpu.roll(whole, n * U, 1) for n in range(1, per_tile)]
                    for a in range(per_tile):
                        copied = turned[(0 - a) % per_tile]
                        for g in range(1, per_tile):
                            copied = jnp.where(place == g, turned[(g - a) % per_tile], copied)
                        table_ref[(at * per_source + tile) * per_tile + a] = copied
                return 0

            lax.fori_loop(0, per_source // unrolled, body, 0)
        table_ref[3 * per_source * per_tile] = jnp.zeros((2 * R, LANES), F32)

    def body(some, _):
        for one in range(CHILDREN):
            c = some * CHILDREN + one
            entry = (step * clusters + c) * NBR
            for half in range(NBR // per_tile):
                joined = table_ref[idx_ref[entry + half * per_tile]]
                for k in range(1, per_tile):
                    joined = jnp.where(place == k, table_ref[idx_ref[entry + half * per_tile + k]], joined)
                first = pl.multiple_of(c * 2 * R, 2 * R)
                lhs_ref[pl.ds(first, 2 * R), half * LANES : (half + 1) * LANES] = joined.astype(BF16)
        return 0

    lax.fori_loop(0, clusters // CHILDREN, body, 0)
    for box in range(clusters // CHILDREN):
        rows = slice(box * 2 * R * CHILDREN, (box + 1) * 2 * R * CHILDREN)
        cols = slice(box * WIDE, (box + 1) * WIDE)
        by_real = times_transposed(lhs_ref[rows, :], blocks_ref[0, cols, :])
        by_imag = times_transposed(lhs_ref[rows, :], blocks_ref[1, cols, :])
        real = []
        imag = []
        for i in range(CHILDREN):
            top = slice(2 * R * i, 2 * R * i + R)
            bottom = slice(2 * R * i + R, 2 * R * (i + 1))
            real.append(by_real[top] - by_imag[bottom])
            imag.append(by_imag[top] + by_real[bottom])
        out_ref[0, :, cols] = own_columns(real)
        out_ref[1, :, cols] = own_columns(imag)


def near_part(index, below, own, above, blocks):
    width = own.shape[2]
    steps = 4
    per_step = width // steps
    whole = pl.BlockSpec((2, R, width), lambda s, *_: (0, 0, 0))
    return pl.pallas_call(
        near_kernel,
        grid_spec=pltpu.PrefetchScalarGridSpec(
            num_scalar_prefetch=1,
            grid=(steps,),
            in_specs=[whole, whole, whole, pl.BlockSpec((2, per_step, NBR * U), lambda s, *_: (0, s, 0))],
            out_specs=pl.BlockSpec((2, R, per_step), lambda s, *_: (0, 0, s)),
            scratch_shapes=[
                pltpu.VMEM((3 * width // U + 1, 2 * R, LANES), F32),
                pltpu.VMEM((per_step // U * 2 * R, NBR * U), BF16),
            ],
        ),
        out_shape=jax.ShapeDtypeStruct((2, R, width), F32),
        compiler_params=ROOM,
        cost_estimate=cost(1),
        name="near_part",
    )(index, below, own, above, blocks)


def down_kernel(got_ref, mat_ref, out_ref, sum_ref):
    step = pl.program_id(0)
    last = pl.num_programs(0) - 1
    pieces = []
    for chip in range(got_ref.shape[0]):
        both = got_ref[chip].astype(F32).reshape(-1, 2, R, LANES)
        pieces += [both[:, 0].reshape(-1, LANES), both[:, 1].reshape(-1, LANES)]
    added = times_transposed(jnp.concatenate(pieces, axis=1).astype(BF16), mat_ref[...])

    @pl.when(step == 0)
    def begin():
        sum_ref[...] = added

    @pl.when(jnp.logical_and(step > 0, step < last))
    def go_on():
        sum_ref[...] += added

    @pl.when(step == last)
    def end():
        out_ref[...] = (sum_ref[...] + added).astype(BF16)


def from_boxes(received, matrix):
    rows = received.shape[1] // 2
    steps = 2
    chips = CHIPS // steps
    return pl.pallas_call(
        down_kernel,
        grid=(steps,),
        in_specs=[
            pl.BlockSpec((chips, 2 * rows, LANES), lambda s: (s, 0, 0)),
            pl.BlockSpec((DEPTH, 2 * chips * LANES), lambda s: (0, s)),
        ],
        out_specs=pl.BlockSpec((rows, DEPTH), lambda s: (0, 0)),
        out_shape=jax.ShapeDtypeStruct((rows, DEPTH), BF16),
        scratch_shapes=[pltpu.VMEM((rows, DEPTH), F32)],
        compiler_params=LESS,
        cost_estimate=cost(1),
        name="from_boxes",
    )(received, matrix)


def far_kernel(hi_ref, own_ref, other_ref, rad_ref, near_ref, out_ref):
    low_half = hi_ref[0] == 0
    boxes = out_ref.shape[2] // WIDE
    low = low_lanes(2 * R)
    for pair in range(boxes // 2):
        rows = slice(pair * 2 * R, (pair + 1) * 2 * R)
        pieces = [[], []]
        for i in range(CHILDREN):
            cols = slice(i * LANES, (i + 1) * LANES)
            own, other = own_ref[rows, cols].astype(F32), other_ref[rows, cols].astype(F32)
            zero, one = jnp.where(low_half, own, other), jnp.where(low_half, other, own)
            real = jnp.where(low, zero, swap_halves(one))
            imag = jnp.where(low, swap_halves(zero), one)
            for k in range(2):
                part = slice(k * R, (k + 1) * R)
                pieces[k].append(jnp.concatenate([real[part], imag[part]], axis=1))
                pieces[k].append(jnp.concatenate([imag[part], -real[part]], axis=1))
        for k in range(2):
            fields = jnp.concatenate(pieces[k], axis=0).astype(BF16)
            cols = slice((2 * pair + k) * WIDE, (2 * pair + k + 1) * WIDE)
            slab = jnp.concatenate([rad_ref[0, cols, :], rad_ref[1, cols, :]], axis=1)
            terms = times_transposed(fields, slab)
            for part in range(2):
                own = [terms[2 * R * i + part * R : 2 * R * i + (part + 1) * R] for i in range(CHILDREN)]
                out_ref[part, :, cols] = near_ref[part, :, cols] + own_columns(own)


def far_part(hi, own, other, radiation, near_field):
    width = near_field.shape[2]
    rows = own.shape[0]
    steps = 2
    per_step = width // steps
    field = pl.BlockSpec((rows // steps, DEPTH), lambda s, *_: (s, 0))
    wave = pl.BlockSpec((2, R, per_step), lambda s, *_: (0, 0, s))
    return pl.pallas_call(
        far_kernel,
        grid_spec=pltpu.PrefetchScalarGridSpec(
            num_scalar_prefetch=1,
            grid=(steps,),
            in_specs=[field, field, pl.BlockSpec((2, per_step, LANES), lambda s, *_: (0, s, 0)), wave],
            out_specs=wave,
        ),
        out_shape=jax.ShapeDtypeStruct((2, R, width), F32),
        compiler_params=LESS,
        cost_estimate=cost(1),
        name="far_part",
    )(hi, own, other, radiation, near_field)


def swapped(array):
    return lax.all_to_all(array, INSIDE, split_axis=0, concat_axis=0, tiled=True)


def padded(array):
    return jnp.pad(array, [(0, 0)] * (array.ndim - 1) + [(0, LANES - array.shape[-1])])


def to_owners(boxes, samples):
    rows = boxes.shape[1]
    if samples != LANES:
        boxes = boxes.reshape(CHIPS, rows, LANES // samples, samples).transpose(0, 2, 1, 3).reshape(-1, rows, samples)
    got = swapped(boxes)
    if samples != LANES:
        got = padded(got)
    return got.reshape(-1, 2 * R, LANES)


def from_owners(fields, rows, samples):
    fields = fields.reshape(-1, rows, LANES)
    if samples == LANES:
        return swapped(fields)
    got = swapped(fields[..., :samples]).reshape(CHIPS, LANES // samples, rows, samples)
    return got.transpose(0, 2, 1, 3).reshape(CHIPS, rows, LANES)


def operator_table(translation):
    groups, mids = lax.axis_size("grp"), lax.axis_size("mid")
    core = lax.axis_index("core")
    pairs = [
        (((h * groups + g) * mids + m) * 2 + c, ((g * 2 + h) * mids + m) * 2 + c)
        for g in range(groups)
        for h in range(2)
        for m in range(mids)
        for c in range(2)
    ]
    mine = lax.ppermute(jnp.swapaxes(translation, 1, 2), ALL, pairs)
    other = across(mine, "core").astype(F32)
    mine = mine.astype(F32)
    low = jnp.where(core == 0, mine, other)
    high = jnp.where(core == 0, other, mine)
    operator = padded(jnp.swapaxes(jnp.concatenate([low, high], axis=1), 1, 2))
    return jnp.pad(operator, ((0, 0), (0, -operator.shape[1] % R), (0, 0)))


def target_lists(trans_box, trans_off, hi, core):
    groups, mids = lax.axis_size("grp"), lax.axis_size("mid")
    total = trans_box.shape[0]
    per = total // (groups * mids * 4)
    device, inside = trans_box // per, trans_box % per
    group, side = device // (4 * mids), device // (2 * mids) % 2
    mid, its_core = device // 2 % mids, device % 2
    block = (side ^ hi) * 2 + (its_core ^ core)
    place = (block * (groups * mids) + group * mids + mid) * per + inside
    lists = jnp.concatenate([place, trans_off], axis=1).reshape(groups, 2, mids, 2, per, 2 * IL)
    lists = jnp.where(core == 0, lists[:, :, :, 0], lists[:, :, :, 1])
    first, second = lists[:, 0].reshape(-1), lists[:, 1].reshape(-1)
    return jnp.where(hi == 0, first, second), jnp.where(hi == 0, second, first)


def local(
    currents,
    near_blocks,
    near_list,
    near_count,
    radiation,
    interp,
    shift_angle,
    translation,
    trans_box,
    trans_off,
):
    clusters = near_list.shape[0]
    samples = 2 * translation.shape[2]
    rows = clusters // CHILDREN * 2 * R
    hi, core = lax.axis_index("hi"), lax.axis_index("core")
    side = hi.reshape(1).astype(jnp.int32)
    radiation = radiation.reshape(2, clusters * U, LANES)
    near_blocks = near_blocks.reshape(2, clusters * U, NBR * U)

    first = (lax.axis_index(ALL) - 1) * clusters
    live = jnp.arange(NBR, dtype=jnp.int32)[None, :] < near_count[:, None]
    index = jnp.where(live, near_list - first, 3 * clusters).reshape(-1)
    lists = target_lists(trans_box, trans_off, hi, core)

    leaf_own, leaf_other = leaves(side, currents, radiation)
    leaf_partner = across(leaf_other, "hi")
    boxes_own, matrix = to_boxes(leaf_own, interp, shift_angle)
    rows_own = to_owners(boxes_own, samples)
    swapped_own = across(rows_own, "core")
    operators = operator_table(translation)
    below, above = neighbours(currents)
    leaf_partner, lists, index, operators, below, above = lax.optimization_barrier(
        (leaf_partner, lists, index, operators, below, above)
    )
    rows_partner = to_owners(to_boxes_again(leaf_partner, matrix), samples)
    parts = (rows_own, swapped_own, rows_partner, across(rows_partner, "core"))

    fields_partner = translate(lists[1], operators, parts)
    down_partner = from_boxes(from_owners(fields_partner, rows, samples), matrix)
    fields_own = translate(lists[0], operators, parts)
    down_partner, index = lax.optimization_barrier((down_partner, index))
    down_other = across(down_partner, "hi")
    near_field = near_part(index, below, currents, above, near_blocks)
    down_own = from_boxes(from_owners(fields_own, rows, samples), matrix)
    return far_part(side, down_own, down_other, radiation, near_field)


def solution(mesh):
    devices = mesh.devices
    groups, rest = devices.shape
    cut = Mesh(devices.reshape(groups, 2, rest // 4, 2), ALL)
    placed = (
        P(None, None, ALL),
        P(None, ALL, None, None),
        P(ALL, None),
        P(ALL),
        P(None, ALL, None, None),
        P(),
        P(),
        P(None, None, ALL),
        P(),
        P(),
    )
    return jax.shard_map(local, mesh=cut, in_specs=placed, out_specs=P(None, None, ALL), check_vma=False)
```

```python
import functools

import jax
import jax.numpy as jnp
from jax import lax
from jax.experimental import pallas as pl
from jax.experimental.pallas import tpu as pltpu
from jax.sharding import Mesh
from jax.sharding import PartitionSpec as P

R = 8
U = 32
NBR = 8
K0 = 64
K1 = 1024
IL = 12
CHILDREN = 8
WIDE = CHILDREN * U
LANES = 128
HALF = 64
CHIPS = K1 // LANES
DEPTH = 2 * CHILDREN * K0
ALL = ("grp", "hi", "mid", "core")
INSIDE = ("grp", "mid")
F32 = jnp.float32
BF16 = jnp.bfloat16
ROOM = pltpu.CompilerParams(vmem_limit_bytes=58 * 2**20)
LESS = pltpu.CompilerParams(vmem_limit_bytes=28 * 2**20)


def cost(megabytes):
    return pl.CostEstimate(flops=10**6, bytes_accessed=megabytes * 10**6, transcendentals=0)


def neighbours(array):
    size = lax.axis_size(ALL)
    pairs = [(i, i + 1) for i in range(1, size - 1, 2)] + [(i + 1, i) for i in range(1, size - 1, 2)]
    outside = lax.ppermute(array, ALL, pairs)
    inside = across(array, "core")
    first = lax.axis_index("core") == 0
    return jnp.where(first, outside, inside), jnp.where(first, inside, outside)


def across(array, axis):
    return lax.ppermute(array, axis, [(0, 1), (1, 0)])


def swap_halves(array):
    return pltpu.roll(array, HALF, 1)


def low_lanes(rows):
    return lax.broadcasted_iota(jnp.int32, (rows, LANES), 1) < HALF


def times_transposed(left, right):
    return lax.dot_general(left, right, (((1,), (1,)), ((), ())), preferred_element_type=F32)


def own_columns(pieces):
    child = lax.broadcasted_iota(jnp.int32, (R, WIDE), 1) // U
    picked = pieces[0]
    for i in range(1, CHILDREN):
        picked = jnp.where(child == i, pieces[i], picked)
    return picked


def leaf_kernel(hi_ref, cur_ref, rad_ref, own_ref, other_ref):
    low_half = hi_ref[0] == 0
    boxes = cur_ref.shape[2] // WIDE
    low = low_lanes(2 * R)
    row_child = lax.broadcasted_iota(jnp.int32, (2 * R * CHILDREN, WIDE), 0) // (2 * R)
    col_child = lax.broadcasted_iota(jnp.int32, (2 * R * CHILDREN, WIDE), 1) // U
    diagonal = row_child == col_child
    for pair in range(boxes // 2):
        found = []
        for box in (2 * pair, 2 * pair + 1):
            cols = slice(box * WIDE, (box + 1) * WIDE)
            own = [cur_ref[0, :, cols].astype(F32), cur_ref[1, :, cols].astype(F32)]
            spread = jnp.where(diagonal, jnp.concatenate(own * CHILDREN, axis=0), 0.0)
            slab = jnp.concatenate([rad_ref[0, cols, :], rad_ref[1, cols, :]], axis=1)
            found.append(jnp.dot(spread.astype(BF16), slab, preferred_element_type=F32))
        for i in range(CHILDREN):
            by_real = jnp.concatenate([f[2 * R * i : 2 * R * i + R] for f in found], axis=0)
            by_imag = jnp.concatenate([f[2 * R * i + R : 2 * R * (i + 1)] for f in found], axis=0)
            real = by_real[:, :LANES] - by_imag[:, LANES:]
            imag = by_real[:, LANES:] + by_imag[:, :LANES]
            zero = jnp.where(low, real, swap_halves(imag))
            one = jnp.where(low, swap_halves(real), imag)
            rows = slice(pair * 2 * R, (pair + 1) * 2 * R)
            cols = slice(i * LANES, (i + 1) * LANES)
            own_ref[rows, cols] = jnp.where(low_half, zero, one).astype(BF16)
            other_ref[rows, cols] = jnp.where(low_half, one, zero).astype(BF16)


def leaves(hi, currents, radiation):
    width = currents.shape[2]
    rows = width // WIDE * R
    steps = 2
    per_step = width // steps
    shape = jax.ShapeDtypeStruct((rows, DEPTH), BF16)
    spec = pl.BlockSpec((rows // steps, DEPTH), lambda s, *_: (s, 0))
    return pl.pallas_call(
        leaf_kernel,
        grid_spec=pltpu.PrefetchScalarGridSpec(
            num_scalar_prefetch=1,
            grid=(steps,),
            in_specs=[
                pl.BlockSpec((2, R, per_step), lambda s, *_: (0, 0, s)),
                pl.BlockSpec((2, per_step, LANES), lambda s, *_: (0, s, 0)),
            ],
            out_specs=[spec, spec],
        ),
        out_shape=[shape, shape],
        compiler_params=ROOM,
        cost_estimate=cost(1),
        name="leaves",
    )(hi, currents, radiation)


def put_patterns(box_ref, patterns):
    boxes = patterns.shape[0] // R
    for chip in range(box_ref.shape[0]):
        real = patterns[:, 2 * chip * LANES : (2 * chip + 1) * LANES].reshape(boxes, 1, R, LANES)
        imag = patterns[:, (2 * chip + 1) * LANES : (2 * chip + 2) * LANES].reshape(boxes, 1, R, LANES)
        both = jnp.concatenate([real, imag], axis=1).reshape(boxes * 2 * R, LANES)
        box_ref[chip] = both.astype(BF16)


def up_kernel(lhs_ref, interp_ref, angle_ref, box_ref, mat_ref):
    cosine, sine = jnp.cos(angle_ref[...]), jnp.sin(angle_ref[...])
    for chip in range(box_ref.shape[0]):
        cols = slice(chip * LANES, (chip + 1) * LANES)
        to_real = slice(2 * chip * LANES, (2 * chip + 1) * LANES)
        to_imag = slice((2 * chip + 1) * LANES, (2 * chip + 2) * LANES)
        weights = interp_ref[:, cols].astype(F32)
        for i in range(CHILDREN):
            from_real = slice(2 * i * K0, (2 * i + 1) * K0)
            from_imag = slice((2 * i + 1) * K0, (2 * i + 2) * K0)
            even, odd = weights * cosine[i : i + 1, cols], weights * sine[i : i + 1, cols]
            mat_ref[from_real, to_real] = even.astype(BF16)
            mat_ref[from_real, to_imag] = odd.astype(BF16)
            mat_ref[from_imag, to_real] = (-odd).astype(BF16)
            mat_ref[from_imag, to_imag] = even.astype(BF16)
    put_patterns(box_ref, jnp.dot(lhs_ref[...], mat_ref[...], preferred_element_type=F32))


def again_kernel(lhs_ref, mat_ref, box_ref):
    put_patterns(box_ref, jnp.dot(lhs_ref[...], mat_ref[...], preferred_element_type=F32))


def to_boxes(lhs, interp, angle):
    rows = lhs.shape[0]
    steps = 2
    chips = CHIPS // steps
    return pl.pallas_call(
        up_kernel,
        grid=(steps,),
        in_specs=[
            pl.BlockSpec((rows, DEPTH), lambda s: (0, 0)),
            pl.BlockSpec((K0, chips * LANES), lambda s: (0, s)),
            pl.BlockSpec((CHILDREN, chips * LANES), lambda s: (0, s)),
        ],
        out_specs=[
            pl.BlockSpec((chips, 2 * rows, LANES), lambda s: (s, 0, 0)),
            pl.BlockSpec((DEPTH, 2 * chips * LANES), lambda s: (0, s)),
        ],
        out_shape=[
            jax.ShapeDtypeStruct((CHIPS, 2 * rows, LANES), BF16),
            jax.ShapeDtypeStruct((DEPTH, 2 * K1), BF16),
        ],
        compiler_params=ROOM,
        cost_estimate=cost(1),
        name="to_boxes",
    )(lhs, interp, angle)


def to_boxes_again(lhs, matrix):
    rows = lhs.shape[0]
    steps = 1
    chips = CHIPS // steps
    return pl.pallas_call(
        again_kernel,
        grid=(steps,),
        in_specs=[
            pl.BlockSpec((rows, DEPTH), lambda s: (0, 0)),
            pl.BlockSpec((DEPTH, 2 * chips * LANES), lambda s: (0, s)),
        ],
        out_specs=pl.BlockSpec((chips, 2 * rows, LANES), lambda s: (s, 0, 0)),
        out_shape=jax.ShapeDtypeStruct((CHIPS, 2 * rows, LANES), BF16),
        compiler_params=LESS,
        cost_estimate=cost(6),
        name="to_boxes_again",
    )(lhs, matrix)


def translate_kernel(list_ref, oper_ref, one_ref, two_ref, three_ref, four_ref, out_ref, box_ref, table_ref, sems, *, group):
    step = pl.program_id(0)
    per_step = out_ref.shape[0]

    @pl.when(step == 0)
    def fetch():
        copies = []
        for at, source in enumerate((one_ref, two_ref, three_ref, four_ref)):
            boxes = source.shape[0]
            copies.append(pltpu.make_async_copy(source, box_ref.at[pl.ds(at * boxes, boxes)], sems.at[at]))
        for copy in copies:
            copy.start()

        def spread(at, _):
            for part in range(2):
                some = oper_ref[part, pl.ds(pl.multiple_of(at * R, R), R), :]
                for one in range(R):
                    table_ref[at * R + one, part] = jnp.broadcast_to(some[one : one + 1], (R, LANES))
            return 0

        lax.fori_loop(0, oper_ref.shape[1] // R, spread, 0)
        for copy in copies:
            copy.wait()

    def body(at, _):
        first = (step * per_step + at * group) * (2 * IL)
        done = []
        for k in range(group):
            real = imag = None
            for j in range(IL):
                entry = first + k * 2 * IL + j
                tile = box_ref[list_ref[entry]].astype(F32)
                offset = list_ref[entry + IL]
                by_real, by_imag = table_ref[offset, 0], table_ref[offset, 1]
                box_real, box_imag = tile[:R], tile[R:]
                one = by_real * box_real - by_imag * box_imag
                two = by_real * box_imag + by_imag * box_real
                real = one if j == 0 else real + one
                imag = two if j == 0 else imag + two
            done.append(jnp.concatenate([real, imag], axis=0).astype(BF16))
        for k in range(group):
            out_ref[at * group + k] = done[k]
        return 0

    lax.fori_loop(0, per_step // group, body, 0)


def translate(lists, operators, parts):
    targets = lists.shape[0] // (2 * IL)
    boxes = parts[0].shape[0]
    steps = 1
    per_step = targets // steps
    anywhere = pl.BlockSpec(memory_space=pl.ANY)
    return pl.pallas_call(
        functools.partial(translate_kernel, group=16),
        grid_spec=pltpu.PrefetchScalarGridSpec(
            num_scalar_prefetch=1,
            grid=(steps,),
            in_specs=[pl.BlockSpec(operators.shape, lambda s, *_: (0, 0, 0))] + [anywhere] * 4,
            out_specs=pl.BlockSpec((per_step, 2 * R, LANES), lambda s, *_: (s, 0, 0)),
            scratch_shapes=[
                pltpu.VMEM((4 * boxes, 2 * R, LANES), BF16),
                pltpu.VMEM((operators.shape[1], 2, R, LANES), F32),
                pltpu.SemaphoreType.DMA((4,)),
            ],
        ),
        out_shape=jax.ShapeDtypeStruct((targets, 2 * R, LANES), BF16),
        compiler_params=LESS,
        cost_estimate=cost(25),
        name="translate",
    )(lists, operators, *parts)


def near_kernel(idx_ref, below_ref, own_ref, above_ref, blocks_ref, out_ref, table_ref, lhs_ref):
    step = pl.program_id(0)
    width = own_ref.shape[2]
    per_source = width // LANES
    clusters = blocks_ref.shape[1] // U
    per_tile = LANES // U
    place = lax.broadcasted_iota(jnp.int32, (2 * R, LANES), 1) // U

    @pl.when(step == 0)
    def fill():
        unrolled = 4
        for at, source in enumerate((below_ref, own_ref, above_ref)):

            def body(some, _):
                for one in range(unrolled):
                    tile = some * unrolled + one
                    cols = pl.ds(pl.multiple_of(tile * LANES, LANES), LANES)
                    parts = [source[0, :, cols].astype(F32), source[1, :, cols].astype(F32)]
                    whole = jnp.concatenate(parts, axis=0)
                    turned = [whole] + [pltpu.roll(whole, n * U, 1) for n in range(1, per_tile)]
                    for a in range(per_tile):
                        copied = turned[(0 - a) % per_tile]
                        for g in range(1, per_tile):
                            copied = jnp.where(place == g, turned[(g - a) % per_tile], copied)
                        table_ref[(at * per_source + tile) * per_tile + a] = copied
                return 0

            lax.fori_loop(0, per_source // unrolled, body, 0)
        table_ref[3 * per_source * per_tile] = jnp.zeros((2 * R, LANES), F32)

    def body(some, _):
        for one in range(CHILDREN):
            c = some * CHILDREN + one
            entry = (step * clusters + c) * NBR
            for half in range(NBR // per_tile):
                joined = table_ref[idx_ref[entry + half * per_tile]]
                for k in range(1, per_tile):
                    joined = jnp.where(place == k, table_ref[idx_ref[entry + half * per_tile + k]], joined)
                first = pl.multiple_of(c * 2 * R, 2 * R)
                lhs_ref[pl.ds(first, 2 * R), half * LANES : (half + 1) * LANES] = joined.astype(BF16)
        return 0

    lax.fori_loop(0, clusters // CHILDREN, body, 0)
    for box in range(clusters // CHILDREN):
        rows = slice(box * 2 * R * CHILDREN, (box + 1) * 2 * R * CHILDREN)
        cols = slice(box * WIDE, (box + 1) * WIDE)
        by_real = times_transposed(lhs_ref[rows, :], blocks_ref[0, cols, :])
        by_imag = times_transposed(lhs_ref[rows, :], blocks_ref[1, cols, :])
        real = []
        imag = []
        for i in range(CHILDREN):
            top = slice(2 * R * i, 2 * R * i + R)
            bottom = slice(2 * R * i + R, 2 * R * (i + 1))
            real.append(by_real[top] - by_imag[bottom])
            imag.append(by_imag[top] + by_real[bottom])
        out_ref[0, :, cols] = own_columns(real)
        out_ref[1, :, cols] = own_columns(imag)


def near_part(index, below, own, above, blocks):
    width = own.shape[2]
    steps = 2
    per_step = width // steps
    whole = pl.BlockSpec((2, R, width), lambda s, *_: (0, 0, 0))
    return pl.pallas_call(
        near_kernel,
        grid_spec=pltpu.PrefetchScalarGridSpec(
            num_scalar_prefetch=1,
            grid=(steps,),
            in_specs=[whole, whole, whole, pl.BlockSpec((2, per_step, NBR * U), lambda s, *_: (0, s, 0))],
            out_specs=pl.BlockSpec((2, R, per_step), lambda s, *_: (0, 0, s)),
            scratch_shapes=[
                pltpu.VMEM((3 * width // U + 1, 2 * R, LANES), F32),
                pltpu.VMEM((per_step // U * 2 * R, NBR * U), BF16),
            ],
        ),
        out_shape=jax.ShapeDtypeStruct((2, R, width), F32),
        compiler_params=ROOM,
        cost_estimate=cost(1),
        name="near_part",
    )(index, below, own, above, blocks)


def down_kernel(got_ref, mat_ref, out_ref):
    pieces = []
    for chip in range(got_ref.shape[0]):
        both = got_ref[chip].astype(F32).reshape(-1, 2, R, LANES)
        pieces += [both[:, 0].reshape(-1, LANES), both[:, 1].reshape(-1, LANES)]
    fields = jnp.concatenate(pieces, axis=1).astype(BF16)
    out_ref[...] = times_transposed(fields, mat_ref[...]).astype(BF16)


def from_boxes(received, matrix):
    rows = received.shape[1] // 2
    steps = 1
    chips = CHIPS // steps
    return pl.pallas_call(
        down_kernel,
        grid=(steps,),
        in_specs=[
            pl.BlockSpec((chips, 2 * rows, LANES), lambda s: (s, 0, 0)),
            pl.BlockSpec((DEPTH, 2 * chips * LANES), lambda s: (0, s)),
        ],
        out_specs=pl.BlockSpec((rows, DEPTH), lambda s: (0, 0)),
        out_shape=jax.ShapeDtypeStruct((rows, DEPTH), BF16),
        compiler_params=LESS,
        cost_estimate=cost(1),
        name="from_boxes",
    )(received, matrix)


def far_kernel(hi_ref, own_ref, other_ref, rad_ref, near_ref, out_ref):
    low_half = hi_ref[0] == 0
    boxes = out_ref.shape[2] // WIDE
    low = low_lanes(2 * R)
    for pair in range(boxes // 2):
        rows = slice(pair * 2 * R, (pair + 1) * 2 * R)
        pieces = [[], []]
        for i in range(CHILDREN):
            cols = slice(i * LANES, (i + 1) * LANES)
            own, other = own_ref[rows, cols].astype(F32), other_ref[rows, cols].astype(F32)
            zero, one = jnp.where(low_half, own, other), jnp.where(low_half, other, own)
            real = jnp.where(low, zero, swap_halves(one))
            imag = jnp.where(low, swap_halves(zero), one)
            for k in range(2):
                part = slice(k * R, (k + 1) * R)
                pieces[k].append(jnp.concatenate([real[part], imag[part]], axis=1))
                pieces[k].append(jnp.concatenate([imag[part], -real[part]], axis=1))
        for k in range(2):
            fields = jnp.concatenate(pieces[k], axis=0).astype(BF16)
            cols = slice((2 * pair + k) * WIDE, (2 * pair + k + 1) * WIDE)
            slab = jnp.concatenate([rad_ref[0, cols, :], rad_ref[1, cols, :]], axis=1)
            terms = times_transposed(fields, slab)
            for part in range(2):
                own = [terms[2 * R * i + part * R : 2 * R * i + (part + 1) * R] for i in range(CHILDREN)]
                out_ref[part, :, cols] = near_ref[part, :, cols] + own_columns(own)


def far_part(hi, own, other, radiation, near_field):
    width = near_field.shape[2]
    rows = own.shape[0]
    steps = 2
    per_step = width // steps
    field = pl.BlockSpec((rows // steps, DEPTH), lambda s, *_: (s, 0))
    wave = pl.BlockSpec((2, R, per_step), lambda s, *_: (0, 0, s))
    return pl.pallas_call(
        far_kernel,
        grid_spec=pltpu.PrefetchScalarGridSpec(
            num_scalar_prefetch=1,
            grid=(steps,),
            in_specs=[field, field, pl.BlockSpec((2, per_step, LANES), lambda s, *_: (0, s, 0)), wave],
            out_specs=wave,
        ),
        out_shape=jax.ShapeDtypeStruct((2, R, width), F32),
        compiler_params=LESS,
        cost_estimate=cost(1),
        name="far_part",
    )(hi, own, other, radiation, near_field)


def swapped(array):
    return lax.all_to_all(array, INSIDE, split_axis=0, concat_axis=0, tiled=True)


def padded(array):
    return jnp.pad(array, [(0, 0)] * (array.ndim - 1) + [(0, LANES - array.shape[-1])])


def to_owners(boxes, samples):
    rows = boxes.shape[1]
    if samples != LANES:
        boxes = boxes.reshape(CHIPS, rows, LANES // samples, samples).transpose(0, 2, 1, 3).reshape(-1, rows, samples)
    got = swapped(boxes)
    if samples != LANES:
        got = padded(got)
    return got.reshape(-1, 2 * R, LANES)


def from_owners(fields, rows, samples):
    fields = fields.reshape(-1, rows, LANES)
    if samples == LANES:
        return swapped(fields)
    got = swapped(fields[..., :samples]).reshape(CHIPS, LANES // samples, rows, samples)
    return got.transpose(0, 2, 1, 3).reshape(CHIPS, rows, LANES)


def operator_table(translation):
    groups, mids = lax.axis_size("grp"), lax.axis_size("mid")
    core = lax.axis_index("core")
    pairs = [
        (((h * groups + g) * mids + m) * 2 + c, ((g * 2 + h) * mids + m) * 2 + c)
        for g in range(groups)
        for h in range(2)
        for m in range(mids)
        for c in range(2)
    ]
    mine = lax.ppermute(jnp.swapaxes(translation, 1, 2), ALL, pairs)
    other = across(mine, "core").astype(F32)
    mine = mine.astype(F32)
    low = jnp.where(core == 0, mine, other)
    high = jnp.where(core == 0, other, mine)
    operator = padded(jnp.swapaxes(jnp.concatenate([low, high], axis=1), 1, 2))
    return jnp.pad(operator, ((0, 0), (0, -operator.shape[1] % R), (0, 0)))


def target_lists(trans_box, trans_off, hi, core):
    groups, mids = lax.axis_size("grp"), lax.axis_size("mid")
    total = trans_box.shape[0]
    per = total // (groups * mids * 4)
    device, inside = trans_box // per, trans_box % per
    group, side = device // (4 * mids), device // (2 * mids) % 2
    mid, its_core = device // 2 % mids, device % 2
    block = (side ^ hi) * 2 + (its_core ^ core)
    place = (block * (groups * mids) + group * mids + mid) * per + inside
    lists = jnp.concatenate([place, trans_off], axis=1).reshape(groups, 2, mids, 2, per, 2 * IL)
    lists = jnp.where(core == 0, lists[:, :, :, 0], lists[:, :, :, 1])
    first, second = lists[:, 0].reshape(-1), lists[:, 1].reshape(-1)
    return jnp.where(hi == 0, first, second), jnp.where(hi == 0, second, first)


def local(
    currents,
    near_blocks,
    near_list,
    near_count,
    radiation,
    interp,
    shift_angle,
    translation,
    trans_box,
    trans_off,
):
    clusters = near_list.shape[0]
    samples = 2 * translation.shape[2]
    rows = clusters // CHILDREN * 2 * R
    hi, core = lax.axis_index("hi"), lax.axis_index("core")
    side = hi.reshape(1).astype(jnp.int32)
    radiation = radiation.reshape(2, clusters * U, LANES)
    near_blocks = near_blocks.reshape(2, clusters * U, NBR * U)

    first = (lax.axis_index(ALL) - 1) * clusters
    live = jnp.arange(NBR, dtype=jnp.int32)[None, :] < near_count[:, None]
    index = jnp.where(live, near_list - first, 3 * clusters).reshape(-1)
    lists = target_lists(trans_box, trans_off, hi, core)

    leaf_own, leaf_other = leaves(side, currents, radiation)
    leaf_partner = across(leaf_other, "hi")
    boxes_own, matrix = to_boxes(leaf_own, interp, shift_angle)
    rows_own = to_owners(boxes_own, samples)
    swapped_own = across(rows_own, "core")
    operators = operator_table(translation)
    below, above = neighbours(currents)
    leaf_partner, lists, index, operators, below, above = lax.optimization_barrier(
        (leaf_partner, lists, index, operators, below, above)
    )
    rows_partner = to_owners(to_boxes_again(leaf_partner, matrix), samples)
    parts = (rows_own, swapped_own, rows_partner, across(rows_partner, "core"))

    fields_partner = translate(lists[1], operators, parts)
    down_partner = from_boxes(from_owners(fields_partner, rows, samples), matrix)
    fields_own = translate(lists[0], operators, parts)
    down_partner, index = lax.optimization_barrier((down_partner, index))
    down_other = across(down_partner, "hi")
    near_field = near_part(index, below, currents, above, near_blocks)
    down_own = from_boxes(from_owners(fields_own, rows, samples), matrix)
    return far_part(side, down_own, down_other, radiation, near_field)


def solution(mesh):
    devices = mesh.devices
    groups, rest = devices.shape
    cut = Mesh(devices.reshape(groups, 2, rest // 4, 2), ALL)
    placed = (
        P(None, None, ALL),
        P(None, ALL, None, None),
        P(ALL, None),
        P(ALL),
        P(None, ALL, None, None),
        P(),
        P(),
        P(None, None, ALL),
        P(),
        P(),
    )
    return jax.shard_map(local, mesh=cut, in_specs=placed, out_specs=P(None, None, ALL), check_vma=False)
```

```python
import functools

import jax
import jax.numpy as jnp
from jax import lax
from jax.experimental import pallas as pl
from jax.experimental.pallas import tpu as pltpu
from jax.sharding import Mesh
from jax.sharding import PartitionSpec as P

R = 8
U = 32
NBR = 8
K0 = 64
K1 = 1024
IL = 12
CHILDREN = 8
WIDE = CHILDREN * U
LANES = 128
HALF = 64
CHIPS = K1 // LANES
DEPTH = 2 * CHILDREN * K0
ALL = ("grp", "hi", "mid", "core")
INSIDE = ("grp", "mid")
F32 = jnp.float32
BF16 = jnp.bfloat16
ROOM = pltpu.CompilerParams(vmem_limit_bytes=58 * 2**20)
LESS = pltpu.CompilerParams(vmem_limit_bytes=28 * 2**20)


def cost(megabytes):
    return pl.CostEstimate(flops=10**6, bytes_accessed=megabytes * 10**6, transcendentals=0)


def neighbours(array):
    size = lax.axis_size(ALL)
    pairs = [(i, i + 1) for i in range(1, size - 1, 2)] + [(i + 1, i) for i in range(1, size - 1, 2)]
    outside = lax.ppermute(array, ALL, pairs)
    inside = across(array, "core")
    first = lax.axis_index("core") == 0
    return jnp.where(first, outside, inside), jnp.where(first, inside, outside)


def across(array, axis):
    return lax.ppermute(array, axis, [(0, 1), (1, 0)])


def swap_halves(array):
    return pltpu.roll(array, HALF, 1)


def low_lanes(rows):
    return lax.broadcasted_iota(jnp.int32, (rows, LANES), 1) < HALF


def times_transposed(left, right):
    return lax.dot_general(left, right, (((1,), (1,)), ((), ())), preferred_element_type=F32)


def own_columns(pieces):
    child = lax.broadcasted_iota(jnp.int32, (R, WIDE), 1) // U
    picked = pieces[0]
    for i in range(1, CHILDREN):
        picked = jnp.where(child == i, pieces[i], picked)
    return picked


def leaf_kernel(hi_ref, cur_ref, rad_ref, own_ref, other_ref):
    low_half = hi_ref[0] == 0
    boxes = cur_ref.shape[2] // WIDE
    low = low_lanes(2 * R)
    row_child = lax.broadcasted_iota(jnp.int32, (2 * R * CHILDREN, WIDE), 0) // (2 * R)
    col_child = lax.broadcasted_iota(jnp.int32, (2 * R * CHILDREN, WIDE), 1) // U
    diagonal = row_child == col_child
    for pair in range(boxes // 2):
        found = []
        for box in (2 * pair, 2 * pair + 1):
            cols = slice(box * WIDE, (box + 1) * WIDE)
            own = [cur_ref[0, :, cols].astype(F32), cur_ref[1, :, cols].astype(F32)]
            spread = jnp.where(diagonal, jnp.concatenate(own * CHILDREN, axis=0), 0.0)
            slab = jnp.concatenate([rad_ref[0, cols, :], rad_ref[1, cols, :]], axis=1)
            found.append(jnp.dot(spread.astype(BF16), slab, preferred_element_type=F32))
        for i in range(CHILDREN):
            by_real = jnp.concatenate([f[2 * R * i : 2 * R * i + R] for f in found], axis=0)
            by_imag = jnp.concatenate([f[2 * R * i + R : 2 * R * (i + 1)] for f in found], axis=0)
            real = by_real[:, :LANES] - by_imag[:, LANES:]
            imag = by_real[:, LANES:] + by_imag[:, :LANES]
            zero = jnp.where(low, real, swap_halves(imag))
            one = jnp.where(low, swap_halves(real), imag)
            rows = slice(pair * 2 * R, (pair + 1) * 2 * R)
            cols = slice(i * LANES, (i + 1) * LANES)
            own_ref[rows, cols] = jnp.where(low_half, zero, one).astype(BF16)
            other_ref[rows, cols] = jnp.where(low_half, one, zero).astype(BF16)


def leaves(hi, currents, radiation):
    width = currents.shape[2]
    rows = width // WIDE * R
    steps = 2
    per_step = width // steps
    shape = jax.ShapeDtypeStruct((rows, DEPTH), BF16)
    spec = pl.BlockSpec((rows // steps, DEPTH), lambda s, *_: (s, 0))
    return pl.pallas_call(
        leaf_kernel,
        grid_spec=pltpu.PrefetchScalarGridSpec(
            num_scalar_prefetch=1,
            grid=(steps,),
            in_specs=[
                pl.BlockSpec((2, R, per_step), lambda s, *_: (0, 0, s)),
                pl.BlockSpec((2, per_step, LANES), lambda s, *_: (0, s, 0)),
            ],
            out_specs=[spec, spec],
        ),
        out_shape=[shape, shape],
        compiler_params=ROOM,
        cost_estimate=cost(1),
        name="leaves",
    )(hi, currents, radiation)


def put_patterns(box_ref, patterns):
    boxes = patterns.shape[0] // R
    for chip in range(box_ref.shape[0]):
        real = patterns[:, 2 * chip * LANES : (2 * chip + 1) * LANES].reshape(boxes, 1, R, LANES)
        imag = patterns[:, (2 * chip + 1) * LANES : (2 * chip + 2) * LANES].reshape(boxes, 1, R, LANES)
        both = jnp.concatenate([real, imag], axis=1).reshape(boxes * 2 * R, LANES)
        box_ref[chip] = both.astype(BF16)


def up_kernel(lhs_ref, interp_ref, angle_ref, box_ref, mat_ref):
    cosine, sine = jnp.cos(angle_ref[...]), jnp.sin(angle_ref[...])
    for chip in range(box_ref.shape[0]):
        cols = slice(chip * LANES, (chip + 1) * LANES)
        to_real = slice(2 * chip * LANES, (2 * chip + 1) * LANES)
        to_imag = slice((2 * chip + 1) * LANES, (2 * chip + 2) * LANES)
        weights = interp_ref[:, cols].astype(F32)
        for i in range(CHILDREN):
            from_real = slice(2 * i * K0, (2 * i + 1) * K0)
            from_imag = slice((2 * i + 1) * K0, (2 * i + 2) * K0)
            even, odd = weights * cosine[i : i + 1, cols], weights * sine[i : i + 1, cols]
            mat_ref[from_real, to_real] = even.astype(BF16)
            mat_ref[from_real, to_imag] = odd.astype(BF16)
            mat_ref[from_imag, to_real] = (-odd).astype(BF16)
            mat_ref[from_imag, to_imag] = even.astype(BF16)
    put_patterns(box_ref, jnp.dot(lhs_ref[...], mat_ref[...], preferred_element_type=F32))


def again_kernel(lhs_ref, mat_ref, box_ref):
    put_patterns(box_ref, jnp.dot(lhs_ref[...], mat_ref[...], preferred_element_type=F32))


def to_boxes(lhs, interp, angle):
    rows = lhs.shape[0]
    steps = 2
    chips = CHIPS // steps
    return pl.pallas_call(
        up_kernel,
        grid=(steps,),
        in_specs=[
            pl.BlockSpec((rows, DEPTH), lambda s: (0, 0)),
            pl.BlockSpec((K0, chips * LANES), lambda s: (0, s)),
            pl.BlockSpec((CHILDREN, chips * LANES), lambda s: (0, s)),
        ],
        out_specs=[
            pl.BlockSpec((chips, 2 * rows, LANES), lambda s: (s, 0, 0)),
            pl.BlockSpec((DEPTH, 2 * chips * LANES), lambda s: (0, s)),
        ],
        out_shape=[
            jax.ShapeDtypeStruct((CHIPS, 2 * rows, LANES), BF16),
            jax.ShapeDtypeStruct((DEPTH, 2 * K1), BF16),
        ],
        compiler_params=ROOM,
        cost_estimate=cost(1),
        name="to_boxes",
    )(lhs, interp, angle)


def to_boxes_again(lhs, matrix):
    rows = lhs.shape[0]
    steps = 1
    chips = CHIPS // steps
    return pl.pallas_call(
        again_kernel,
        grid=(steps,),
        in_specs=[
            pl.BlockSpec((rows, DEPTH), lambda s: (0, 0)),
            pl.BlockSpec((DEPTH, 2 * chips * LANES), lambda s: (0, s)),
        ],
        out_specs=pl.BlockSpec((chips, 2 * rows, LANES), lambda s: (s, 0, 0)),
        out_shape=jax.ShapeDtypeStruct((CHIPS, 2 * rows, LANES), BF16),
        compiler_params=LESS,
        cost_estimate=cost(6),
        name="to_boxes_again",
    )(lhs, matrix)


def translate_kernel(list_ref, oper_ref, one_ref, two_ref, three_ref, four_ref, out_ref, box_ref, table_ref, sems, *, group):
    step = pl.program_id(0)
    per_step = out_ref.shape[0]

    @pl.when(step == 0)
    def fetch():
        copies = []
        for at, source in enumerate((one_ref, two_ref, three_ref, four_ref)):
            boxes = source.shape[0]
            copies.append(pltpu.make_async_copy(source, box_ref.at[pl.ds(at * boxes, boxes)], sems.at[at]))
        for copy in copies:
            copy.start()

        def spread(at, _):
            for part in range(2):
                some = oper_ref[part, pl.ds(pl.multiple_of(at * R, R), R), :]
                for one in range(R):
                    table_ref[at * R + one, part] = jnp.broadcast_to(some[one : one + 1], (R, LANES))
            return 0

        lax.fori_loop(0, oper_ref.shape[1] // R, spread, 0)
        for copy in copies:
            copy.wait()

    def body(at, _):
        first = (step * per_step + at * group) * (2 * IL)
        done = []
        for k in range(group):
            real = imag = None
            for j in range(IL):
                entry = first + k * 2 * IL + j
                tile = box_ref[list_ref[entry]].astype(F32)
                offset = list_ref[entry + IL]
                by_real, by_imag = table_ref[offset, 0], table_ref[offset, 1]
                box_real, box_imag = tile[:R], tile[R:]
                one = by_real * box_real - by_imag * box_imag
                two = by_real * box_imag + by_imag * box_real
                real = one if j == 0 else real + one
                imag = two if j == 0 else imag + two
            done.append(jnp.concatenate([real, imag], axis=0).astype(BF16))
        for k in range(group):
            out_ref[at * group + k] = done[k]
        return 0

    lax.fori_loop(0, per_step // group, body, 0)


def translate(lists, operators, parts):
    targets = lists.shape[0] // (2 * IL)
    boxes = parts[0].shape[0]
    steps = 1
    per_step = targets // steps
    anywhere = pl.BlockSpec(memory_space=pl.ANY)
    return pl.pallas_call(
        functools.partial(translate_kernel, group=16),
        grid_spec=pltpu.PrefetchScalarGridSpec(
            num_scalar_prefetch=1,
            grid=(steps,),
            in_specs=[pl.BlockSpec(operators.shape, lambda s, *_: (0, 0, 0))] + [anywhere] * 4,
            out_specs=pl.BlockSpec((per_step, 2 * R, LANES), lambda s, *_: (s, 0, 0)),
            scratch_shapes=[
                pltpu.VMEM((4 * boxes, 2 * R, LANES), BF16),
                pltpu.VMEM((operators.shape[1], 2, R, LANES), F32),
                pltpu.SemaphoreType.DMA((4,)),
            ],
        ),
        out_shape=jax.ShapeDtypeStruct((targets, 2 * R, LANES), BF16),
        compiler_params=LESS,
        cost_estimate=cost(25),
        name="translate",
    )(lists, operators, *parts)


def near_kernel(idx_ref, below_ref, own_ref, above_ref, blocks_ref, out_ref, table_ref, lhs_ref):
    step = pl.program_id(0)
    width = own_ref.shape[2]
    per_source = width // LANES
    clusters = blocks_ref.shape[1] // U
    per_tile = LANES // U
    place = lax.broadcasted_iota(jnp.int32, (2 * R, LANES), 1) // U

    @pl.when(step == 0)
    def fill():
        unrolled = 4
        for at, source in enumerate((below_ref, own_ref, above_ref)):

            def body(some, _):
                for one in range(unrolled):
                    tile = some * unrolled + one
                    cols = pl.ds(pl.multiple_of(tile * LANES, LANES), LANES)
                    parts = [source[0, :, cols].astype(F32), source[1, :, cols].astype(F32)]
                    whole = jnp.concatenate(parts, axis=0)
                    turned = [whole] + [pltpu.roll(whole, n * U, 1) for n in range(1, per_tile)]
                    for a in range(per_tile):
                        copied = turned[(0 - a) % per_tile]
                        for g in range(1, per_tile):
                            copied = jnp.where(place == g, turned[(g - a) % per_tile], copied)
                        table_ref[(at * per_source + tile) * per_tile + a] = copied
                return 0

            lax.fori_loop(0, per_source // unrolled, body, 0)
        table_ref[3 * per_source * per_tile] = jnp.zeros((2 * R, LANES), F32)

    def body(some, _):
        for one in range(CHILDREN):
            c = some * CHILDREN + one
            entry = (step * clusters + c) * NBR
            for half in range(NBR // per_tile):
                joined = table_ref[idx_ref[entry + half * per_tile]]
                for k in range(1, per_tile):
                    joined = jnp.where(place == k, table_ref[idx_ref[entry + half * per_tile + k]], joined)
                first = pl.multiple_of(c * 2 * R, 2 * R)
                lhs_ref[pl.ds(first, 2 * R), half * LANES : (half + 1) * LANES] = joined.astype(BF16)
        return 0

    lax.fori_loop(0, clusters // CHILDREN, body, 0)
    for box in range(clusters // CHILDREN):
        rows = slice(box * 2 * R * CHILDREN, (box + 1) * 2 * R * CHILDREN)
        cols = slice(box * WIDE, (box + 1) * WIDE)
        by_real = times_transposed(lhs_ref[rows, :], blocks_ref[0, cols, :])
        by_imag = times_transposed(lhs_ref[rows, :], blocks_ref[1, cols, :])
        real = []
        imag = []
        for i in range(CHILDREN):
            top = slice(2 * R * i, 2 * R * i + R)
            bottom = slice(2 * R * i + R, 2 * R * (i + 1))
            real.append(by_real[top] - by_imag[bottom])
            imag.append(by_imag[top] + by_real[bottom])
        out_ref[0, :, cols] = own_columns(real)
        out_ref[1, :, cols] = own_columns(imag)


def near_part(index, below, own, above, blocks):
    width = own.shape[2]
    steps = 2
    per_step = width // steps
    whole = pl.BlockSpec((2, R, width), lambda s, *_: (0, 0, 0))
    return pl.pallas_call(
        near_kernel,
        grid_spec=pltpu.PrefetchScalarGridSpec(
            num_scalar_prefetch=1,
            grid=(steps,),
            in_specs=[whole, whole, whole, pl.BlockSpec((2, per_step, NBR * U), lambda s, *_: (0, s, 0))],
            out_specs=pl.BlockSpec((2, R, per_step), lambda s, *_: (0, 0, s)),
            scratch_shapes=[
                pltpu.VMEM((3 * width // U + 1, 2 * R, LANES), F32),
                pltpu.VMEM((per_step // U * 2 * R, NBR * U), BF16),
            ],
        ),
        out_shape=jax.ShapeDtypeStruct((2, R, width), F32),
        compiler_params=ROOM,
        cost_estimate=cost(1),
        name="near_part",
    )(index, below, own, above, blocks)


def down_kernel(got_ref, mat_ref, out_ref):
    pieces = []
    for chip in range(got_ref.shape[0]):
        both = got_ref[chip].astype(F32).reshape(-1, 2, R, LANES)
        pieces += [both[:, 0].reshape(-1, LANES), both[:, 1].reshape(-1, LANES)]
    fields = jnp.concatenate(pieces, axis=1).astype(BF16)
    out_ref[...] = times_transposed(fields, mat_ref[...]).astype(BF16)


def from_boxes(received, matrix):
    rows = received.shape[1] // 2
    steps = 1
    chips = CHIPS // steps
    return pl.pallas_call(
        down_kernel,
        grid=(steps,),
        in_specs=[
            pl.BlockSpec((chips, 2 * rows, LANES), lambda s: (s, 0, 0)),
            pl.BlockSpec((DEPTH, 2 * chips * LANES), lambda s: (0, s)),
        ],
        out_specs=pl.BlockSpec((rows, DEPTH), lambda s: (0, 0)),
        out_shape=jax.ShapeDtypeStruct((rows, DEPTH), BF16),
        compiler_params=LESS,
        cost_estimate=cost(1),
        name="from_boxes",
    )(received, matrix)


def far_kernel(hi_ref, own_ref, other_ref, rad_ref, near_ref, out_ref):
    low_half = hi_ref[0] == 0
    boxes = out_ref.shape[2] // WIDE
    low = low_lanes(2 * R)
    for pair in range(boxes // 2):
        rows = slice(pair * 2 * R, (pair + 1) * 2 * R)
        pieces = [[], []]
        for i in range(CHILDREN):
            cols = slice(i * LANES, (i + 1) * LANES)
            own, other = own_ref[rows, cols].astype(F32), other_ref[rows, cols].astype(F32)
            zero, one = jnp.where(low_half, own, other), jnp.where(low_half, other, own)
            real = jnp.where(low, zero, swap_halves(one))
            imag = jnp.where(low, swap_halves(zero), one)
            for k in range(2):
                part = slice(k * R, (k + 1) * R)
                pieces[k].append(jnp.concatenate([real[part], imag[part]], axis=1))
                pieces[k].append(jnp.concatenate([imag[part], -real[part]], axis=1))
        for k in range(2):
            fields = jnp.concatenate(pieces[k], axis=0).astype(BF16)
            cols = slice((2 * pair + k) * WIDE, (2 * pair + k + 1) * WIDE)
            slab = jnp.concatenate([rad_ref[0, cols, :], rad_ref[1, cols, :]], axis=1)
            terms = times_transposed(fields, slab)
            for part in range(2):
                own = [terms[2 * R * i + part * R : 2 * R * i + (part + 1) * R] for i in range(CHILDREN)]
                out_ref[part, :, cols] = near_ref[part, :, cols] + own_columns(own)


def far_part(hi, own, other, radiation, near_field):
    width = near_field.shape[2]
    rows = own.shape[0]
    steps = 1
    per_step = width // steps
    field = pl.BlockSpec((rows // steps, DEPTH), lambda s, *_: (s, 0))
    wave = pl.BlockSpec((2, R, per_step), lambda s, *_: (0, 0, s))
    return pl.pallas_call(
        far_kernel,
        grid_spec=pltpu.PrefetchScalarGridSpec(
            num_scalar_prefetch=1,
            grid=(steps,),
            in_specs=[field, field, pl.BlockSpec((2, per_step, LANES), lambda s, *_: (0, s, 0)), wave],
            out_specs=wave,
        ),
        out_shape=jax.ShapeDtypeStruct((2, R, width), F32),
        compiler_params=LESS,
        cost_estimate=cost(1),
        name="far_part",
    )(hi, own, other, radiation, near_field)


def swapped(array):
    return lax.all_to_all(array, INSIDE, split_axis=0, concat_axis=0, tiled=True)


def padded(array):
    return jnp.pad(array, [(0, 0)] * (array.ndim - 1) + [(0, LANES - array.shape[-1])])


def to_owners(boxes, samples):
    rows = boxes.shape[1]
    if samples != LANES:
        boxes = boxes.reshape(CHIPS, rows, LANES // samples, samples).transpose(0, 2, 1, 3).reshape(-1, rows, samples)
    got = swapped(boxes)
    if samples != LANES:
        got = padded(got)
    return got.reshape(-1, 2 * R, LANES)


def from_owners(fields, rows, samples):
    fields = fields.reshape(-1, rows, LANES)
    if samples == LANES:
        return swapped(fields)
    got = swapped(fields[..., :samples]).reshape(CHIPS, LANES // samples, rows, samples)
    return got.transpose(0, 2, 1, 3).reshape(CHIPS, rows, LANES)


def operator_table(translation):
    groups, mids = lax.axis_size("grp"), lax.axis_size("mid")
    core = lax.axis_index("core")
    pairs = [
        (((h * groups + g) * mids + m) * 2 + c, ((g * 2 + h) * mids + m) * 2 + c)
        for g in range(groups)
        for h in range(2)
        for m in range(mids)
        for c in range(2)
    ]
    mine = lax.ppermute(jnp.swapaxes(translation, 1, 2), ALL, pairs)
    other = across(mine, "core").astype(F32)
    mine = mine.astype(F32)
    low = jnp.where(core == 0, mine, other)
    high = jnp.where(core == 0, other, mine)
    operator = padded(jnp.swapaxes(jnp.concatenate([low, high], axis=1), 1, 2))
    return jnp.pad(operator, ((0, 0), (0, -operator.shape[1] % R), (0, 0)))


def target_lists(trans_box, trans_off, hi, core):
    groups, mids = lax.axis_size("grp"), lax.axis_size("mid")
    total = trans_box.shape[0]
    per = total // (groups * mids * 4)
    device, inside = trans_box // per, trans_box % per
    group, side = device // (4 * mids), device // (2 * mids) % 2
    mid, its_core = device // 2 % mids, device % 2
    block = (side ^ hi) * 2 + (its_core ^ core)
    place = (block * (groups * mids) + group * mids + mid) * per + inside
    lists = jnp.concatenate([place, trans_off], axis=1).reshape(groups, 2, mids, 2, per, 2 * IL)
    lists = jnp.where(core == 0, lists[:, :, :, 0], lists[:, :, :, 1])
    first, second = lists[:, 0].reshape(-1), lists[:, 1].reshape(-1)
    return jnp.where(hi == 0, first, second), jnp.where(hi == 0, second, first)


def local(
    currents,
    near_blocks,
    near_list,
    near_count,
    radiation,
    interp,
    shift_angle,
    translation,
    trans_box,
    trans_off,
):
    clusters = near_list.shape[0]
    samples = 2 * translation.shape[2]
    rows = clusters // CHILDREN * 2 * R
    hi, core = lax.axis_index("hi"), lax.axis_index("core")
    side = hi.reshape(1).astype(jnp.int32)
    radiation = radiation.reshape(2, clusters * U, LANES)
    near_blocks = near_blocks.reshape(2, clusters * U, NBR * U)

    first = (lax.axis_index(ALL) - 1) * clusters
    live = jnp.arange(NBR, dtype=jnp.int32)[None, :] < near_count[:, None]
    index = jnp.where(live, near_list - first, 3 * clusters).reshape(-1)
    lists = target_lists(trans_box, trans_off, hi, core)

    leaf_own, leaf_other = leaves(side, currents, radiation)
    leaf_partner = across(leaf_other, "hi")
    boxes_own, matrix = to_boxes(leaf_own, interp, shift_angle)
    rows_own = to_owners(boxes_own, samples)
    swapped_own = across(rows_own, "core")
    operators = operator_table(translation)
    below, above = neighbours(currents)
    leaf_partner, lists, index, operators, below, above = lax.optimization_barrier(
        (leaf_partner, lists, index, operators, below, above)
    )
    rows_partner = to_owners(to_boxes_again(leaf_partner, matrix), samples)
    parts = (rows_own, swapped_own, rows_partner, across(rows_partner, "core"))

    fields_partner = translate(lists[1], operators, parts)
    down_partner = from_boxes(from_owners(fields_partner, rows, samples), matrix)
    fields_own = translate(lists[0], operators, parts)
    down_partner, index = lax.optimization_barrier((down_partner, index))
    down_other = across(down_partner, "hi")
    near_field = near_part(index, below, currents, above, near_blocks)
    down_own = from_boxes(from_owners(fields_own, rows, samples), matrix)
    return far_part(side, down_own, down_other, radiation, near_field)


def solution(mesh):
    devices = mesh.devices
    groups, rest = devices.shape
    cut = Mesh(devices.reshape(groups, 2, rest // 4, 2), ALL)
    placed = (
        P(None, None, ALL),
        P(None, ALL, None, None),
        P(ALL, None),
        P(ALL),
        P(None, ALL, None, None),
        P(),
        P(),
        P(None, None, ALL),
        P(),
        P(),
    )
    return jax.shard_map(local, mesh=cut, in_specs=placed, out_specs=P(None, None, ALL), check_vma=False)
```
